32 devices in a mesh: dp: 16 (over z, y, x), mp: 2 (over core).
Axes of the slice: x: 2, y: 2, z: 4, core: 2. Of those that a mesh axis runs over, the one named last changes fastest.
Arguments:
- hidden_in: bfloat16 [4096, 1472], P(('dp', 'mp')), may hold values from -6 to 6
- attention_gain: float32 [1472], replicated, may hold values from 0.25 to 1.75
- query_weight: bfloat16 [1472, 384], P(None, 'mp'), may hold values from -0.078125 to 0.078125
- key_weight: bfloat16 [1472, 384], P(None, 'mp'), may hold values from -0.078125 to 0.078125
- value_weight: bfloat16 [1472, 384], P(None, 'mp'), may hold values from -0.15625 to 0.15625
- output_weight: bfloat16 [384, 1472], P('mp'), may hold values from -0.875 to 0.875
- position_bias: float32 [32, 6], P(None, 'mp'), may hold values from -4 to 4
- feedforward_gain: float32 [1472], replicated, may hold values from 0.25 to 1.75
- gate_weight: bfloat16 [1472, 3584], P(None, 'mp'), may hold values from -0.15625 to 0.15625
- up_weight: bfloat16 [1472, 3584], P(None, 'mp'), may hold values from -0.15625 to 0.15625
- down_weight: bfloat16 [3584, 1472], P('mp'), may hold values from -0.125 to 0.125
- cotangent: bfloat16 [4096, 1472], P(('dp', 'mp')), may hold values from -6 to 6
- item_lengths: int32 [16], replicated, may hold values from 1 to 256, 2560 in all
- item_group: int32 [16], replicated, may hold values from 0 to 15, each once
- bucket_ids: int32 [511], replicated, may hold values from 0 to 31, as said below
Outputs:
- layer_out: float32 [4096, 1472], P(('dp', 'mp'))
- input_grad: float32 [4096, 1472], P(('dp', 'mp'))
- attention_gain_grad: float32 [1472], replicated
- query_grad: float32 [1472, 384], P('dp', 'mp')
- key_grad: float32 [1472, 384], P('dp', 'mp')
- value_grad: float32 [1472, 384], P('dp', 'mp')
- output_grad: float32 [384, 1472], P('mp', 'dp')
- position_bias_grad: float32 [32, 6], P(None, 'mp')
- feedforward_gain_grad: float32 [1472], replicated
- gate_grad: float32 [1472, 3584], P('dp', 'mp')
- up_grad: float32 [1472, 3584], P('dp', 'mp')
- down_grad: float32 [3584, 1472], P('mp', 'dp')
The draws below stay inside these ranges and needn't reach their ends.
Inputs may be any that keep to these rules, and one draw needn't show every extreme that they name: `item_lengths`: the lengths sum to 2560, and one of them is exactly 256. `item_group`: each group number appears once. `bucket_ids`: entry r + 255 is the bucket of a key r positions after its query: 0 at r = 0, never falling as |r| grows for one sign of r, 16 or more exactly where r > 0, and 31 at r = 255.
All inputs are finite; a program needn't handle non-finite values.
Results may differ from the reference program's by a relative error of at most 0.025.
Values may be sent and summed in bfloat16 or wider, within the bound.
A program may use at most 192 MiB of HBM per device.

```python
import math
import jax
import jax.numpy as jnp
import numpy as np
from jax import lax

D = 1472
HEADS = 6
DKV = 64
FF = 3584
BUCKETS = 32
LMAX = 256
GROUPS = 16
ROWS = 4096
N_DP = 16


def draw_bucket_ids(key, part):
    half_count = BUCKETS // 2
    level_index = jnp.arange(half_count - 1, dtype=jnp.int32)
    step_sizes = jax.random.randint(key, (half_count - 1,), 1, 3 + 2 * level_index)
    limits = jnp.minimum(jnp.cumsum(step_sizes), LMAX - (half_count - 1) + level_index)
    offsets = jnp.arange(2 * LMAX - 1, dtype=jnp.int32) - (LMAX - 1)
    distance = jnp.abs(offsets)
    counted = jnp.sum((limits[None, :] <= distance[:, None]).astype(jnp.int32), axis=1)
    return (counted + half_count * (offsets > 0).astype(jnp.int32)).astype(jnp.int32)


def spiked(result, own_key, source, target, parts, factor):
    def block_of(dim):
        return (jnp.arange(result.shape[dim]) // (result.shape[dim] // parts)).reshape((-1,) + (1,) * (result.ndim - 1 - dim))

    one_side = jax.random.permutation(own_key, parts)[block_of(target)]
    far = (block_of(target) + parts // 2) % parts
    return jnp.where((block_of(source) == one_side) | (block_of(source) == far), factor * result, result)


def block_scale(own_key, dims, shards, smallest, top_value):
    def one(position, blocks):
        heights = jax.random.uniform(jax.random.fold_in(jax.random.fold_in(own_key, 6), position), (blocks,), jnp.float32, smallest / len(shards), top_value / len(shards))
        return jnp.repeat(jnp.exp(heights), dims[position] // blocks).reshape((-1,) + (1,) * (len(dims) - position - 1))

    factor_of = one(*shards[0])
    for cut in shards[1:]:
        factor_of = factor_of * one(*cut)
    return factor_of


def profile(count, total, limit, lean):
    portions = [(1 << 20) // math.isqrt(grade ** lean) + 1 for grade in range(2, count + 1)]
    spare, holding = total - limit - (count - 1), [1] * (count - 1)
    while spare > 0:
        free = [i for i in range(count - 1) if holding[i] < limit]
        mass, left = sum([portions[i] for i in free]), spare
        for i in free:
            more = min(limit - holding[i], max(1, left * portions[i] // mass), spare)
            holding[i] = holding[i] + more
            spare = spare - more
    return np.array([limit] + holding)


def ragged(key, amount, total, bound, slope):
    if amount == 2:
        one = jax.random.randint(key, (), max(1, total - bound), min(bound, total - 1) + 1)
        return jnp.stack([one, total - one])
    lengths = jnp.asarray(profile(amount, total, bound, slope), jnp.int32)
    twos = (amount - 1) // 2
    giver, taker = lengths[1:1 + 2 * twos:2], lengths[2:2 + 2 * twos:2]
    margin = jnp.minimum(giver - 1, bound - taker)
    passed = jax.random.randint(jax.random.fold_in(key, 1), (twos,), 0, 1 << 20) % (margin + 1)
    lengths = lengths.at[1:1 + 2 * twos:2].set(giver - passed).at[2:2 + 2 * twos:2].set(taker + passed)
    return lengths[jax.random.permutation(jax.random.fold_in(key, 2), amount)]


def scatter_about(stream_key, extent, width, bound, split=(), held_as=jnp.bfloat16):
    entries = width * jax.random.normal(stream_key, extent, jnp.float32)
    if split:
        entries = entries * block_scale(stream_key, extent, split, -0.22, 0.18)
    return jnp.clip(entries, -bound, bound).astype(held_as)


def gaussian_with(own_key, dims, spread, bound, split, heavy, held_as=jnp.bfloat16):
    values = spread * jax.random.normal(own_key, dims, jnp.float32)
    if split:
        values = values * block_scale(own_key, dims, split, -0.22, 0.18)
    return jnp.clip(spiked(values, jax.random.fold_in(own_key, 3), *heavy), -bound, bound).astype(held_as)


def setup_inputs(seed: int = 0) -> dict:
    seeds = jax.random.split(jax.random.key(seed), 16)
    return {
        "hidden_in": gaussian_with(seeds[0], (ROWS, D), 1.0, 6.0, ((0, 32),), (0, 1, 32, 2.75)),
        "attention_gain": jnp.clip(1.0 + 0.15 * jax.random.normal(seeds[1], (D,), jnp.float32), 0.25, 1.75),
        "query_weight": scatter_about(seeds[2], (D, HEADS * DKV), (4 * D) ** -0.5, 0.078125, ((1, 2),)),
        "key_weight": scatter_about(seeds[3], (D, HEADS * DKV), (4 * D) ** -0.5, 0.078125, ((1, 2),)),
        "value_weight": scatter_about(seeds[4], (D, HEADS * DKV), D ** -0.5, 0.15625, ((1, 2),)),
        "output_weight": scatter_about(seeds[5], (HEADS * DKV, D), (HEADS * DKV // 8) ** -0.5, 0.875, ((0, 2),)),
        "position_bias": scatter_about(seeds[6], (BUCKETS, HEADS), 1.0, 4.0, ((1, 2),), jnp.float32),
        "feedforward_gain": jnp.clip(1.0 + 0.15 * jax.random.normal(seeds[7], (D,), jnp.float32), 0.25, 1.75),
        "gate_weight": scatter_about(seeds[8], (D, FF), D ** -0.5, 0.15625, ((1, 2),)),
        "up_weight": scatter_about(seeds[9], (D, FF), D ** -0.5, 0.15625, ((1, 2),)),
        "down_weight": scatter_about(seeds[10], (FF, D), (FF // 2) ** -0.5, 0.125, ((0, 2),)),
        "cotangent": gaussian_with(seeds[11], (ROWS, D), 1.0, 6.0, ((0, 32),), (0, 1, 32, 2.75)),
        "item_lengths": ragged(seeds[12], GROUPS, 5 * LMAX * N_DP // 8, LMAX, 1).astype(jnp.int32),
        "item_group": jax.random.permutation(seeds[13], GROUPS).astype(jnp.int32),
        "bucket_ids": draw_bucket_ids(jax.random.fold_in(seeds[15], 71), 0),
    }


@jax.custom_vjp
def low(v):
    return lax.optimization_barrier(v.astype(jnp.bfloat16)).astype(jnp.float32)

@jax.custom_vjp
def low_back(v):
    return v

def low_keep(v):
    return (low(v), None)

def low_pass(kept, grad):
    return (grad,)

def back_keep(v):
    return (v, None)

def back_low(kept, grad):
    return (low(grad),)
low.defvjp(low_keep, low_pass)
low_back.defvjp(back_keep, back_low)

def matmul_high(left, right):
    return jnp.matmul(left, right, precision=lax.Precision.HIGHEST)

def rms_norm(values_in, gain_vec):
    inv_rms = lax.rsqrt(lax.optimization_barrier(jnp.mean(values_in * values_in, axis=-1, keepdims=True)) + 1e-06)
    return values_in * inv_rms * gain_vec

def layer(hidden, weights, group_lens, bias_index):
    attention_gain, query_weight, key_weight, value_weight, output_weight, position_bias, feedforward_gain, gate_weight, up_weight, down_weight = weights
    groups_in = hidden.shape[0]
    seq_len = hidden.shape[1]
    normed_one = low(rms_norm(hidden, attention_gain))

    def heads_of(weight_arg):
        projected = low(low_back(matmul_high(normed_one, weight_arg)))
        return projected.reshape(groups_in, seq_len, HEADS, DKV)
    queries = heads_of(query_weight)
    key_rows = heads_of(key_weight)
    values = heads_of(value_weight)
    bias_rows = jnp.transpose(position_bias[bias_index], (2, 0, 1))
    scores = jnp.einsum('bqhd,bkhd->bhqk', queries, key_rows, precision=lax.Precision.HIGHEST) + bias_rows[None]
    scores = low_back(scores)
    allowed = jnp.arange(seq_len, dtype=jnp.int32)[None, :] < group_lens[:, None]
    scores = jnp.where(allowed[:, None, None, :], scores, -1e+30)
    row_peak = lax.optimization_barrier(jnp.max(scores, axis=-1, keepdims=True))
    exps = jnp.exp(scores - row_peak)
    probabilities = low(exps / lax.optimization_barrier(jnp.sum(exps, axis=-1, keepdims=True)))
    attended = jnp.einsum('bhqk,bkhd->bqhd', probabilities, values, precision=lax.Precision.HIGHEST)
    attended = low(low_back(attended.reshape(groups_in, seq_len, HEADS * DKV)))
    middle = hidden + low_back(matmul_high(attended, output_weight))
    normed_two = low(rms_norm(middle, feedforward_gain))
    gate = low_back(matmul_high(normed_two, gate_weight))
    up_rows = low_back(matmul_high(normed_two, up_weight))
    hidden_ff = low(jax.nn.gelu(gate, approximate=True) * up_rows)
    return middle + low_back(matmul_high(hidden_ff, down_weight))

def reference(hidden_in, attention_gain, query_weight, key_weight, value_weight, output_weight, position_bias, feedforward_gain, gate_weight, up_weight, down_weight, cotangent, item_lengths, item_group, bucket_ids):
    groups_per_step = math.gcd(GROUPS, max(1, 4096 // LMAX))
    step_count = GROUPS // groups_per_step
    group_index = jnp.arange(GROUPS, dtype=jnp.int32)
    group_lens = lax.optimization_barrier(jnp.sum(jnp.where(item_group[None, :] == group_index[:, None], item_lengths[None, :], 0), axis=1)).astype(jnp.int32)
    positions = jnp.arange(LMAX, dtype=jnp.int32)
    bias_index = bucket_ids[(positions[None, :] - positions[:, None] + LMAX - 1).astype(jnp.int32)]
    valid = (positions[None, :] < group_lens[:, None]).astype(jnp.float32)
    hidden = hidden_in.astype(jnp.float32).reshape(step_count, groups_per_step, LMAX, D)
    grads_out = (cotangent.astype(jnp.float32).reshape(GROUPS, LMAX, D) * valid[:, :, None]).reshape(step_count, groups_per_step, LMAX, D)
    lens_steps = group_lens.reshape(step_count, groups_per_step)
    weights = tuple((weight_arg.astype(jnp.float32) for weight_arg in (attention_gain, query_weight, key_weight, value_weight, output_weight, position_bias, feedforward_gain, gate_weight, up_weight, down_weight)))

    def one_step(carried, inputs):
        hidden_step, grad_step, lens_step = inputs

        def forward(hidden_arg, weights_arg):
            return layer(hidden_arg, weights_arg, lens_step, bias_index)
        layer_out, pullback = jax.vjp(forward, hidden_step, weights)
        input_grad, weight_grads = pullback(grad_step)
        summed = tuple((total_sofar + term_now for total_sofar, term_now in zip(carried, weight_grads)))
        return (summed, (layer_out, input_grad))
    zeros_init = tuple((jnp.zeros_like(weight_arg) for weight_arg in weights))
    totals, (outputs, input_grads) = lax.scan(one_step, zeros_init, (hidden, grads_out, lens_steps))
    return (outputs.reshape(ROWS, D), input_grads.reshape(ROWS, D), totals[0], totals[1], totals[2], totals[3], totals[4], totals[5], totals[6], totals[7], totals[8], totals[9])
```

```python
import functools
import math

import jax
import jax.numpy as jnp
from jax import lax
from jax.experimental import pallas as pl
from jax.experimental.pallas import tpu as pltpu
from jax.sharding import PartitionSpec as P

DKV = 64
CW = 256
EPS = 1e-06
LAG = 3
GAP = 2
SLOTS = 3
BF = jnp.bfloat16
F32 = jnp.float32
MESH = pl.DeviceIdType.MESH
GELU_C = math.sqrt(2.0 / math.pi)


def dot(left, right):
    return lax.dot_general(left, right, (((1,), (0,)), ((), ())), preferred_element_type=F32)


def dot_nt(left, right):
    return lax.dot_general(left, right, (((1,), (1,)), ((), ())), preferred_element_type=F32)


def dot_tn(left, right):
    return lax.dot_general(left, right, (((0,), (0,)), ((), ())), preferred_element_type=F32)


def column_blocks(width, step=256):
    return [(begin, min(step, width - begin)) for begin in range(0, width, step)]


class Sizes:
    def __init__(self, dp, local_rows, width, head_width, hidden, buckets):
        self.dp = dp
        self.bits = dp.bit_length() - 1
        self.local_rows = local_rows
        self.seq = 2 * local_rows
        self.width = width
        self.head_width = head_width
        self.heads = head_width // DKV
        self.hidden = hidden
        self.buckets = buckets
        self.shard = width // dp
        self.shard_pad = -(-self.shard // 16) * 16
        self.quarter = self.shard_pad * dp // 4
        self.ff_chunks = hidden // CW
        self.ff_total = 3 * self.ff_chunks
        self.chunks = self.ff_total + 4 * head_width // CW
        self.stage_rows = [self.quarter >> k for k in range(self.bits - 1)]
        self.stages = len(self.stage_rows)
        self.wide = -(-width // 256) * 256


def layer_kernel(
    cfg,
    hidden_hbm,
    gain_one,
    wq_hbm,
    wk_hbm,
    wv_hbm,
    wo_hbm,
    position_bias,
    gain_two,
    wg_hbm,
    wu_hbm,
    wd_hbm,
    cot_hbm,
    lengths,
    groups,
    bucket_ids,
    layer_out,
    input_grad,
    small_out,
    final_out,
    hid,
    cot,
    wqkv,
    wo,
    wg,
    wu,
    wd,
    normed_one,
    normed_two,
    middle,
    qkv,
    probs,
    attended,
    trans,
    left_own,
    left_in,
    right_own,
    right_in,
    out_acc,
    grad_acc,
    grad_send,
    grad_in,
    part_send,
    part_in,
    back_send,
    back_in,
    grad_branch,
    grad_qkv,
    small,
    small_in,
    *rest,
):
    stages = cfg.stages
    stage_own = rest[:stages]
    stage_send = rest[stages : 2 * stages]
    stage_in = rest[2 * stages : 3 * stages]
    (
        load_sem,
        weight_sem,
        pair_send_sem,
        pair_recv_sem,
        left_send_sem,
        left_recv_sem,
        right_send_sem,
        right_recv_sem,
        stage_send_sem,
        stage_recv_sem,
        small_send_sem,
        small_recv_sem,
    ) = rest[3 * stages :]

    seq, rows, width, hw, heads = cfg.seq, cfg.local_rows, cfg.width, cfg.head_width, cfg.heads
    me = lax.axis_index("dp")
    core = lax.axis_index("mp")
    bit = [lax.rem(lax.div(me, 1 << k), 2) for k in range(cfg.bits)]
    peer = [me + (1 - 2 * bit[k]) * (1 << k) for k in range(cfg.bits)]
    sibling = (me, 1 - core)
    own_begin = pl.multiple_of(core * rows, rows)
    other_begin = pl.multiple_of((1 - core) * rows, rows)
    own_rows = pl.ds(own_begin, rows)
    other_rows = pl.ds(other_begin, rows)

    def send(src, dst, send_sem, recv_sem, target):
        return pltpu.make_async_remote_copy(
            src_ref=src,
            dst_ref=dst,
            send_sem=send_sem,
            recv_sem=recv_sem,
            device_id=target,
            device_id_type=MESH,
        )

    head_rows = pl.ds(pl.multiple_of(core * hw, hw), hw)
    loads = [
        pltpu.make_async_copy(hidden_hbm, hid.at[own_rows], load_sem.at[0]),
        pltpu.make_async_copy(cot_hbm, cot.at[own_rows], load_sem.at[1]),
        pltpu.make_async_copy(wq_hbm, wqkv.at[0], load_sem.at[2]),
        pltpu.make_async_copy(wk_hbm, wqkv.at[1], load_sem.at[3]),
        pltpu.make_async_copy(wv_hbm, wqkv.at[2], load_sem.at[4]),
        pltpu.make_async_copy(wo_hbm, wo.at[core], load_sem.at[5]),
    ]
    for load in loads:
        load.start()

    def weight_loads(chunk, slot):
        columns = pl.ds(pl.multiple_of(chunk * CW, CW), CW)
        return [
            pltpu.make_async_copy(wg_hbm.at[:, columns], wg.at[slot], weight_sem.at[slot, 0]),
            pltpu.make_async_copy(wu_hbm.at[:, columns], wu.at[slot], weight_sem.at[slot, 1]),
            pltpu.make_async_copy(wd_hbm.at[columns, :], wd.at[slot], weight_sem.at[slot, 2]),
        ]

    barrier = pltpu.get_barrier_semaphore()
    pl.semaphore_signal(barrier, inc=1, device_id=sibling, device_id_type=MESH)
    for k in range(cfg.bits):
        pl.semaphore_signal(barrier, inc=1, device_id=(peer[k], core), device_id_type=MESH)
    pl.semaphore_wait(barrier, cfg.bits + 1)

    pair_hid = send(
        hidden_hbm, hid.at[own_rows], pair_send_sem.at[0], pair_recv_sem.at[0], sibling
    )
    pair_cot = send(cot_hbm, cot.at[own_rows], pair_send_sem.at[1], pair_recv_sem.at[1], sibling)
    pair_wo = send(wo_hbm, wo.at[core], pair_send_sem.at[2], pair_recv_sem.at[2], sibling)
    pair_hid.start()
    pair_cot.start()
    pair_wo.start()
    pair_att = send(
        attended.at[core], attended.at[core], pair_send_sem.at[3], pair_recv_sem.at[3], sibling
    )
    pair_grad = send(grad_send, grad_in, pair_send_sem.at[4], pair_recv_sem.at[4], sibling)
    pair_part = send(part_send, part_in, pair_send_sem.at[5], pair_recv_sem.at[5], sibling)
    pair_back = send(back_send, back_in, pair_send_sem.at[6], pair_recv_sem.at[6], sibling)

    for slot in range(2):
        for load in weight_loads(slot, slot):
            load.start()

    group_len = jnp.int32(0)
    for item in range(lengths.shape[0]):
        group_len = group_len + jnp.where(groups[item] == me, lengths[item], 0)

    left_axis = (0, 1, 1, 1)

    def build_left(source, which):
        for begin, size in column_blocks(width, 128):
            trans[begin : begin + size, :] = jnp.transpose(
                source[:, begin : begin + size].astype(F32)
            )
        first = left_axis[which]
        for index in range(cfg.dp):
            low = (index & 1, (index >> 1) & 1)
            place = 0
            for k in range(2, cfg.bits):
                place = 2 * place + ((index >> k) & 1)
            block = trans[index * cfg.shard : index * cfg.shard + cfg.shard_pad, :]
            left_own[
                which,
                low[first],
                low[1 - first],
                place * cfg.shard_pad : (place + 1) * cfg.shard_pad,
                :,
            ] = block.astype(BF)

    def left_copy(which):
        first = left_axis[which]
        return send(
            left_own.at[which, 1 - bit[first]],
            left_in.at[which],
            left_send_sem.at[which],
            left_recv_sem.at[which],
            (peer[first], core),
        )

    def right_copy(chunk, first):
        return send(
            right_own.at[chunk],
            right_in.at[chunk],
            right_send_sem.at[chunk],
            right_recv_sem.at[chunk],
            (peer[first], core),
        )

    tail = trans.shape[0] - width
    trans[width:, :] = jnp.zeros((tail, seq), F32)

    loads[0].wait()
    pair_hid.wait()

    def norm_one_rows(step, carry):
        block = pl.ds(pl.multiple_of(step * 32, 32), 32)
        x = hid[block, :].astype(F32)
        inv = lax.rsqrt(jnp.mean(x * x, axis=1, keepdims=True) + EPS)
        normed_one[block, :] = (x * inv * gain_one[...]).astype(BF)
        return carry

    lax.fori_loop(0, seq // 32, norm_one_rows, 0)

    for part in range(3):
        loads[2 + part].wait()
        qkv[part] = dot(normed_one[...], wqkv[part]).astype(BF)

    key_valid = lax.broadcasted_iota(jnp.int32, (seq, seq), 1) < group_len
    ids = bucket_ids[...]
    mixed = []
    for head in range(heads):
        lanes = slice(head * DKV, (head + 1) * DKV)
        by_offset = jnp.zeros(ids.shape, F32)
        for bucket in range(cfg.buckets):
            by_offset = jnp.where(ids == bucket, position_bias[bucket, head], by_offset)
        bias = pltpu.roll(
            jnp.broadcast_to(by_offset, (seq, 2 * seq)),
            seq + 1,
            1,
            stride=1,
            stride_axis=0,
        )[:, :seq]
        scores = dot_nt(qkv[0, :, lanes], qkv[1, :, lanes]) + bias
        scores = jnp.where(key_valid, scores, -1e30)
        exps = jnp.exp(scores - jnp.max(scores, axis=1, keepdims=True))
        prob = exps / jnp.sum(exps, axis=1, keepdims=True)
        probs[head] = prob
        mixed.append(dot(prob.astype(BF), qkv[2, :, lanes]).astype(BF))
    own_attended = jnp.concatenate(mixed, axis=1)
    attended[core] = own_attended
    pair_att.start()

    loads[1].wait()
    pair_cot.wait()

    def mask_rows(step, carry):
        begin = pl.multiple_of(step * 32, 32)
        block = pl.ds(begin, 32)
        keep = begin + lax.broadcasted_iota(jnp.int32, (32, width), 0) < group_len
        cot[block, :] = jnp.where(keep, cot[block, :].astype(F32), 0.0).astype(BF)
        return carry

    lax.fori_loop(0, seq // 32, mask_rows, 0)
    build_left(cot, 0)
    left_copy(0).start()
    build_left(normed_one, 2)
    left_copy(2).start()

    loads[5].wait()
    pair_wo.wait()
    pair_att.wait()
    for begin, size in column_blocks(width):
        columns = slice(begin, begin + size)
        middle[:, columns] = (
            hid[:, columns].astype(F32)
            + dot(attended[0], wo[0, :, columns])
            + dot(attended[1], wo[1, :, columns])
        )

    def norm_two_rows(step, carry):
        block = pl.ds(pl.multiple_of(step * 32, 32), 32)
        x = middle[block, :]
        inv = lax.rsqrt(jnp.mean(x * x, axis=1, keepdims=True) + EPS)
        normed_two[block, :] = (x * inv * gain_two[...]).astype(BF)
        out_acc[block, :] = jnp.zeros((32, width), F32)
        grad_acc[block, :] = jnp.zeros((32, width), F32)
        return carry

    lax.fori_loop(0, seq // 32, norm_two_rows, 0)
    build_left(normed_two, 1)
    left_copy(1).start()
    small[...] = jnp.zeros_like(small)

    def feed_forward(chunk):
        slot = lax.rem(chunk, 2)
        for load in weight_loads(chunk, slot):
            load.wait()
        normed = normed_two[...]
        gate = dot(normed, wg[slot])
        up = dot(normed, wu[slot])
        grad_hidden = dot_nt(cot[...], wd[slot])
        square = gate * gate
        tanh = jnp.tanh(GELU_C * (gate + 0.044715 * (square * gate)))
        half = 0.5 * (1.0 + tanh)
        gelu = gate * half
        slope = half + (0.5 * GELU_C) * gate * (1.0 - tanh * tanh) * (
            1.0 + (3 * 0.044715) * square
        )
        hidden = (gelu * up).astype(BF)
        grad_gate = (grad_hidden * up * slope).astype(BF)
        grad_up = (grad_hidden * gelu).astype(BF)
        base = 3 * chunk
        right_own[base] = hidden
        right_own[base + 1] = grad_gate
        right_own[base + 2] = grad_up
        right_copy(base, 0).start()
        right_copy(base + 1, 1).start()
        right_copy(base + 2, 1).start()
        for begin, size in column_blocks(width):
            columns = slice(begin, begin + size)
            out_acc[:, columns] += dot(hidden, wd[slot, :, columns])
            grad_acc[:, columns] += dot_nt(grad_gate, wg[slot, columns, :]) + dot_nt(
                grad_up, wu[slot, columns, :]
            )

        @pl.when(chunk < cfg.ff_chunks - 2)
        def _():
            for load in weight_loads(chunk + 2, slot):
                load.start()

    def exchange_sums():
        grad_send[...] = grad_acc[...].astype(BF)
        pair_grad.start()
        part_send[...] = out_acc[other_rows, :].astype(BF)
        pair_part.start()

    def norm_two_back():
        pair_grad.wait()
        gain = gain_two[...]

        def back_rows(step, carry):
            block = pl.ds(pl.multiple_of(step * 32, 32), 32)
            grad = grad_acc[block, :] + grad_in[block, :].astype(F32)
            x = middle[block, :]
            inv = lax.rsqrt(jnp.mean(x * x, axis=1, keepdims=True) + EPS)
            unit = x * inv
            scaled = grad * gain
            inner = jnp.mean(scaled * unit, axis=1, keepdims=True)
            total = cot[block, :].astype(F32) + inv * (scaled - unit * inner)
            grad_acc[block, :] = total
            grad_branch[block, :] = total.astype(BF)
            mine = lax.div(step * 32, rows) == core
            small[1:2, :width] += jnp.where(
                mine, jnp.sum(grad * unit, axis=0, keepdims=True), 0.0
            )
            return carry

        lax.fori_loop(0, seq // 32, back_rows, 0)
        build_left(grad_branch, 3)
        left_copy(3).start()

    def attention_back():
        grad_att = dot_nt(grad_branch[...], wo[core]).astype(BF)
        flip = (
            lax.broadcasted_iota(jnp.int32, (seq, seq), 0)
            + lax.broadcasted_iota(jnp.int32, (seq, seq), 1)
            == seq - 1
        ).astype(BF)
        parts = [[], [], []]
        for head in range(heads):
            lanes = slice(head * DKV, (head + 1) * DKV)
            grad_mixed = grad_att[:, lanes]
            prob = probs[head]
            grad_probs = dot_nt(grad_mixed, qkv[2, :, lanes])
            inner = jnp.sum(prob * grad_probs, axis=1, keepdims=True)
            grad_scores = (prob * (grad_probs - inner)).astype(BF)
            parts[0].append(dot(grad_scores, qkv[1, :, lanes]).astype(BF))
            parts[1].append(dot_tn(grad_scores, qkv[0, :, lanes]).astype(BF))
            parts[2].append(dot_tn(prob.astype(BF), grad_mixed).astype(BF))
            flipped = jnp.concatenate(
                [dot(flip, grad_scores), jnp.zeros((seq, seq), F32)], axis=1
            )
            skewed = pltpu.roll(flipped, 0, 1, stride=1, stride_axis=0)
            small[2 + head : 3 + head, : 2 * seq] = jnp.sum(skewed, axis=0, keepdims=True)
        for part in range(3):
            grad_qkv[part] = jnp.concatenate(parts[part], axis=1)
        joined = jnp.concatenate(
            parts[0] + parts[1] + parts[2] + [attended[core]], axis=1
        )
        for index in range(cfg.chunks - cfg.ff_total):
            chunk = cfg.ff_total + index
            right_own[chunk] = joined[:, index * CW : (index + 1) * CW]
            right_copy(chunk, 1).start()

    def norm_one_sums():
        for begin, size in column_blocks(width):
            columns = slice(begin, begin + size)
            back_send[:, columns] = sum(
                dot_nt(grad_qkv[part, other_rows, :], wqkv[part, columns, :]) for part in range(3)
            ).astype(BF)
        pair_back.start()
        for begin, size in column_blocks(width):
            columns = slice(begin, begin + size)
            input_grad[:, columns] = sum(
                dot_nt(grad_qkv[part, own_rows, :], wqkv[part, columns, :]) for part in range(3)
            )

    def small_copy(k):
        target = sibling if k == cfg.bits else (peer[k], core)
        return send(
            small, small_in.at[k], small_send_sem.at[k], small_recv_sem.at[k], target
        )

    def finish_rows():
        pair_part.wait()
        pair_back.wait()
        gain = gain_one[...]

        def last_rows(step, carry):
            block = pl.ds(pl.multiple_of(step * 32, 32), 32)
            whole = pl.ds(pl.multiple_of(own_begin + step * 32, 32), 32)
            grad = input_grad[block, :] + back_in[block, :].astype(F32)
            x = hid[whole, :].astype(F32)
            inv = lax.rsqrt(jnp.mean(x * x, axis=1, keepdims=True) + EPS)
            unit = x * inv
            scaled = grad * gain
            inner = jnp.mean(scaled * unit, axis=1, keepdims=True)
            input_grad[block, :] = grad_acc[whole, :] + inv * (scaled - unit * inner)
            layer_out[block, :] = (
                middle[whole, :] + out_acc[whole, :] + part_in[block, :].astype(F32)
            )
            small[0:1, :width] += jnp.sum(grad * unit, axis=0, keepdims=True)
            return carry

        lax.fori_loop(0, rows // 32, last_rows, 0)
        small_copy(0).start()

    def small_stage(k):
        small_copy(k).wait()
        if k == cfg.bits:
            row = lax.broadcasted_iota(jnp.int32, small.shape, 0)
            small_out[...] = small[...] + jnp.where(row < 2, small_in[k], 0.0)
        else:
            small[...] = small[...] + small_in[k]
            small_copy(k + 1).start()

    def chunk_kind(chunk):
        tail_part = lax.div(chunk, cfg.ff_total)
        kind = lax.rem(chunk, 3)
        which = (1 - tail_part) * lax.div(kind + 1, 2) + 2 * tail_part
        y_first = 1 - lax.div(2 - which, 2)
        return which, y_first

    def stage_copy(k, chunk, target):
        slot = lax.rem(chunk, SLOTS)
        return send(
            stage_send[k].at[slot],
            stage_in[k].at[chunk],
            stage_send_sem.at[k, slot],
            stage_recv_sem.at[k, chunk],
            (target, core),
        )

    def stage_target(k, chunk):
        if k > 0:
            return peer[k + 1]
        y_first = chunk_kind(chunk)[1]
        return y_first * peer[0] + (1 - y_first) * peer[1]

    def form(chunk):
        which, y_first = chunk_kind(chunk)
        slot = lax.rem(chunk, SLOTS)
        first_bit = y_first * bit[1] + (1 - y_first) * bit[0]
        second_bit = y_first * bit[0] + (1 - y_first) * bit[1]

        @pl.when(chunk == 0)
        def _():
            left_copy(0).wait()

        @pl.when(chunk == 1)
        def _():
            left_copy(1).wait()

        @pl.when(chunk == cfg.ff_total)
        def _():
            left_copy(2).wait()

        right_copy(chunk, 0).wait()

        def product(left, quarter):
            return dot(left_own[left, first_bit, quarter], right_own[chunk]) + dot(
                left_in[left, quarter], right_in[chunk]
            )

        @pl.when(chunk < cfg.chunks - 1)
        def _():
            stage_send[0][slot] = product(which, 1 - second_bit).astype(BF)
            stage_copy(0, chunk, stage_target(0, chunk)).start()
            stage_own[0][slot] = product(which, second_bit)

        @pl.when(chunk == cfg.chunks - 1)
        def _():
            left_copy(3).wait()
            split = lax.broadcasted_iota(jnp.int32, (cfg.quarter, CW), 1) < CW - hw

            def both(quarter):
                return jnp.where(split, product(2, quarter), product(3, quarter))

            stage_send[0][slot] = both(1 - second_bit).astype(BF)
            stage_copy(0, chunk, stage_target(0, chunk)).start()
            stage_own[0][slot] = both(second_bit)

    def halve(k, chunk):
        slot = lax.rem(chunk, SLOTS)
        stage_copy(k - 1, chunk, stage_target(k - 1, chunk)).wait()
        if k == stages:
            final_out[chunk] = stage_own[k - 1][slot] + stage_in[k - 1][chunk].astype(F32)
            return
        half = cfg.stage_rows[k]
        mine = bit[k + 1]

        def total(which):
            part = pl.ds(pl.multiple_of(which * half, 16), half)
            return stage_own[k - 1][slot, part, :] + stage_in[k - 1][chunk, part, :].astype(F32)

        stage_send[k][slot] = total(1 - mine).astype(BF)
        stage_copy(k, chunk, stage_target(k, chunk)).start()
        stage_own[k][slot] = total(mine)

    last_ff = 3 * (cfg.ff_chunks - 1)
    pieces = [exchange_sums, norm_two_back, attention_back, norm_one_sums, finish_rows]
    pieces += [functools.partial(small_stage, k) for k in range(cfg.bits + 1)]
    ticks = max(LAG + cfg.chunks + GAP * stages, last_ff + len(pieces))

    def tick(t, carry):
        for k in range(stages, 0, -1):
            chunk = t - LAG - GAP * k

            @pl.when(jnp.logical_and(chunk >= 0, chunk < cfg.chunks))
            def _(k=k, chunk=chunk):
                halve(k, chunk)

        new = t - LAG

        @pl.when(jnp.logical_and(new >= 0, new < cfg.chunks))
        def _():
            form(new)

        @pl.when(jnp.logical_and(lax.rem(t, 3) == 0, t <= last_ff))
        def _():
            feed_forward(lax.div(t, 3))

        for index, piece in enumerate(pieces):

            @pl.when(t == last_ff + index)
            def _(piece=piece):
                piece()

        return carry

    lax.fori_loop(0, ticks, tick, 0)


def shards(
    mesh,
    hidden_in,
    attention_gain,
    query_weight,
    key_weight,
    value_weight,
    output_weight,
    position_bias,
    feedforward_gain,
    gate_weight,
    up_weight,
    down_weight,
    cotangent,
    item_lengths,
    item_group,
    bucket_ids,
):
    rows, width = hidden_in.shape
    head_width = query_weight.shape[1]
    hidden = gate_weight.shape[1]
    buckets = position_bias.shape[0]
    cfg = Sizes(mesh.shape["dp"], rows, width, head_width, hidden, buckets)
    seq, stages = cfg.seq, cfg.stages
    any_spec = pl.BlockSpec(memory_space=pl.ANY)
    vmem = pl.BlockSpec(memory_space=pltpu.VMEM)
    smem = pl.BlockSpec(memory_space=pltpu.SMEM)
    small_shape = (8, cfg.wide)
    scratch = [
        pltpu.VMEM((seq, width), BF),
        pltpu.VMEM((seq, width), BF),
        pltpu.VMEM((3, width, head_width), BF),
        pltpu.VMEM((2, head_width, width), BF),
        pltpu.VMEM((2, width, CW), BF),
        pltpu.VMEM((2, width, CW), BF),
        pltpu.VMEM((2, CW, width), BF),
        pltpu.VMEM((seq, width), BF),
        pltpu.VMEM((seq, width), BF),
        pltpu.VMEM((seq, width), F32),
        pltpu.VMEM((3, seq, head_width), BF),
        pltpu.VMEM((cfg.heads, seq, seq), F32),
        pltpu.VMEM((2, seq, head_width), BF),
        pltpu.VMEM((width + cfg.shard_pad, seq), F32),
        pltpu.VMEM((4, 2, 2, cfg.quarter, seq), BF),
        pltpu.VMEM((4, 2, cfg.quarter, seq), BF),
        pltpu.VMEM((cfg.chunks, seq, CW), BF),
        pltpu.VMEM((cfg.chunks, seq, CW), BF),
        pltpu.VMEM((seq, width), F32),
        pltpu.VMEM((seq, width), F32),
        pltpu.VMEM((seq, width), BF),
        pltpu.VMEM((seq, width), BF),
        pltpu.VMEM((rows, width), BF),
        pltpu.VMEM((rows, width), BF),
        pltpu.VMEM((rows, width), BF),
        pltpu.VMEM((rows, width), BF),
        pltpu.VMEM((seq, width), BF),
        pltpu.VMEM((3, seq, head_width), BF),
        pltpu.VMEM(small_shape, F32),
        pltpu.VMEM((cfg.bits + 1,) + small_shape, F32),
    ]
    scratch += [pltpu.VMEM((SLOTS, size, CW), F32) for size in cfg.stage_rows]
    scratch += [pltpu.VMEM((SLOTS, size, CW), BF) for size in cfg.stage_rows]
    scratch += [pltpu.VMEM((cfg.chunks, size, CW), BF) for size in cfg.stage_rows]
    dma = pltpu.SemaphoreType.DMA
    scratch += [
        dma((6,)),
        dma((2, 3)),
        dma((7,)),
        dma((7,)),
        dma((4,)),
        dma((4,)),
        dma((cfg.chunks,)),
        dma((cfg.chunks,)),
        dma((stages, SLOTS)),
        dma((stages, cfg.chunks)),
        dma((cfg.bits + 1,)),
        dma((cfg.bits + 1,)),
    ]
    padded_ids = jnp.pad(bucket_ids, (0, 2 * seq - bucket_ids.shape[0]), constant_values=-1)
    layer_out, input_grad, small_sum, final = pl.pallas_call(
        functools.partial(layer_kernel, cfg),
        out_shape=[
            jax.ShapeDtypeStruct((rows, width), F32),
            jax.ShapeDtypeStruct((rows, width), F32),
            jax.ShapeDtypeStruct(small_shape, F32),
            jax.ShapeDtypeStruct((cfg.chunks, cfg.shard_pad, CW), F32),
        ],
        in_specs=[
            any_spec,
            vmem,
            any_spec,
            any_spec,
            any_spec,
            any_spec,
            smem,
            vmem,
            any_spec,
            any_spec,
            any_spec,
            any_spec,
            smem,
            smem,
            vmem,
        ],
        out_specs=[vmem, vmem, vmem, vmem],
        scratch_shapes=scratch,
        compiler_params=pltpu.CompilerParams(
            collective_id=0, has_side_effects=True, vmem_limit_bytes=60 * 1024 * 1024
        ),
        cost_estimate=pl.CostEstimate(
            flops=14 * 10**9, bytes_accessed=24 * 10**6, transcendentals=10**6
        ),
    )(
        hidden_in,
        attention_gain.reshape(1, width),
        query_weight,
        key_weight,
        value_weight,
        output_weight,
        position_bias,
        feedforward_gain.reshape(1, width),
        gate_weight,
        up_weight,
        down_weight,
        cotangent,
        item_lengths,
        item_group,
        padded_ids.reshape(1, -1),
    )

    ff = cfg.ff_total
    shard = cfg.shard

    def joined(first):
        part = final[first:ff:3, :shard, :]
        return jnp.transpose(part, (1, 0, 2)).reshape(shard, hidden)

    down_sum = jnp.transpose(final[0:ff:3, :shard, :], (0, 2, 1)).reshape(hidden, shard)
    attention = jnp.transpose(final[ff:, :shard, :], (1, 0, 2)).reshape(shard, 4 * head_width)
    query_sum, key_sum, value_sum = (
        attention[:, part * head_width : (part + 1) * head_width] for part in range(3)
    )
    output_sum = attention[:, 3 * head_width :].T
    onehot = (
        bucket_ids[None, :] == jnp.arange(buckets, dtype=jnp.int32)[:, None]
    ).astype(F32)
    diagonals = small_sum[2 : 2 + cfg.heads, : bucket_ids.shape[0]]
    bias_total = lax.dot_general(
        onehot, diagonals, (((1,), (1,)), ((), ())), precision=lax.Precision.HIGHEST
    )
    return (
        layer_out,
        input_grad,
        small_sum[0, :width],
        query_sum,
        key_sum,
        value_sum,
        output_sum,
        bias_total,
        small_sum[1, :width],
        joined(1),
        joined(2),
        down_sum,
    )


def solution(mesh):
    in_specs = (
        P(("dp", "mp"), None),
        P(),
        P(None, "mp"),
        P(None, "mp"),
        P(None, "mp"),
        P("mp", None),
        P(None, "mp"),
        P(),
        P(None, "mp"),
        P(None, "mp"),
        P("mp", None),
        P(("dp", "mp"), None),
        P(),
        P(),
        P(),
    )
    out_specs = (
        P(("dp", "mp"), None),
        P(("dp", "mp"), None),
        P(),
        P("dp", "mp"),
        P("dp", "mp"),
        P("dp", "mp"),
        P("mp", "dp"),
        P(None, "mp"),
        P(),
        P("dp", "mp"),
        P("dp", "mp"),
        P("mp", "dp"),
    )
    return jax.shard_map(
        functools.partial(shards, mesh),
        mesh=mesh,
        in_specs=in_specs,
        out_specs=out_specs,
        check_vma=False,
    )
```

```python
import functools
import math

import jax
import jax.numpy as jnp
from jax import lax
from jax.experimental import pallas as pl
from jax.experimental.pallas import tpu as pltpu
from jax.sharding import PartitionSpec as P

DKV = 64
CW = 256
EPS = 1e-06
LAG = 3
GAP = 2
SLOTS = 3
STEP = 64
MROWS = 368
BF = jnp.bfloat16
F32 = jnp.float32
MESH = pl.DeviceIdType.MESH
GELU_C = math.sqrt(2.0 / math.pi)


def dot(left, right):
    return lax.dot_general(left, right, (((1,), (0,)), ((), ())), preferred_element_type=F32)


def dot_nt(left, right):
    return lax.dot_general(left, right, (((1,), (1,)), ((), ())), preferred_element_type=F32)


def dot_tn(left, right):
    return lax.dot_general(left, right, (((0,), (0,)), ((), ())), preferred_element_type=F32)


def blocks_of(extent, step):
    return [slice(begin, min(begin + step, extent)) for begin in range(0, extent, step)]


def fold(block):
    return jnp.sum(block.reshape(block.shape[0] // 8, 8, block.shape[1]), axis=0)


class Sizes:
    def __init__(self, dp, local_rows, width, head_width, hidden, buckets):
        self.dp = dp
        self.bits = dp.bit_length() - 1
        self.local_rows = local_rows
        self.seq = 2 * local_rows
        self.width = width
        self.head_width = head_width
        self.heads = head_width // DKV
        self.hidden = hidden
        self.buckets = buckets
        self.shard = width // dp
        self.shard_pad = -(-self.shard // 16) * 16
        self.quarter = self.shard_pad * dp // 4
        self.ff_chunks = hidden // CW
        self.ff_total = 3 * self.ff_chunks
        self.chunks = self.ff_total + 4 * head_width // CW
        self.stage_rows = [self.quarter >> k for k in range(self.bits - 1)]
        self.stages = len(self.stage_rows)
        self.wide = -(-width // 256) * 256
        self.tall = width + self.shard_pad


def layer_kernel(
    cfg,
    hidden_hbm,
    gain_one,
    wq_hbm,
    wk_hbm,
    wv_hbm,
    wo_hbm,
    position_bias,
    gain_two,
    wg_hbm,
    wu_hbm,
    wd_hbm,
    cot_hbm,
    lengths,
    groups,
    bucket_ids,
    layer_out,
    input_grad,
    small_out,
    ff_out,
    query_out,
    key_out,
    value_out,
    output_out,
    hid,
    cot_raw,
    cot,
    gains,
    wqkv,
    wo,
    wo_t,
    wg,
    wu,
    wd,
    normed_one,
    normed_two,
    middle,
    qkv,
    probs,
    attended,
    trans,
    left_own,
    left_in,
    right_own,
    right_in,
    out_acc,
    grad_acc,
    grad_send,
    grad_in,
    part_send,
    part_in,
    back_send,
    back_in,
    grad_branch,
    grad_qkv,
    small,
    small_in,
    att_final,
    *rest,
):
    stages = cfg.stages
    stage_own = rest[:stages]
    stage_send = rest[stages : 2 * stages]
    stage_in = rest[2 * stages : 3 * stages]
    (
        load_sem,
        weight_sem,
        pair_send_sem,
        pair_recv_sem,
        left_send_sem,
        left_recv_sem,
        right_send_sem,
        right_recv_sem,
        stage_send_sem,
        stage_recv_sem,
        small_send_sem,
        small_recv_sem,
    ) = rest[3 * stages :]

    seq, rows, width, hw, heads = cfg.seq, cfg.local_rows, cfg.width, cfg.head_width, cfg.heads
    me = lax.axis_index("dp")
    core = lax.axis_index("mp")
    bit = [lax.rem(lax.div(me, 1 << k), 2) for k in range(cfg.bits)]
    peer = [me + (1 - 2 * bit[k]) * (1 << k) for k in range(cfg.bits)]
    sibling = (me, 1 - core)
    own_lanes = pl.ds(pl.multiple_of(core * rows, rows), rows)
    other_lanes = pl.ds(pl.multiple_of((1 - core) * rows, rows), rows)

    def send(src, dst, send_sem, recv_sem, target):
        return pltpu.make_async_remote_copy(
            src_ref=src,
            dst_ref=dst,
            send_sem=send_sem,
            recv_sem=recv_sem,
            device_id=target,
            device_id_type=MESH,
        )

    loads = [
        pltpu.make_async_copy(hidden_hbm, hid.at[core], load_sem.at[0]),
        pltpu.make_async_copy(cot_hbm, cot_raw.at[core], load_sem.at[1]),
        pltpu.make_async_copy(wq_hbm, wqkv.at[0], load_sem.at[2]),
        pltpu.make_async_copy(wk_hbm, wqkv.at[1], load_sem.at[3]),
        pltpu.make_async_copy(wv_hbm, wqkv.at[2], load_sem.at[4]),
        pltpu.make_async_copy(wo_hbm, wo.at[core], load_sem.at[5]),
    ]
    for load in loads:
        load.start()

    def weight_loads(chunk, slot):
        columns = pl.ds(pl.multiple_of(chunk * CW, CW), CW)
        return [
            pltpu.make_async_copy(src.at[:, columns], dst.at[slot], weight_sem.at[slot, index])
            for index, (src, dst) in enumerate(((wg_hbm, wg), (wu_hbm, wu), (wd_hbm, wd)))
        ]

    barrier = pltpu.get_barrier_semaphore()
    pl.semaphore_signal(barrier, inc=1, device_id=sibling, device_id_type=MESH)
    for k in range(cfg.bits):
        pl.semaphore_signal(barrier, inc=1, device_id=(peer[k], core), device_id_type=MESH)
    for index, gain in enumerate((gain_one, gain_two)):
        for block in blocks_of(width, 128):
            size = block.stop - block.start
            gains[index, block, :] = jnp.transpose(
                jnp.broadcast_to(gain[0:1, block], (128, size))
            )
    pl.semaphore_wait(barrier, cfg.bits + 1)

    pair_hid = send(
        hidden_hbm, hid.at[core], pair_send_sem.at[0], pair_recv_sem.at[0], sibling
    )
    pair_cot = send(
        cot_hbm, cot_raw.at[core], pair_send_sem.at[1], pair_recv_sem.at[1], sibling
    )
    pair_wo = send(wo_hbm, wo.at[core], pair_send_sem.at[2], pair_recv_sem.at[2], sibling)
    pair_hid.start()
    pair_cot.start()
    pair_wo.start()
    pair_att = send(
        attended.at[core], attended.at[core], pair_send_sem.at[3], pair_recv_sem.at[3], sibling
    )
    pair_grad = send(grad_send, grad_in, pair_send_sem.at[4], pair_recv_sem.at[4], sibling)
    pair_part = send(part_send, part_in, pair_send_sem.at[5], pair_recv_sem.at[5], sibling)
    pair_back = send(back_send, back_in, pair_send_sem.at[6], pair_recv_sem.at[6], sibling)

    for slot in range(2):
        for load in weight_loads(slot, slot):
            load.start()

    group_len = jnp.int32(0)
    for item in range(lengths.shape[0]):
        group_len = group_len + jnp.where(groups[item] == me, lengths[item], 0)

    left_axis = (0, 1, 1, 1)

    def build_left(source, which):
        first = left_axis[which]
        for index in range(cfg.dp):
            low = (index & 1, (index >> 1) & 1)
            place = 0
            for k in range(2, cfg.bits):
                place = 2 * place + ((index >> k) & 1)
            block = source[index * cfg.shard : index * cfg.shard + cfg.shard_pad, :]
            left_own[
                which,
                low[first],
                low[1 - first],
                place * cfg.shard_pad : (place + 1) * cfg.shard_pad,
                :,
            ] = block.astype(BF)

    def left_copy(which):
        first = left_axis[which]
        return send(
            left_own.at[which, 1 - bit[first]],
            left_in.at[which],
            left_send_sem.at[which],
            left_recv_sem.at[which],
            (peer[first], core),
        )

    def right_copy(chunk, first):
        return send(
            right_own.at[chunk],
            right_in.at[chunk],
            right_send_sem.at[chunk],
            right_recv_sem.at[chunk],
            (peer[first], core),
        )

    for scratch in (trans, grad_acc):
        scratch[width:, :] = jnp.zeros((cfg.tall - width, seq), F32)

    step_rows = STEP
    steps = width // step_rows

    def rows_at(step):
        return pl.ds(pl.multiple_of(step * step_rows, step_rows), step_rows)

    def whole(ref, block):
        return jnp.concatenate([ref[0, block, :], ref[1, block, :]], axis=1)

    def gain_at(index, block, lanes):
        part = gains[index, block, :]
        return jnp.concatenate([part] * (lanes // 128), axis=1)

    def column_sum(term, lanes):
        zero = jnp.zeros((8, lanes), F32)
        total = lax.fori_loop(0, steps, lambda i, acc: acc + fold(term(rows_at(i))), zero)
        return jnp.sum(total, axis=0, keepdims=True)

    def inverse_rms(term, lanes):
        def square(block):
            x = term(block)
            return x * x

        return lax.rsqrt(column_sum(square, lanes) * (1.0 / width) + EPS)

    loads[0].wait()
    pair_hid.wait()

    def x_at(block):
        return whole(hid, block).astype(F32)

    inv_one = inverse_rms(x_at, seq)

    def norm_one_rows(step, carry):
        block = rows_at(step)
        normed = x_at(block) * inv_one * gain_at(0, block, seq)
        trans[block, :] = normed
        normed_one[block, :] = normed.astype(BF)
        return carry

    lax.fori_loop(0, steps, norm_one_rows, 0)

    for part in range(3):
        loads[2 + part].wait()
        qkv[part] = dot(wqkv[part], normed_one[...]).astype(BF)

    key_valid = lax.broadcasted_iota(jnp.int32, (seq, seq), 0) < group_len
    ids = bucket_ids[...]
    for head in range(heads):
        part = slice(head * DKV, (head + 1) * DKV)
        by_offset = jnp.zeros(ids.shape, F32)
        for bucket in range(cfg.buckets):
            by_offset = jnp.where(ids == bucket, position_bias[head, bucket], by_offset)
        bias = pltpu.roll(
            jnp.broadcast_to(by_offset, (seq, 2 * seq)),
            seq + 1,
            1,
            stride=1,
            stride_axis=0,
        )[:, :seq]
        scores = dot_tn(qkv[1, part, :], qkv[0, part, :]) + bias
        scores = jnp.where(key_valid, scores, -1e30)
        exps = jnp.exp(scores - jnp.max(scores, axis=0, keepdims=True))
        prob = exps / jnp.sum(exps, axis=0, keepdims=True)
        probs[head] = prob
        attended[core, part, :] = dot(qkv[2, part, :], prob.astype(BF)).astype(BF)
    pair_att.start()

    build_left(trans, 2)
    left_copy(2).start()
    loads[1].wait()
    pair_cot.wait()
    row_valid = lax.broadcasted_iota(jnp.int32, (step_rows, seq), 1) < group_len

    def mask_rows(step, carry):
        block = rows_at(step)
        trans[block, :] = jnp.where(row_valid, whole(cot_raw, block).astype(F32), 0.0)
        return carry

    lax.fori_loop(0, steps, mask_rows, 0)
    build_left(trans, 0)
    left_copy(0).start()
    for block in blocks_of(width, 128):
        cot[:, block] = jnp.transpose(trans[block, :]).astype(BF)

    loads[5].wait()
    pair_wo.wait()
    for block in blocks_of(width, 128):
        wo_t[block, :] = jnp.transpose(
            jnp.concatenate([wo[0, :, block], wo[1, :, block]], axis=0).astype(F32)
        ).astype(BF)
    pair_att.wait()
    both = attended[...].reshape(2 * hw, seq)
    for block in blocks_of(width, MROWS):
        middle[block, :] = x_at(block) + dot(wo_t[block, :], both)

    inv_two = inverse_rms(lambda block: middle[block, :], seq)

    def norm_two_rows(step, carry):
        block = rows_at(step)
        trans[block, :] = middle[block, :] * inv_two * gain_at(1, block, seq)
        out_acc[block, :] = jnp.zeros((step_rows, seq), F32)
        grad_acc[block, :] = jnp.zeros((step_rows, seq), F32)
        return carry

    lax.fori_loop(0, steps, norm_two_rows, 0)
    build_left(trans, 1)
    left_copy(1).start()
    for block in blocks_of(width, 128):
        normed_two[:, block] = jnp.transpose(trans[block, :]).astype(BF)
    small[...] = jnp.zeros_like(small)

    def feed_forward(chunk):
        slot = lax.rem(chunk, 2)
        for load in weight_loads(chunk, slot):
            load.wait()
        normed = normed_two[...]
        gate = dot(normed, wg[slot])
        up = dot(normed, wu[slot])
        grad_hidden = dot(cot[...], wd[slot])
        square = gate * gate
        tanh = jnp.tanh(GELU_C * (gate + 0.044715 * (square * gate)))
        half = 0.5 * (1.0 + tanh)
        gelu = gate * half
        slope = half + (0.5 * GELU_C) * gate * (1.0 - tanh * tanh) * (
            1.0 + (3 * 0.044715) * square
        )
        hidden = (gelu * up).astype(BF)
        grad_gate = (grad_hidden * up * slope).astype(BF)
        grad_up = (grad_hidden * gelu).astype(BF)
        base = 3 * chunk
        right_own[base] = hidden
        right_own[base + 1] = grad_gate
        right_own[base + 2] = grad_up
        right_copy(base, 0).start()
        right_copy(base + 1, 1).start()
        right_copy(base + 2, 1).start()
        for block in blocks_of(width, MROWS):
            out_acc[block, :] += dot_nt(wd[slot, block, :], hidden)
            grad_acc[block, :] += dot_nt(wg[slot, block, :], grad_gate) + dot_nt(
                wu[slot, block, :], grad_up
            )

        @pl.when(chunk < cfg.ff_chunks - 2)
        def _():
            for load in weight_loads(chunk + 2, slot):
                load.start()

    def exchange_sums():
        grad_send[...] = grad_acc[:width, :].astype(BF)
        pair_grad.start()
        part_send[...] = out_acc[:, other_lanes].astype(BF)
        pair_part.start()

    def lane_mask(shape, dimension):
        lane = lax.broadcasted_iota(jnp.int32, shape, dimension)
        return (lax.div(lane, rows) == core).astype(F32)

    def lane_sums(weights, source):
        return lax.dot_general(
            weights,
            source,
            (((1,), (1,)), ((), ())),
            precision=lax.Precision.HIGHEST,
            preferred_element_type=F32,
        )[0:1, :]

    def norm_two_back():
        pair_grad.wait()

        def grad_at(block):
            return grad_acc[block, :] + grad_in[block, :].astype(F32)

        inv = inverse_rms(lambda block: middle[block, :], seq)
        inner = (
            column_sum(
                lambda block: grad_at(block) * gain_at(1, block, seq) * middle[block, :], seq
            )
            * inv
            * (1.0 / width)
        )

        def back_rows(step, carry):
            block = rows_at(step)
            grad = grad_at(block)
            unit = middle[block, :] * inv
            masked = jnp.where(row_valid, whole(cot_raw, block).astype(F32), 0.0)
            total = masked + inv * (grad * gain_at(1, block, seq) - unit * inner)
            trans[block, :] = grad * unit
            grad_acc[block, :] = total
            grad_branch[block, :] = total.astype(BF)
            return carry

        lax.fori_loop(0, steps, back_rows, 0)
        build_left(grad_acc, 3)
        left_copy(3).start()
        mask = lane_mask((8, seq), 1)
        small[1:2, :width] = lane_sums(mask, trans[:width, :])

    def attention_back():
        grad_att = dot(wo[core], grad_branch[...]).astype(BF)
        flip = (
            lax.broadcasted_iota(jnp.int32, (seq, seq), 0)
            + lax.broadcasted_iota(jnp.int32, (seq, seq), 1)
            == seq - 1
        ).astype(BF)
        for head in range(heads):
            part = slice(head * DKV, (head + 1) * DKV)
            grad_mixed = grad_att[part, :]
            prob = probs[head]
            grad_probs = dot_tn(qkv[2, part, :], grad_mixed)
            inner = jnp.sum(prob * grad_probs, axis=0, keepdims=True)
            grad_scores = (prob * (grad_probs - inner)).astype(BF)
            grad_qkv[0, part, :] = dot(qkv[1, part, :], grad_scores).astype(BF)
            grad_qkv[1, part, :] = dot_nt(qkv[0, part, :], grad_scores).astype(BF)
            grad_qkv[2, part, :] = dot_nt(grad_mixed, prob.astype(BF)).astype(BF)
            flipped = jnp.concatenate(
                [dot(flip, grad_scores), jnp.zeros((seq, seq), F32)], axis=1
            )
            skewed = pltpu.roll(flipped, 0, 1, stride=1, stride_axis=0)
            small[2 + head : 3 + head, : 2 * seq] = jnp.sum(skewed, axis=0, keepdims=True)
        joined = jnp.concatenate(
            [grad_qkv[...].reshape(3 * hw, seq), attended[core]], axis=0
        ).astype(F32)
        for index in range(cfg.chunks - cfg.ff_total):
            chunk = cfg.ff_total + index
            right_own[chunk] = jnp.transpose(joined[index * CW : (index + 1) * CW, :]).astype(BF)
            right_copy(chunk, 1).start()

    def norm_one_sums():
        for block in blocks_of(width, 128):
            back_send[block, :] = sum(
                dot_tn(wqkv[part, :, block], grad_qkv[part, :, other_lanes]) for part in range(3)
            ).astype(BF)
        pair_back.start()
        for block in blocks_of(width, 128):
            input_grad[block, :] = sum(
                dot_tn(wqkv[part, :, block], grad_qkv[part, :, own_lanes]) for part in range(3)
            )

    def small_copy(k):
        target = sibling if k == cfg.bits else (peer[k], core)
        return send(
            small, small_in.at[k], small_send_sem.at[k], small_recv_sem.at[k], target
        )

    def finish_rows():
        pair_part.wait()
        pair_back.wait()

        def x_own(block):
            return hid[core, block, :].astype(F32)

        def grad_at(block):
            return input_grad[block, :] + back_in[block, :].astype(F32)

        inv = inverse_rms(x_own, rows)
        inner = (
            column_sum(lambda block: grad_at(block) * gain_at(0, block, rows) * x_own(block), rows)
            * inv
            * (1.0 / width)
        )

        def last_rows(step, carry):
            block = rows_at(step)
            grad = grad_at(block)
            unit = x_own(block) * inv
            input_grad[block, :] = grad_acc[block, own_lanes] + inv * (
                grad * gain_at(0, block, rows) - unit * inner
            )
            layer_out[block, :] = (
                middle[block, own_lanes]
                + out_acc[block, own_lanes]
                + part_in[block, :].astype(F32)
            )
            trans[block, :rows] = grad * unit
            return carry

        lax.fori_loop(0, steps, last_rows, 0)
        small[0:1, :width] = lane_sums(jnp.ones((8, rows), F32), trans[:width, :rows])
        small_copy(0).start()

    def small_stage(k):
        small_copy(k).wait()
        if k == cfg.bits:
            row = lax.broadcasted_iota(jnp.int32, small.shape, 0)
            small_out[...] = small[...] + jnp.where(row < 2, small_in[k], 0.0)
        else:
            small[...] = small[...] + small_in[k]
            small_copy(k + 1).start()

    def chunk_kind(chunk):
        tail_part = lax.div(chunk, cfg.ff_total)
        kind = lax.rem(chunk, 3)
        which = (1 - tail_part) * lax.div(kind + 1, 2) + 2 * tail_part
        y_first = 1 - lax.div(2 - which, 2)
        return which, y_first

    def stage_copy(k, chunk, target):
        slot = lax.rem(chunk, SLOTS)
        return send(
            stage_send[k].at[slot],
            stage_in[k].at[chunk],
            stage_send_sem.at[k, slot],
            stage_recv_sem.at[k, chunk],
            (target, core),
        )

    def stage_target(k, chunk):
        if k > 0:
            return peer[k + 1]
        y_first = chunk_kind(chunk)[1]
        return y_first * peer[0] + (1 - y_first) * peer[1]

    def form(chunk):
        which, y_first = chunk_kind(chunk)
        slot = lax.rem(chunk, SLOTS)
        first_bit = y_first * bit[1] + (1 - y_first) * bit[0]
        second_bit = y_first * bit[0] + (1 - y_first) * bit[1]

        @pl.when(chunk == 0)
        def _():
            left_copy(0).wait()

        @pl.when(chunk == 1)
        def _():
            left_copy(1).wait()

        @pl.when(chunk == cfg.ff_total)
        def _():
            left_copy(2).wait()

        right_copy(chunk, 0).wait()

        def product(left, quarter):
            return dot(left_own[left, first_bit, quarter], right_own[chunk]) + dot(
                left_in[left, quarter], right_in[chunk]
            )

        @pl.when(chunk < cfg.chunks - 1)
        def _():
            stage_send[0][slot] = product(which, 1 - second_bit).astype(BF)
            stage_copy(0, chunk, stage_target(0, chunk)).start()
            stage_own[0][slot] = product(which, second_bit)

        @pl.when(chunk == cfg.chunks - 1)
        def _():
            left_copy(3).wait()
            split = lax.broadcasted_iota(jnp.int32, (cfg.quarter, CW), 1) < CW - hw

            def mixed(quarter):
                return jnp.where(split, product(2, quarter), product(3, quarter))

            stage_send[0][slot] = mixed(1 - second_bit).astype(BF)
            stage_copy(0, chunk, stage_target(0, chunk)).start()
            stage_own[0][slot] = mixed(second_bit)

    def halve(k, chunk):
        slot = lax.rem(chunk, SLOTS)
        stage_copy(k - 1, chunk, stage_target(k - 1, chunk)).wait()
        if k == stages:
            result = stage_own[k - 1][slot] + stage_in[k - 1][chunk].astype(F32)

            @pl.when(chunk < cfg.ff_total)
            def _():
                columns = pl.ds(pl.multiple_of(lax.div(chunk, 3) * CW, CW), CW)
                ff_out[lax.rem(chunk, 3), :, columns] = result[: cfg.shard, :]

            @pl.when(chunk >= cfg.ff_total)
            def _():
                att_final[lax.rem(chunk, cfg.ff_total)] = result

            return
        half = cfg.stage_rows[k]
        mine = bit[k + 1]

        def total(which):
            part = pl.ds(pl.multiple_of(which * half, 16), half)
            return stage_own[k - 1][slot, part, :] + stage_in[k - 1][chunk, part, :].astype(F32)

        stage_send[k][slot] = total(1 - mine).astype(BF)
        stage_copy(k, chunk, stage_target(k, chunk)).start()
        stage_own[k][slot] = total(mine)

    last_ff = 3 * (cfg.ff_chunks - 1)
    pieces = [exchange_sums, norm_two_back, attention_back, norm_one_sums, finish_rows]
    pieces += [functools.partial(small_stage, k) for k in range(cfg.bits + 1)]
    ticks = max(LAG + cfg.chunks + GAP * stages, last_ff + len(pieces))

    def tick(t, carry):
        for k in range(stages, 0, -1):
            chunk = t - LAG - GAP * k

            @pl.when(jnp.logical_and(chunk >= 0, chunk < cfg.chunks))
            def _(k=k, chunk=chunk):
                halve(k, chunk)

        new = t - LAG

        @pl.when(jnp.logical_and(new >= 0, new < cfg.chunks))
        def _():
            form(new)

        @pl.when(jnp.logical_and(lax.rem(t, 3) == 0, t <= last_ff))
        def _():
            feed_forward(lax.div(t, 3))

        for index, piece in enumerate(pieces):

            @pl.when(t == last_ff + index)
            def _(piece=piece):
                piece()

        return carry

    lax.fori_loop(0, ticks, tick, 0)

    flat = jnp.concatenate([att_final[index] for index in range(cfg.chunks - cfg.ff_total)], axis=1)
    for part, ref in enumerate((query_out, key_out, value_out)):
        ref[...] = flat[: cfg.shard, part * hw : (part + 1) * hw]
    output_out[...] = jnp.transpose(flat[:, 3 * hw :])[:, : cfg.shard]


def shards(
    mesh,
    hidden_in,
    attention_gain,
    query_weight,
    key_weight,
    value_weight,
    output_weight,
    position_bias,
    feedforward_gain,
    gate_weight,
    up_weight,
    down_weight,
    cotangent,
    item_lengths,
    item_group,
    bucket_ids,
):
    rows, width = hidden_in.shape
    hw = query_weight.shape[1]
    hidden = gate_weight.shape[1]
    buckets = position_bias.shape[0]
    cfg = Sizes(mesh.shape["dp"], rows, width, hw, hidden, buckets)
    seq, stages, shard = cfg.seq, cfg.stages, cfg.shard
    any_spec = pl.BlockSpec(memory_space=pl.ANY)
    vmem = pl.BlockSpec(memory_space=pltpu.VMEM)
    smem = pl.BlockSpec(memory_space=pltpu.SMEM)
    small_shape = (8, cfg.wide)
    scratch = [
        pltpu.VMEM((2, width, rows), BF),
        pltpu.VMEM((2, width, rows), BF),
        pltpu.VMEM((seq, width), BF),
        pltpu.VMEM((2, width, 128), F32),
        pltpu.VMEM((3, hw, width), BF),
        pltpu.VMEM((2, hw, width), BF),
        pltpu.VMEM((width, 2 * hw), BF),
        pltpu.VMEM((2, width, CW), BF),
        pltpu.VMEM((2, width, CW), BF),
        pltpu.VMEM((2, width, CW), BF),
        pltpu.VMEM((width, seq), BF),
        pltpu.VMEM((seq, width), BF),
        pltpu.VMEM((width, seq), F32),
        pltpu.VMEM((3, hw, seq), BF),
        pltpu.VMEM((cfg.heads, seq, seq), F32),
        pltpu.VMEM((2, hw, seq), BF),
        pltpu.VMEM((cfg.tall, seq), F32),
        pltpu.VMEM((4, 2, 2, cfg.quarter, seq), BF),
        pltpu.VMEM((4, 2, cfg.quarter, seq), BF),
        pltpu.VMEM((cfg.chunks, seq, CW), BF),
        pltpu.VMEM((cfg.chunks, seq, CW), BF),
        pltpu.VMEM((width, seq), F32),
        pltpu.VMEM((cfg.tall, seq), F32),
        pltpu.VMEM((width, seq), BF),
        pltpu.VMEM((width, seq), BF),
        pltpu.VMEM((width, rows), BF),
        pltpu.VMEM((width, rows), BF),
        pltpu.VMEM((width, rows), BF),
        pltpu.VMEM((width, rows), BF),
        pltpu.VMEM((width, seq), BF),
        pltpu.VMEM((3, hw, seq), BF),
        pltpu.VMEM(small_shape, F32),
        pltpu.VMEM((cfg.bits + 1,) + small_shape, F32),
        pltpu.VMEM((cfg.chunks - cfg.ff_total, cfg.shard_pad, CW), F32),
    ]
    scratch += [pltpu.VMEM((SLOTS, size, CW), F32) for size in cfg.stage_rows]
    scratch += [pltpu.VMEM((SLOTS, size, CW), BF) for size in cfg.stage_rows]
    scratch += [pltpu.VMEM((cfg.chunks, size, CW), BF) for size in cfg.stage_rows]
    dma = pltpu.SemaphoreType.DMA
    scratch += [
        dma((6,)),
        dma((2, 3)),
        dma((7,)),
        dma((7,)),
        dma((4,)),
        dma((4,)),
        dma((cfg.chunks,)),
        dma((cfg.chunks,)),
        dma((stages, SLOTS)),
        dma((stages, cfg.chunks)),
        dma((cfg.bits + 1,)),
        dma((cfg.bits + 1,)),
    ]
    reversed_ids = jnp.pad(
        jnp.flip(bucket_ids), (0, 2 * seq - bucket_ids.shape[0]), constant_values=-1
    )
    (
        layer_out,
        input_grad,
        small_sum,
        ff_sum,
        query_sum,
        key_sum,
        value_sum,
        output_sum,
    ) = pl.pallas_call(
        functools.partial(layer_kernel, cfg),
        out_shape=[
            jax.ShapeDtypeStruct((width, rows), F32),
            jax.ShapeDtypeStruct((width, rows), F32),
            jax.ShapeDtypeStruct(small_shape, F32),
            jax.ShapeDtypeStruct((3, shard, hidden), F32),
            jax.ShapeDtypeStruct((shard, hw), F32),
            jax.ShapeDtypeStruct((shard, hw), F32),
            jax.ShapeDtypeStruct((shard, hw), F32),
            jax.ShapeDtypeStruct((hw, shard), F32),
        ],
        in_specs=[
            any_spec,
            vmem,
            any_spec,
            any_spec,
            any_spec,
            any_spec,
            smem,
            vmem,
            any_spec,
            any_spec,
            any_spec,
            any_spec,
            smem,
            smem,
            vmem,
        ],
        out_specs=[vmem] * 8,
        scratch_shapes=scratch,
        compiler_params=pltpu.CompilerParams(
            collective_id=0, has_side_effects=True, vmem_limit_bytes=60 * 1024 * 1024
        ),
        cost_estimate=pl.CostEstimate(
            flops=14 * 10**9, bytes_accessed=24 * 10**6, transcendentals=10**6
        ),
    )(
        hidden_in.T,
        attention_gain.reshape(1, width),
        query_weight.T,
        key_weight.T,
        value_weight.T,
        output_weight,
        position_bias.T,
        feedforward_gain.reshape(1, width),
        gate_weight,
        up_weight,
        down_weight.T,
        cotangent.T,
        item_lengths,
        item_group,
        reversed_ids.reshape(1, -1),
    )
    onehot = (
        jnp.flip(bucket_ids)[None, :] == jnp.arange(buckets, dtype=jnp.int32)[:, None]
    ).astype(F32)
    diagonals = small_sum[2 : 2 + cfg.heads, : bucket_ids.shape[0]]
    bias_total = lax.dot_general(
        onehot, diagonals, (((1,), (1,)), ((), ())), precision=lax.Precision.HIGHEST
    )
    return (
        layer_out.T,
        input_grad.T,
        small_sum[0, :width],
        query_sum,
        key_sum,
        value_sum,
        output_sum,
        bias_total,
        small_sum[1, :width],
        ff_sum[1],
        ff_sum[2],
        ff_sum[0].T,
    )


def solution(mesh):
    in_specs = (
        P(("dp", "mp"), None),
        P(),
        P(None, "mp"),
        P(None, "mp"),
        P(None, "mp"),
        P("mp", None),
        P(None, "mp"),
        P(),
        P(None, "mp"),
        P(None, "mp"),
        P("mp", None),
        P(("dp", "mp"), None),
        P(),
        P(),
        P(),
    )
    out_specs = (
        P(("dp", "mp"), None),
        P(("dp", "mp"), None),
        P(),
        P("dp", "mp"),
        P("dp", "mp"),
        P("dp", "mp"),
        P("mp", "dp"),
        P(None, "mp"),
        P(),
        P("dp", "mp"),
        P("dp", "mp"),
        P("mp", "dp"),
    )
    return jax.shard_map(
        functools.partial(shards, mesh),
        mesh=mesh,
        in_specs=in_specs,
        out_specs=out_specs,
        check_vma=False,
    )
```

```python
import functools
import math

import jax
import jax.numpy as jnp
from jax import lax
from jax.experimental import pallas as pl
from jax.experimental.pallas import tpu as pltpu
from jax.sharding import PartitionSpec as P

DKV = 64
CW = 256
EPS = 1e-06
LAG = 3
GAP = 3
SLOTS = 4
FF_TICKS = 2
SMALL_GAP = 3
AXES = ((0, 1, 2), (1, 0, 2), (2, 1, 0), (2, 1, 0))
STEP = 64
MROWS = 368
BF = jnp.bfloat16
F32 = jnp.float32
MESH = pl.DeviceIdType.MESH
GELU_C = math.sqrt(2.0 / math.pi)


def dot(left, right):
    return lax.dot_general(left, right, (((1,), (0,)), ((), ())), preferred_element_type=F32)


def dot_nt(left, right):
    return lax.dot_general(left, right, (((1,), (1,)), ((), ())), preferred_element_type=F32)


def dot_tn(left, right):
    return lax.dot_general(left, right, (((0,), (0,)), ((), ())), preferred_element_type=F32)


def blocks_of(extent, step):
    return [slice(begin, min(begin + step, extent)) for begin in range(0, extent, step)]


def fold(block):
    return jnp.sum(block.reshape(block.shape[0] // 8, 8, block.shape[1]), axis=0)


class Sizes:
    def __init__(self, dp, local_rows, width, head_width, hidden, buckets):
        self.dp = dp
        self.bits = dp.bit_length() - 1
        self.local_rows = local_rows
        self.seq = 2 * local_rows
        self.width = width
        self.head_width = head_width
        self.heads = head_width // DKV
        self.hidden = hidden
        self.buckets = buckets
        self.shard = width // dp
        self.shard_pad = -(-self.shard // 16) * 16
        self.quarter = self.shard_pad * dp // 4
        self.ff_chunks = hidden // CW
        self.ff_total = 3 * self.ff_chunks
        self.chunks = self.ff_total + 4 * head_width // CW
        self.stage_rows = [self.quarter >> k for k in range(self.bits - 1)]
        self.stages = len(self.stage_rows)
        self.half = -(-width // 256) * 128
        self.tall = width + self.shard_pad
        self.orders = [axes + tuple(range(3, self.bits)) for axes in AXES]


def layer_kernel(
    cfg,
    hidden_hbm,
    gain_one,
    wq_hbm,
    wk_hbm,
    wv_hbm,
    wo_hbm,
    position_bias,
    gain_two,
    wg_hbm,
    wu_hbm,
    wd_hbm,
    cot_hbm,
    lengths,
    groups,
    bucket_ids,
    layer_out,
    input_grad,
    small_out,
    ff_out,
    query_out,
    key_out,
    value_out,
    output_out,
    hid,
    cot_raw,
    cot,
    gains,
    wqkv,
    wo,
    wo_t,
    wg,
    wu,
    wd,
    normed_one,
    normed_two,
    middle,
    qkv,
    probs,
    attended,
    trans,
    left_own,
    left_in,
    right_own,
    right_in,
    out_acc,
    grad_acc,
    grad_send,
    grad_in,
    part_send,
    part_in,
    back_send,
    back_in,
    grad_branch,
    grad_qkv,
    small,
    small_in,
    att_final,
    ids_row,
    *rest,
):
    stages = cfg.stages
    stage_own = rest[:stages]
    stage_send = rest[stages : 2 * stages]
    stage_in = rest[2 * stages : 3 * stages]
    (
        load_sem,
        weight_sem,
        pair_send_sem,
        pair_recv_sem,
        left_send_sem,
        left_recv_sem,
        share_send_sem,
        share_recv_sem,
        right_send_sem,
        right_recv_sem,
        stage_send_sem,
        stage_recv_sem,
        small_send_sem,
        small_recv_sem,
    ) = rest[3 * stages :]

    seq, rows, width, hw, heads = cfg.seq, cfg.local_rows, cfg.width, cfg.head_width, cfg.heads
    me = lax.axis_index("dp")
    core = lax.axis_index("mp")
    bit = [lax.rem(lax.div(me, 1 << k), 2) for k in range(cfg.bits)]
    peer = [me + (1 - 2 * bit[k]) * (1 << k) for k in range(cfg.bits)]
    sibling = (me, 1 - core)
    own_lanes = pl.ds(pl.multiple_of(core * rows, rows), rows)
    other_lanes = pl.ds(pl.multiple_of((1 - core) * rows, rows), rows)

    def send(src, dst, send_sem, recv_sem, target):
        return pltpu.make_async_remote_copy(
            src_ref=src,
            dst_ref=dst,
            send_sem=send_sem,
            recv_sem=recv_sem,
            device_id=target,
            device_id_type=MESH,
        )

    loads = [
        pltpu.make_async_copy(hidden_hbm, hid.at[core], load_sem.at[0]),
        pltpu.make_async_copy(cot_hbm, cot_raw.at[core], load_sem.at[1]),
        pltpu.make_async_copy(wq_hbm, wqkv.at[0], load_sem.at[2]),
        pltpu.make_async_copy(wk_hbm, wqkv.at[1], load_sem.at[3]),
        pltpu.make_async_copy(wv_hbm, wqkv.at[2], load_sem.at[4]),
        pltpu.make_async_copy(wo_hbm, wo.at[core], load_sem.at[5]),
    ]
    for load in loads:
        load.start()

    def weight_loads(chunk, slot):
        columns = pl.ds(pl.multiple_of(chunk * CW, CW), CW)
        return [
            pltpu.make_async_copy(src.at[:, columns], dst.at[slot], weight_sem.at[slot, index])
            for index, (src, dst) in enumerate(((wg_hbm, wg), (wu_hbm, wu), (wd_hbm, wd)))
        ]

    barrier = pltpu.get_barrier_semaphore()
    pl.semaphore_signal(barrier, inc=1, device_id=sibling, device_id_type=MESH)
    for k in range(cfg.bits):
        pl.semaphore_signal(barrier, inc=1, device_id=(peer[k], core), device_id_type=MESH)
    for index, gain in enumerate((gain_one, gain_two)):
        line = gain[...].reshape(1, width)
        for block in blocks_of(width, 128):
            size = block.stop - block.start
            gains[index, block, :] = jnp.transpose(
                jnp.broadcast_to(line[:, block], (128, size))
            )
    pl.semaphore_wait(barrier, cfg.bits + 1)

    pair_hid = send(
        hidden_hbm, hid.at[core], pair_send_sem.at[0], pair_recv_sem.at[0], sibling
    )
    pair_cot = send(
        cot_hbm, cot_raw.at[core], pair_send_sem.at[1], pair_recv_sem.at[1], sibling
    )
    pair_wo = send(wo_hbm, wo.at[core], pair_send_sem.at[2], pair_recv_sem.at[2], sibling)
    pair_hid.start()
    pair_cot.start()
    pair_wo.start()
    pair_att = send(
        attended.at[core], attended.at[core], pair_send_sem.at[3], pair_recv_sem.at[3], sibling
    )
    pair_grad = send(grad_send, grad_in, pair_send_sem.at[4], pair_recv_sem.at[4], sibling)
    pair_part = send(part_send, part_in, pair_send_sem.at[5], pair_recv_sem.at[5], sibling)
    pair_back = send(back_send, back_in, pair_send_sem.at[6], pair_recv_sem.at[6], sibling)

    for slot in range(2):
        for load in weight_loads(slot, slot):
            load.start()

    group_len = jnp.int32(0)
    for item in range(lengths.shape[0]):
        group_len = group_len + jnp.where(groups[item] == me, lengths[item], 0)

    def build_left(source, which):
        order = cfg.orders[which]
        for index in range(cfg.dp):
            bits = [(index >> k) & 1 for k in order]
            place = 0
            for value in bits[2:]:
                place = 2 * place + value
            block = source[index * cfg.shard : index * cfg.shard + cfg.shard_pad, :]
            left_own[
                which,
                bits[0],
                bits[1],
                place * cfg.shard_pad : (place + 1) * cfg.shard_pad,
                :,
            ] = block.astype(BF)

    def left_copy(which):
        first = cfg.orders[which][0]
        return send(
            left_own.at[which, 1 - bit[first], core],
            left_in.at[which, core],
            left_send_sem.at[which],
            left_recv_sem.at[which],
            (peer[first], core),
        )

    def left_share(which):
        return send(
            left_in.at[which, core],
            left_in.at[which, core],
            share_send_sem.at[which],
            share_recv_sem.at[which],
            sibling,
        )

    def left_pass(which):
        left_copy(which).wait()
        left_share(which).start()

    def pick(chunk, level, values):
        ks = [cfg.orders[which][level] for which in range(3)]
        if ks[0] == ks[1] == ks[2]:
            return values[ks[0]]
        tail_part = lax.div(chunk, cfg.ff_total)
        hidden_part = (1 - tail_part) * (1 - lax.div(lax.rem(chunk, 3) + 1, 2))
        parts = (hidden_part, 1 - tail_part - hidden_part, tail_part)
        return sum(part * values[k] for part, k in zip(parts, ks))

    def right_copy(chunk):
        return send(
            right_own.at[chunk],
            right_in.at[chunk],
            right_send_sem.at[chunk],
            right_recv_sem.at[chunk],
            (pick(chunk, 0, peer), core),
        )

    for scratch in (trans, grad_acc):
        scratch[width:, :] = jnp.zeros((cfg.tall - width, seq), F32)

    step_rows = STEP
    steps = width // step_rows

    def rows_at(step):
        return pl.ds(pl.multiple_of(step * step_rows, step_rows), step_rows)

    def whole(ref, block):
        return jnp.concatenate([ref[0, block, :], ref[1, block, :]], axis=1)

    def gain_at(index, block, lanes):
        part = gains[index, block, :]
        return jnp.concatenate([part] * (lanes // 128), axis=1)

    def column_sum(term, lanes):
        zero = jnp.zeros((8, lanes), F32)
        total = lax.fori_loop(0, steps, lambda i, acc: acc + fold(term(rows_at(i))), zero)
        return jnp.sum(total, axis=0, keepdims=True)

    def inverse_rms(term, lanes):
        def square(block):
            x = term(block)
            return x * x

        return lax.rsqrt(column_sum(square, lanes) * (1.0 / width) + EPS)

    loads[0].wait()
    pair_hid.wait()

    def x_at(block):
        return whole(hid, block).astype(F32)

    inv_one = inverse_rms(x_at, seq)

    def norm_one_rows(step, carry):
        block = rows_at(step)
        normed = x_at(block) * inv_one * gain_at(0, block, seq)
        trans[block, :] = normed
        normed_one[block, :] = normed.astype(BF)
        return carry

    lax.fori_loop(0, steps, norm_one_rows, 0)

    for part in range(3):
        loads[2 + part].wait()
        qkv[part] = dot(wqkv[part], normed_one[...]).astype(BF)

    key_valid = lax.broadcasted_iota(jnp.int32, (seq, seq), 0) < group_len
    ids_row[...] = jnp.full(ids_row.shape, -1, jnp.int32)
    ids_row[:, : bucket_ids.shape[0]] = bucket_ids[...].reshape(1, -1)
    ids = ids_row[...]
    for head in range(heads):
        part = slice(head * DKV, (head + 1) * DKV)
        by_offset = jnp.zeros(ids.shape, F32)
        for bucket in range(cfg.buckets):
            by_offset = jnp.where(ids == bucket, position_bias[head, bucket], by_offset)
        bias = pltpu.roll(
            jnp.broadcast_to(by_offset, (seq, 2 * seq)),
            seq + 1,
            1,
            stride=1,
            stride_axis=0,
        )[:, :seq]
        scores = dot_tn(qkv[1, part, :], qkv[0, part, :]) + jnp.transpose(bias)
        scores = jnp.where(key_valid, scores, -1e30)
        exps = jnp.exp(scores - jnp.max(scores, axis=0, keepdims=True))
        prob = exps / jnp.sum(exps, axis=0, keepdims=True)
        probs[head] = prob
        attended[core, part, :] = dot(qkv[2, part, :], prob.astype(BF)).astype(BF)
    pair_att.start()

    build_left(trans, 2)
    left_copy(2).start()
    loads[1].wait()
    pair_cot.wait()
    row_valid = lax.broadcasted_iota(jnp.int32, (step_rows, seq), 1) < group_len

    def mask_rows(step, carry):
        block = rows_at(step)
        trans[block, :] = jnp.where(row_valid, whole(cot_raw, block).astype(F32), 0.0)
        return carry

    lax.fori_loop(0, steps, mask_rows, 0)
    build_left(trans, 0)
    left_copy(0).start()
    for block in blocks_of(width, 128):
        cot[:, block] = jnp.transpose(trans[block, :]).astype(BF)

    loads[5].wait()
    pair_wo.wait()
    for block in blocks_of(width, 128):
        wo_t[block, :] = jnp.transpose(
            jnp.concatenate([wo[0, :, block], wo[1, :, block]], axis=0).astype(F32)
        ).astype(BF)
    pair_att.wait()
    both = attended[...].reshape(2 * hw, seq)
    for block in blocks_of(width, MROWS):
        middle[block, :] = x_at(block) + dot(wo_t[block, :], both)

    inv_two = inverse_rms(lambda block: middle[block, :], seq)

    def norm_two_rows(step, carry):
        block = rows_at(step)
        trans[block, :] = middle[block, :] * inv_two * gain_at(1, block, seq)
        out_acc[block, :] = jnp.zeros((step_rows, seq), F32)
        grad_acc[block, :] = jnp.zeros((step_rows, seq), F32)
        return carry

    lax.fori_loop(0, steps, norm_two_rows, 0)
    build_left(trans, 1)
    left_copy(1).start()
    for block in blocks_of(width, 128):
        normed_two[:, block] = jnp.transpose(trans[block, :]).astype(BF)
    small[...] = jnp.zeros_like(small)

    def feed_forward(chunk):
        slot = lax.rem(chunk, 2)
        for load in weight_loads(chunk, slot):
            load.wait()
        normed = normed_two[...]
        gate = dot(normed, wg[slot])
        up = dot(normed, wu[slot])
        grad_hidden = dot(cot[...], wd[slot])
        square = gate * gate
        tanh = jnp.tanh(GELU_C * (gate + 0.044715 * (square * gate)))
        half = 0.5 * (1.0 + tanh)
        gelu = gate * half
        slope = half + (0.5 * GELU_C) * gate * (1.0 - tanh * tanh) * (
            1.0 + (3 * 0.044715) * square
        )
        hidden = (gelu * up).astype(BF)
        grad_gate = (grad_hidden * up * slope).astype(BF)
        grad_up = (grad_hidden * gelu).astype(BF)
        base = 3 * chunk
        right_own[base] = hidden
        right_own[base + 1] = grad_gate
        right_own[base + 2] = grad_up
        for block in blocks_of(width, MROWS):
            out_acc[block, :] += dot_nt(wd[slot, block, :], hidden)
            grad_acc[block, :] += dot_nt(wg[slot, block, :], grad_gate) + dot_nt(
                wu[slot, block, :], grad_up
            )

        @pl.when(chunk < cfg.ff_chunks - 2)
        def _():
            for load in weight_loads(chunk + 2, slot):
                load.start()

    def exchange_sums():
        grad_send[...] = grad_acc[:width, :].astype(BF)
        pair_grad.start()
        part_send[...] = out_acc[:, other_lanes].astype(BF)
        pair_part.start()

    def lane_mask(shape, dimension):
        lane = lax.broadcasted_iota(jnp.int32, shape, dimension)
        return (lax.div(lane, rows) == core).astype(F32)

    def lane_sums(weights, source):
        return lax.dot_general(
            weights,
            source,
            (((1,), (1,)), ((), ())),
            precision=lax.Precision.HIGHEST,
            preferred_element_type=F32,
        )[0:1, :]

    def put_small(row, line):
        small[row : row + 1, :] = line[:, : cfg.half]
        small[row + 1 : row + 2, : width - cfg.half] = line[:, cfg.half :]

    def norm_two_back():
        pair_grad.wait()

        def grad_at(block):
            return grad_acc[block, :] + grad_in[block, :].astype(F32)

        inv = inverse_rms(lambda block: middle[block, :], seq)
        inner = (
            column_sum(
                lambda block: grad_at(block) * gain_at(1, block, seq) * middle[block, :], seq
            )
            * inv
            * (1.0 / width)
        )

        def back_rows(step, carry):
            block = rows_at(step)
            grad = grad_at(block)
            unit = middle[block, :] * inv
            masked = jnp.where(row_valid, whole(cot_raw, block).astype(F32), 0.0)
            total = masked + inv * (grad * gain_at(1, block, seq) - unit * inner)
            trans[block, :] = grad * unit
            grad_acc[block, :] = total
            grad_branch[block, :] = total.astype(BF)
            return carry

        lax.fori_loop(0, steps, back_rows, 0)
        build_left(grad_acc, 3)
        left_copy(3).start()
        mask = lane_mask((8, seq), 1)
        put_small(2, lane_sums(mask, trans[:width, :]))

    def attention_back():
        grad_att = dot(wo[core], grad_branch[...]).astype(BF)
        flip = (
            lax.broadcasted_iota(jnp.int32, (seq, seq), 0)
            + lax.broadcasted_iota(jnp.int32, (seq, seq), 1)
            == seq - 1
        ).astype(BF)
        for head in range(heads):
            part = slice(head * DKV, (head + 1) * DKV)
            grad_mixed = grad_att[part, :]
            prob = probs[head]
            grad_probs = dot_tn(qkv[2, part, :], grad_mixed)
            inner = jnp.sum(prob * grad_probs, axis=0, keepdims=True)
            grad_scores = (prob * (grad_probs - inner)).astype(BF)
            grad_qkv[0, part, :] = dot(qkv[1, part, :], grad_scores).astype(BF)
            grad_qkv[1, part, :] = dot_nt(qkv[0, part, :], grad_scores).astype(BF)
            grad_qkv[2, part, :] = dot_nt(grad_mixed, prob.astype(BF)).astype(BF)
            flipped = jnp.concatenate(
                [dot(grad_scores, flip), jnp.zeros((seq, seq), F32)], axis=1
            )
            skewed = pltpu.roll(flipped, 0, 1, stride=1, stride_axis=0)
            small[4 + head : 5 + head, : 2 * seq] = jnp.sum(skewed, axis=0, keepdims=True)
        joined = jnp.concatenate(
            [grad_qkv[...].reshape(3 * hw, seq), attended[core]], axis=0
        ).astype(F32)
        for index in range(cfg.chunks - cfg.ff_total):
            chunk = cfg.ff_total + index
            right_own[chunk] = jnp.transpose(joined[index * CW : (index + 1) * CW, :]).astype(BF)

    def norm_one_sums():
        for block in blocks_of(width, 128):
            back_send[block, :] = sum(
                dot_tn(wqkv[part, :, block], grad_qkv[part, :, other_lanes]) for part in range(3)
            ).astype(BF)
        pair_back.start()
        for block in blocks_of(width, 128):
            input_grad[block, :] = sum(
                dot_tn(wqkv[part, :, block], grad_qkv[part, :, own_lanes]) for part in range(3)
            )

    def small_copy(k):
        target = sibling if k == cfg.bits else (peer[k], core)
        return send(
            small, small_in.at[k], small_send_sem.at[k], small_recv_sem.at[k], target
        )

    def finish_rows():
        pair_part.wait()
        pair_back.wait()

        def x_own(block):
            return hid[core, block, :].astype(F32)

        def grad_at(block):
            return input_grad[block, :] + back_in[block, :].astype(F32)

        inv = inverse_rms(x_own, rows)
        inner = (
            column_sum(lambda block: grad_at(block) * gain_at(0, block, rows) * x_own(block), rows)
            * inv
            * (1.0 / width)
        )

        def last_rows(step, carry):
            block = rows_at(step)
            grad = grad_at(block)
            unit = x_own(block) * inv
            input_grad[block, :] = grad_acc[block, own_lanes] + inv * (
                grad * gain_at(0, block, rows) - unit * inner
            )
            layer_out[block, :] = (
                middle[block, own_lanes]
                + out_acc[block, own_lanes]
                + part_in[block, :].astype(F32)
            )
            trans[block, :rows] = grad * unit
            return carry

        lax.fori_loop(0, steps, last_rows, 0)
        put_small(0, lane_sums(jnp.ones((8, rows), F32), trans[:width, :rows]))
        small_copy(0).start()

    def small_stage(k):
        small_copy(k).wait()
        if k == cfg.bits:
            row = lax.broadcasted_iota(jnp.int32, small.shape, 0)
            small_out[...] = small[...] + jnp.where(row < 4, small_in[k], 0.0)
        else:
            small[...] = small[...] + small_in[k]
            small_copy(k + 1).start()

    def stage_copy(k, chunk, target):
        slot = lax.rem(chunk, SLOTS)
        return send(
            stage_send[k].at[slot],
            stage_in[k].at[chunk],
            stage_send_sem.at[k, slot],
            stage_recv_sem.at[k, chunk],
            (target, core),
        )

    def stage_target(k, chunk):
        return pick(chunk, k + 1, peer)

    def form(chunk):
        tail_part = lax.div(chunk, cfg.ff_total)
        which = (1 - tail_part) * lax.div(lax.rem(chunk, 3) + 1, 2) + 2 * tail_part
        slot = lax.rem(chunk, SLOTS)
        first_bit = pick(chunk, 0, bit)
        second_bit = pick(chunk, 1, bit)

        @pl.when(chunk == 0)
        def _():
            left_pass(0)
            left_pass(2)
            left_share(0).wait()

        @pl.when(chunk == 1)
        def _():
            left_pass(1)
            left_share(1).wait()

        @pl.when(chunk == cfg.ff_total)
        def _():
            left_share(2).wait()

        @pl.when(chunk == cfg.chunks - 2)
        def _():
            left_pass(3)

        right_copy(chunk).wait()

        def product(left, quarter):
            return dot(left_own[left, first_bit, quarter], right_own[chunk]) + dot(
                left_in[left, quarter], right_in[chunk]
            )

        @pl.when(chunk < cfg.chunks - 1)
        def _():
            stage_send[0][slot] = product(which, 1 - second_bit).astype(BF)
            stage_copy(0, chunk, stage_target(0, chunk)).start()
            stage_own[0][slot] = product(which, second_bit)

        @pl.when(chunk == cfg.chunks - 1)
        def _():
            left_share(3).wait()
            split = lax.broadcasted_iota(jnp.int32, (cfg.quarter, CW), 1) < CW - hw

            def mixed(quarter):
                return jnp.where(split, product(2, quarter), product(3, quarter))

            stage_send[0][slot] = mixed(1 - second_bit).astype(BF)
            stage_copy(0, chunk, stage_target(0, chunk)).start()
            stage_own[0][slot] = mixed(second_bit)

    def halve(k, chunk):
        slot = lax.rem(chunk, SLOTS)
        stage_copy(k - 1, chunk, stage_target(k - 1, chunk)).wait()
        if k == stages:
            result = stage_own[k - 1][slot] + stage_in[k - 1][chunk].astype(F32)

            @pl.when(chunk < cfg.ff_total)
            def _():
                columns = pl.ds(pl.multiple_of(lax.div(chunk, 3) * CW, CW), CW)
                ff_out[lax.rem(chunk, 3), :, columns] = result[: cfg.shard, :]

            @pl.when(chunk >= cfg.ff_total)
            def _():
                att_final[lax.rem(chunk, cfg.ff_total)] = result

            return
        half = cfg.stage_rows[k]
        mine = pick(chunk, k + 1, bit)

        def total(which):
            part = pl.ds(pl.multiple_of(which * half, 16), half)
            return stage_own[k - 1][slot, part, :] + stage_in[k - 1][chunk, part, :].astype(F32)

        stage_send[k][slot] = total(1 - mine).astype(BF)
        stage_copy(k, chunk, stage_target(k, chunk)).start()
        stage_own[k][slot] = total(mine)

    last_ff = FF_TICKS * (cfg.ff_chunks - 1)
    pieces = [exchange_sums, norm_two_back, attention_back, norm_one_sums, finish_rows]
    pieces = [(last_ff + index, piece) for index, piece in enumerate(pieces)]
    for k in range(cfg.bits + 1):
        pieces.append((pieces[-1][0] + SMALL_GAP, functools.partial(small_stage, k)))
    ticks = max(LAG + cfg.chunks + GAP * stages, pieces[-1][0] + 1)

    def tick(t, carry):
        for k in range(stages, 0, -1):
            chunk = t - LAG - GAP * k

            @pl.when(jnp.logical_and(chunk >= 0, chunk < cfg.chunks))
            def _(k=k, chunk=chunk):
                halve(k, chunk)

        new = t - LAG

        @pl.when(jnp.logical_and(new >= 0, new < cfg.chunks))
        def _():
            form(new)

        @pl.when(jnp.logical_and(lax.rem(t, FF_TICKS) == 0, t <= last_ff))
        def _():
            feed_forward(lax.div(t, FF_TICKS))

        for when, piece in pieces:

            @pl.when(t == when)
            def _(piece=piece):
                piece()

        @pl.when(t < cfg.chunks)
        def _():
            right_copy(t).start()

        return carry

    lax.fori_loop(0, ticks, tick, 0)

    flat = jnp.concatenate([att_final[index] for index in range(cfg.chunks - cfg.ff_total)], axis=1)
    for part, ref in enumerate((query_out, key_out, value_out)):
        ref[...] = flat[: cfg.shard, part * hw : (part + 1) * hw]
    output_out[...] = jnp.transpose(flat[:, 3 * hw :])[:, : cfg.shard]


def finish_kernel(
    cfg,
    layer_in,
    grad_in,
    query_in,
    key_in,
    value_in,
    output_in,
    ff_in,
    small,
    bucket_ids,
    layer_out,
    grad_out,
    gain_one,
    query_out,
    key_out,
    value_out,
    output_out,
    bias_out,
    gain_two,
    gate_out,
    up_out,
    down_out,
    *rest,
):
    pairs = [
        (ff_in.at[0], down_out),
        (ff_in.at[1], gate_out),
        (ff_in.at[2], up_out),
        (layer_in, layer_out),
        (grad_in, grad_out),
        (query_in, query_out),
        (key_in, key_out),
        (value_in, value_out),
        (output_in, output_out),
    ]
    buffers, (load_sem, store_sem) = rest[:-2], rest[-2:]
    loads, stores = [], []
    for index, ((src, dst), buffer) in enumerate(zip(pairs, buffers)):
        loads.append(pltpu.make_async_copy(src, buffer, load_sem.at[index]))
        stores.append(pltpu.make_async_copy(buffer, dst, store_sem.at[index]))
    for load in loads:
        load.start()
    for load, store in zip(loads, stores):
        load.wait()
        store.start()
    for row, gain in ((0, gain_one), (2, gain_two)):
        line = jnp.concatenate([small[row : row + 1, :], small[row + 1 : row + 2, :]], axis=1)
        gain[...] = line[:, : cfg.width].reshape(cfg.width)
    offsets = bucket_ids.shape[0]
    bucket = lax.broadcasted_iota(jnp.int32, (cfg.buckets, offsets), 0)
    onehot = (bucket_ids[...].reshape(1, offsets) == bucket).astype(F32)
    sums = lax.dot_general(
        small[:, :offsets],
        onehot,
        (((1,), (1,)), ((), ())),
        precision=lax.Precision.HIGHEST,
        preferred_element_type=F32,
    )
    bias_out[...] = sums[4 : 4 + cfg.heads, :]
    for store in stores:
        store.wait()


def shards(
    mesh,
    hidden_in,
    attention_gain,
    query_weight,
    key_weight,
    value_weight,
    output_weight,
    position_bias,
    feedforward_gain,
    gate_weight,
    up_weight,
    down_weight,
    cotangent,
    item_lengths,
    item_group,
    bucket_ids,
):
    rows, width = hidden_in.shape
    hw = query_weight.shape[1]
    hidden = gate_weight.shape[1]
    buckets = position_bias.shape[0]
    cfg = Sizes(mesh.shape["dp"], rows, width, hw, hidden, buckets)
    seq, stages, shard = cfg.seq, cfg.stages, cfg.shard
    any_spec = pl.BlockSpec(memory_space=pl.ANY)
    vmem = pl.BlockSpec(memory_space=pltpu.VMEM)
    smem = pl.BlockSpec(memory_space=pltpu.SMEM)
    small_shape = (8, cfg.half)
    scratch = [
        pltpu.VMEM((2, width, rows), BF),
        pltpu.VMEM((2, width, rows), BF),
        pltpu.VMEM((seq, width), BF),
        pltpu.VMEM((2, width, 128), F32),
        pltpu.VMEM((3, hw, width), BF),
        pltpu.VMEM((2, hw, width), BF),
        pltpu.VMEM((width, 2 * hw), BF),
        pltpu.VMEM((2, width, CW), BF),
        pltpu.VMEM((2, width, CW), BF),
        pltpu.VMEM((2, width, CW), BF),
        pltpu.VMEM((width, seq), BF),
        pltpu.VMEM((seq, width), BF),
        pltpu.VMEM((width, seq), F32),
        pltpu.VMEM((3, hw, seq), BF),
        pltpu.VMEM((cfg.heads, seq, seq), F32),
        pltpu.VMEM((2, hw, seq), BF),
        pltpu.VMEM((cfg.tall, seq), F32),
        pltpu.VMEM((4, 2, 2, cfg.quarter, seq), BF),
        pltpu.VMEM((4, 2, cfg.quarter, seq), BF),
        pltpu.VMEM((cfg.chunks, seq, CW), BF),
        pltpu.VMEM((cfg.chunks, seq, CW), BF),
        pltpu.VMEM((width, seq), F32),
        pltpu.VMEM((cfg.tall, seq), F32),
        pltpu.VMEM((width, seq), BF),
        pltpu.VMEM((width, seq), BF),
        pltpu.VMEM((width, rows), BF),
        pltpu.VMEM((width, rows), BF),
        pltpu.VMEM((width, rows), BF),
        pltpu.VMEM((width, rows), BF),
        pltpu.VMEM((width, seq), BF),
        pltpu.VMEM((3, hw, seq), BF),
        pltpu.VMEM(small_shape, F32),
        pltpu.VMEM((cfg.bits + 1,) + small_shape, F32),
        pltpu.VMEM((cfg.chunks - cfg.ff_total, cfg.shard_pad, CW), F32),
        pltpu.VMEM((1, 2 * seq), jnp.int32),
    ]
    scratch += [pltpu.VMEM((SLOTS, size, CW), F32) for size in cfg.stage_rows]
    scratch += [pltpu.VMEM((SLOTS, size, CW), BF) for size in cfg.stage_rows]
    scratch += [pltpu.VMEM((cfg.chunks, size, CW), BF) for size in cfg.stage_rows]
    dma = pltpu.SemaphoreType.DMA
    scratch += [
        dma((6,)),
        dma((2, 3)),
        dma((7,)),
        dma((7,)),
        dma((4,)),
        dma((4,)),
        dma((4,)),
        dma((4,)),
        dma((cfg.chunks,)),
        dma((cfg.chunks,)),
        dma((stages, SLOTS)),
        dma((stages, cfg.chunks)),
        dma((cfg.bits + 1,)),
        dma((cfg.bits + 1,)),
    ]
    (
        layer_out,
        input_grad,
        small_sum,
        ff_sum,
        query_sum,
        key_sum,
        value_sum,
        output_sum,
    ) = pl.pallas_call(
        functools.partial(layer_kernel, cfg),
        out_shape=[
            jax.ShapeDtypeStruct((width, rows), F32),
            jax.ShapeDtypeStruct((width, rows), F32),
            jax.ShapeDtypeStruct(small_shape, F32),
            jax.ShapeDtypeStruct((3, shard, hidden), F32),
            jax.ShapeDtypeStruct((shard, hw), F32),
            jax.ShapeDtypeStruct((shard, hw), F32),
            jax.ShapeDtypeStruct((shard, hw), F32),
            jax.ShapeDtypeStruct((hw, shard), F32),
        ],
        in_specs=[
            any_spec,
            vmem,
            any_spec,
            any_spec,
            any_spec,
            any_spec,
            smem,
            vmem,
            any_spec,
            any_spec,
            any_spec,
            any_spec,
            smem,
            smem,
            vmem,
        ],
        out_specs=[vmem] * 8,
        scratch_shapes=scratch,
        compiler_params=pltpu.CompilerParams(
            collective_id=0, has_side_effects=True, vmem_limit_bytes=60 * 1024 * 1024
        ),
        cost_estimate=pl.CostEstimate(
            flops=14 * 10**9, bytes_accessed=24 * 10**6, transcendentals=10**6
        ),
    )(
        hidden_in.T,
        attention_gain,
        query_weight.T,
        key_weight.T,
        value_weight.T,
        output_weight,
        position_bias.T,
        feedforward_gain,
        gate_weight,
        up_weight,
        down_weight.T,
        cotangent.T,
        item_lengths,
        item_group,
        bucket_ids,
    )
    def like(array):
        return jax.ShapeDtypeStruct(array.shape, array.dtype)

    one_ff = jax.ShapeDtypeStruct((shard, hidden), F32)
    outs = pl.pallas_call(
        functools.partial(finish_kernel, cfg),
        out_shape=[
            like(layer_out),
            like(input_grad),
            like(attention_gain),
            like(query_sum),
            like(key_sum),
            like(value_sum),
            like(output_sum),
            jax.ShapeDtypeStruct((cfg.heads, buckets), F32),
            like(feedforward_gain),
            one_ff,
            one_ff,
            one_ff,
        ],
        in_specs=[any_spec] * 7 + [vmem, vmem],
        out_specs=[any_spec] * 2 + [vmem] + [any_spec] * 4 + [vmem] * 2 + [any_spec] * 3,
        scratch_shapes=[
            pltpu.VMEM(array.shape, F32)
            for array in (one_ff,) * 3
            + (layer_out, input_grad, query_sum, key_sum, value_sum, output_sum)
        ]
        + [dma((9,)), dma((9,))],
        compiler_params=pltpu.CompilerParams(vmem_limit_bytes=16 * 1024 * 1024),
    )(
        layer_out,
        input_grad,
        query_sum,
        key_sum,
        value_sum,
        output_sum,
        ff_sum,
        small_sum,
        bucket_ids,
    )
    layer_out, input_grad, gain_one, query, key, value, output, bias, gain_two, gate, up, down = outs
    return (
        layer_out.T,
        input_grad.T,
        gain_one,
        query,
        key,
        value,
        output,
        bias.T,
        gain_two,
        gate,
        up,
        down.T,
    )


def solution(mesh):
    in_specs = (
        P(("dp", "mp"), None),
        P(),
        P(None, "mp"),
        P(None, "mp"),
        P(None, "mp"),
        P("mp", None),
        P(None, "mp"),
        P(),
        P(None, "mp"),
        P(None, "mp"),
        P("mp", None),
        P(("dp", "mp"), None),
        P(),
        P(),
        P(),
    )
    out_specs = (
        P(("dp", "mp"), None),
        P(("dp", "mp"), None),
        P(),
        P("dp", "mp"),
        P("dp", "mp"),
        P("dp", "mp"),
        P("mp", "dp"),
        P(None, "mp"),
        P(),
        P("dp", "mp"),
        P("dp", "mp"),
        P("mp", "dp"),
    )
    return jax.shard_map(
        functools.partial(shards, mesh),
        mesh=mesh,
        in_specs=in_specs,
        out_specs=out_specs,
        check_vma=False,
    )
```

```python
import functools
import math

import jax
import jax.numpy as jnp
from jax import lax
from jax.experimental import pallas as pl
from jax.experimental.pallas import tpu as pltpu
from jax.sharding import PartitionSpec as P

DKV = 64
CW = 256
EPS = 1e-06
LAG = 5
GAP = 4
SLOTS = GAP + 1
FF_TICKS = 2
LEAD = 1
SMALL_GAP = 3
AXES = ((0, 1, 2), (1, 0, 2), (2, 0, 1), (2, 1, 0), (2, 1, 0))
STEP = 64
MROWS = 368
BF = jnp.bfloat16
F32 = jnp.float32
MESH = pl.DeviceIdType.MESH
GELU_C = math.sqrt(2.0 / math.pi)


def dot(left, right):
    return lax.dot_general(left, right, (((1,), (0,)), ((), ())), preferred_element_type=F32)


def dot_nt(left, right):
    return lax.dot_general(left, right, (((1,), (1,)), ((), ())), preferred_element_type=F32)


def dot_tn(left, right):
    return lax.dot_general(left, right, (((0,), (0,)), ((), ())), preferred_element_type=F32)


def blocks_of(extent, step):
    return [slice(begin, min(begin + step, extent)) for begin in range(0, extent, step)]


def fold(block):
    return jnp.sum(block.reshape(block.shape[0] // 8, 8, block.shape[1]), axis=0)


class Sizes:
    def __init__(self, dp, local_rows, width, head_width, hidden, buckets):
        self.dp = dp
        self.bits = dp.bit_length() - 1
        self.local_rows = local_rows
        self.seq = 2 * local_rows
        self.width = width
        self.head_width = head_width
        self.heads = head_width // DKV
        self.hidden = hidden
        self.buckets = buckets
        self.shard = width // dp
        self.shard_pad = -(-self.shard // 16) * 16
        self.quarter = self.shard_pad * dp // 4
        self.ff_chunks = hidden // CW
        self.ff_total = 3 * self.ff_chunks
        self.chunks = self.ff_total + 4 * head_width // CW
        self.stage_rows = [self.quarter >> k for k in range(self.bits - 1)]
        self.stages = len(self.stage_rows)
        self.half = -(-width // 256) * 128
        self.tall = width + self.shard_pad
        self.orders = [axes + tuple(range(3, self.bits)) for axes in AXES]


def layer_kernel(
    cfg,
    hidden_hbm,
    gain_one,
    wq_hbm,
    wk_hbm,
    wv_hbm,
    wo_hbm,
    position_bias,
    gain_two,
    wg_hbm,
    wu_hbm,
    wd_hbm,
    cot_hbm,
    lengths,
    groups,
    bucket_ids,
    layer_out,
    input_grad,
    small_out,
    ff_out,
    query_out,
    key_out,
    value_out,
    output_out,
    hid,
    cot_raw,
    cot,
    gains,
    wqkv,
    wo,
    wo_t,
    wg,
    wu,
    wd,
    normed_one,
    normed_two,
    middle,
    qkv,
    probs,
    attended,
    trans,
    left_own,
    left_in,
    right_own,
    right_in,
    out_acc,
    grad_acc,
    grad_in,
    part_send,
    part_in,
    back_send,
    back_in,
    grad_branch,
    grad_qkv,
    small,
    small_in,
    att_final,
    ids_row,
    *rest,
):
    grad_send = normed_one
    stages = cfg.stages
    stage_own = rest[:stages]
    stage_send = rest[stages : 2 * stages]
    stage_in = rest[2 * stages : 3 * stages]
    (
        load_sem,
        weight_sem,
        pair_send_sem,
        pair_recv_sem,
        left_send_sem,
        left_recv_sem,
        share_send_sem,
        share_recv_sem,
        right_send_sem,
        right_recv_sem,
        stage_send_sem,
        stage_recv_sem,
        small_send_sem,
        small_recv_sem,
    ) = rest[3 * stages :]

    seq, rows, width, hw, heads = cfg.seq, cfg.local_rows, cfg.width, cfg.head_width, cfg.heads
    me = lax.axis_index("dp")
    core = lax.axis_index("mp")
    bit = [lax.rem(lax.div(me, 1 << k), 2) for k in range(cfg.bits)]
    peer = [me + (1 - 2 * bit[k]) * (1 << k) for k in range(cfg.bits)]
    sibling = (me, 1 - core)
    own_lanes = pl.ds(pl.multiple_of(core * rows, rows), rows)
    other_lanes = pl.ds(pl.multiple_of((1 - core) * rows, rows), rows)

    def send(src, dst, send_sem, recv_sem, target):
        return pltpu.make_async_remote_copy(
            src_ref=src,
            dst_ref=dst,
            send_sem=send_sem,
            recv_sem=recv_sem,
            device_id=target,
            device_id_type=MESH,
        )

    loads = [
        pltpu.make_async_copy(hidden_hbm, hid.at[core], load_sem.at[0]),
        pltpu.make_async_copy(cot_hbm, cot_raw.at[core], load_sem.at[1]),
        pltpu.make_async_copy(wq_hbm, wqkv.at[0], load_sem.at[2]),
        pltpu.make_async_copy(wk_hbm, wqkv.at[1], load_sem.at[3]),
        pltpu.make_async_copy(wv_hbm, wqkv.at[2], load_sem.at[4]),
        pltpu.make_async_copy(wo_hbm, wo.at[core], load_sem.at[5]),
    ]
    for load in loads:
        load.start()

    def weight_loads(chunk, slot):
        columns = pl.ds(pl.multiple_of(chunk * CW, CW), CW)
        return [
            pltpu.make_async_copy(src.at[:, columns], dst.at[slot], weight_sem.at[slot, index])
            for index, (src, dst) in enumerate(((wg_hbm, wg), (wu_hbm, wu), (wd_hbm, wd)))
        ]

    barrier = pltpu.get_barrier_semaphore()
    pl.semaphore_signal(barrier, inc=1, device_id=sibling, device_id_type=MESH)
    for k in range(cfg.bits):
        pl.semaphore_signal(barrier, inc=1, device_id=(peer[k], core), device_id_type=MESH)
    for index, gain in enumerate((gain_one, gain_two)):
        line = gain[...].reshape(1, width)
        for block in blocks_of(width, 128):
            size = block.stop - block.start
            gains[index, block, :] = jnp.transpose(
                jnp.broadcast_to(line[:, block], (128, size))
            )
    pl.semaphore_wait(barrier, cfg.bits + 1)

    pair_hid = send(
        hidden_hbm, hid.at[core], pair_send_sem.at[0], pair_recv_sem.at[0], sibling
    )
    pair_cot = send(
        cot_hbm, cot_raw.at[core], pair_send_sem.at[1], pair_recv_sem.at[1], sibling
    )
    pair_wo = send(wo_hbm, wo.at[core], pair_send_sem.at[2], pair_recv_sem.at[2], sibling)
    pair_hid.start()
    pair_cot.start()
    pair_wo.start()
    pair_att = send(
        attended.at[core], attended.at[core], pair_send_sem.at[3], pair_recv_sem.at[3], sibling
    )
    pair_grad = send(grad_send, grad_in, pair_send_sem.at[4], pair_recv_sem.at[4], sibling)
    pair_part = send(part_send, part_in, pair_send_sem.at[5], pair_recv_sem.at[5], sibling)
    pair_back = send(back_send, back_in, pair_send_sem.at[6], pair_recv_sem.at[6], sibling)

    for slot in range(2):
        for load in weight_loads(slot, slot):
            load.start()

    group_len = jnp.int32(0)
    for item in range(lengths.shape[0]):
        group_len = group_len + jnp.where(groups[item] == me, lengths[item], 0)

    def build_left(source, which):
        order = cfg.orders[which]
        for index in range(cfg.dp):
            bits = [(index >> k) & 1 for k in order]
            place = 0
            for value in bits[2:]:
                place = 2 * place + value
            block = source[index * cfg.shard : index * cfg.shard + cfg.shard_pad, :]
            left_own[
                which,
                bits[0],
                bits[1],
                place * cfg.shard_pad : (place + 1) * cfg.shard_pad,
                :,
            ] = block.astype(BF)

    def left_copy(which):
        first = cfg.orders[which][0]
        return send(
            left_own.at[which, 1 - bit[first], core],
            left_in.at[which, core],
            left_send_sem.at[which],
            left_recv_sem.at[which],
            (peer[first], core),
        )

    def left_share(which):
        return send(
            left_in.at[which, core],
            left_in.at[which, core],
            share_send_sem.at[which],
            share_recv_sem.at[which],
            sibling,
        )

    def left_pass(which):
        left_copy(which).wait()
        left_share(which).start()

    def pick(chunk, level, values):
        ks = [cfg.orders[which][level] for which in range(4)]
        if len(set(ks)) == 1:
            return values[ks[0]]
        tail_part = lax.div(chunk, cfg.ff_total)
        kind = lax.rem(chunk, 3)
        parts = (
            (1 - tail_part) * lax.div((1 - kind) * (2 - kind), 2),
            (1 - tail_part) * kind * (2 - kind),
            (1 - tail_part) * lax.div(kind * (kind - 1), 2),
            tail_part,
        )
        return sum(part * values[k] for part, k in zip(parts, ks))

    def right_copy(chunk):
        return send(
            right_own.at[chunk],
            right_in.at[chunk],
            right_send_sem.at[chunk],
            right_recv_sem.at[chunk],
            (pick(chunk, 0, peer), core),
        )

    for scratch in (trans, grad_acc):
        scratch[width:, :] = jnp.zeros((cfg.tall - width, seq), F32)

    step_rows = STEP
    steps = width // step_rows

    def rows_at(step):
        return pl.ds(pl.multiple_of(step * step_rows, step_rows), step_rows)

    def whole(ref, block):
        return jnp.concatenate([ref[0, block, :], ref[1, block, :]], axis=1)

    def gain_at(index, block, lanes):
        part = gains[index, block, :]
        return jnp.concatenate([part] * (lanes // 128), axis=1)

    def column_sum(term, lanes):
        zero = jnp.zeros((8, lanes), F32)
        total = lax.fori_loop(0, steps, lambda i, acc: acc + fold(term(rows_at(i))), zero)
        return jnp.sum(total, axis=0, keepdims=True)

    def inverse_rms(term, lanes):
        def square(block):
            x = term(block)
            return x * x

        return lax.rsqrt(column_sum(square, lanes) * (1.0 / width) + EPS)

    loads[0].wait()
    pair_hid.wait()

    def x_at(block):
        return whole(hid, block).astype(F32)

    inv_one = inverse_rms(x_at, seq)

    def norm_one_rows(step, carry):
        block = rows_at(step)
        normed = x_at(block) * inv_one * gain_at(0, block, seq)
        trans[block, :] = normed
        normed_one[block, :] = normed.astype(BF)
        return carry

    lax.fori_loop(0, steps, norm_one_rows, 0)

    for part in range(3):
        loads[2 + part].wait()
        qkv[part] = dot(wqkv[part], normed_one[...]).astype(BF)

    key_valid = lax.broadcasted_iota(jnp.int32, (seq, seq), 0) < group_len
    ids_row[...] = jnp.full(ids_row.shape, -1, jnp.int32)
    ids_row[:, : bucket_ids.shape[0]] = bucket_ids[...].reshape(1, -1)
    ids = ids_row[...]
    for head in range(heads):
        part = slice(head * DKV, (head + 1) * DKV)
        by_offset = jnp.zeros(ids.shape, F32)
        for bucket in range(cfg.buckets):
            by_offset = jnp.where(ids == bucket, position_bias[head, bucket], by_offset)
        bias = pltpu.roll(
            jnp.broadcast_to(by_offset, (seq, 2 * seq)),
            seq + 1,
            1,
            stride=1,
            stride_axis=0,
        )[:, :seq]
        scores = dot_tn(qkv[1, part, :], qkv[0, part, :]) + jnp.transpose(bias)
        scores = jnp.where(key_valid, scores, -1e30)
        exps = jnp.exp(scores - jnp.max(scores, axis=0, keepdims=True))
        prob = exps / jnp.sum(exps, axis=0, keepdims=True)
        probs[head] = prob
        attended[core, part, :] = dot(qkv[2, part, :], prob.astype(BF)).astype(BF)
    pair_att.start()

    build_left(trans, 3)
    left_copy(3).start()
    loads[1].wait()
    pair_cot.wait()
    row_valid = lax.broadcasted_iota(jnp.int32, (step_rows, seq), 1) < group_len

    def mask_rows(step, carry):
        block = rows_at(step)
        trans[block, :] = jnp.where(row_valid, whole(cot_raw, block).astype(F32), 0.0)
        return carry

    lax.fori_loop(0, steps, mask_rows, 0)
    build_left(trans, 0)
    left_copy(0).start()
    for block in blocks_of(width, 128):
        cot[:, block] = jnp.transpose(trans[block, :]).astype(BF)

    loads[5].wait()
    pair_wo.wait()
    for block in blocks_of(width, 128):
        wo_t[block, :] = jnp.transpose(
            jnp.concatenate([wo[0, :, block], wo[1, :, block]], axis=0).astype(F32)
        ).astype(BF)
    pair_att.wait()
    both = attended[...].reshape(2 * hw, seq)
    for block in blocks_of(width, MROWS):
        middle[block, :] = x_at(block) + dot(wo_t[block, :], both)

    inv_two = inverse_rms(lambda block: middle[block, :], seq)

    def norm_two_rows(step, carry):
        block = rows_at(step)
        trans[block, :] = middle[block, :] * inv_two * gain_at(1, block, seq)
        out_acc[block, :] = jnp.zeros((step_rows, seq), F32)
        grad_acc[block, :] = jnp.zeros((step_rows, seq), F32)
        return carry

    lax.fori_loop(0, steps, norm_two_rows, 0)
    build_left(trans, 1)
    left_copy(1).start()
    build_left(trans, 2)
    left_copy(2).start()
    for block in blocks_of(width, 128):
        normed_two[:, block] = jnp.transpose(trans[block, :]).astype(BF)
    small[...] = jnp.zeros_like(small)

    def feed_forward(chunk):
        slot = lax.rem(chunk, 2)
        for load in weight_loads(chunk, slot):
            load.wait()
        normed = normed_two[...]
        gate = dot(normed, wg[slot])
        up = dot(normed, wu[slot])
        grad_hidden = dot(cot[...], wd[slot])
        square = gate * gate
        tanh = jnp.tanh(GELU_C * (gate + 0.044715 * (square * gate)))
        half = 0.5 * (1.0 + tanh)
        gelu = gate * half
        slope = half + (0.5 * GELU_C) * gate * (1.0 - tanh * tanh) * (
            1.0 + (3 * 0.044715) * square
        )
        hidden = (gelu * up).astype(BF)
        grad_gate = (grad_hidden * up * slope).astype(BF)
        grad_up = (grad_hidden * gelu).astype(BF)
        base = 3 * chunk
        right_own[base] = hidden
        right_own[base + 1] = grad_gate
        right_own[base + 2] = grad_up
        for block in blocks_of(width, MROWS):
            out_acc[block, :] += dot_nt(wd[slot, block, :], hidden)
            grad_acc[block, :] += dot_nt(wg[slot, block, :], grad_gate) + dot_nt(
                wu[slot, block, :], grad_up
            )

        @pl.when(chunk < cfg.ff_chunks - 2)
        def _():
            for load in weight_loads(chunk + 2, slot):
                load.start()

    def exchange_sums():
        grad_send[...] = grad_acc[:width, :].astype(BF)
        pair_grad.start()
        part_send[...] = out_acc[:, other_lanes].astype(BF)
        pair_part.start()

    def lane_mask(shape, dimension):
        lane = lax.broadcasted_iota(jnp.int32, shape, dimension)
        return (lax.div(lane, rows) == core).astype(F32)

    def lane_sums(weights, source):
        return lax.dot_general(
            weights,
            source,
            (((1,), (1,)), ((), ())),
            precision=lax.Precision.HIGHEST,
            preferred_element_type=F32,
        )[0:1, :]

    def put_small(row, line):
        small[row : row + 1, :] = line[:, : cfg.half]
        small[row + 1 : row + 2, : width - cfg.half] = line[:, cfg.half :]

    def norm_two_back():
        pair_grad.wait()

        def grad_at(block):
            return grad_acc[block, :] + grad_in[block, :].astype(F32)

        inv = inverse_rms(lambda block: middle[block, :], seq)
        inner = (
            column_sum(
                lambda block: grad_at(block) * gain_at(1, block, seq) * middle[block, :], seq
            )
            * inv
            * (1.0 / width)
        )

        def back_rows(step, carry):
            block = rows_at(step)
            grad = grad_at(block)
            unit = middle[block, :] * inv
            masked = jnp.where(row_valid, whole(cot_raw, block).astype(F32), 0.0)
            total = masked + inv * (grad * gain_at(1, block, seq) - unit * inner)
            trans[block, :] = grad * unit
            grad_acc[block, :] = total
            grad_branch[block, :] = total.astype(BF)
            return carry

        lax.fori_loop(0, steps, back_rows, 0)
        build_left(grad_acc, 4)
        left_copy(4).start()
        mask = lane_mask((8, seq), 1)
        put_small(2, lane_sums(mask, trans[:width, :]))

    def attention_back():
        grad_att = dot(wo[core], grad_branch[...]).astype(BF)
        flip = (
            lax.broadcasted_iota(jnp.int32, (seq, seq), 0)
            + lax.broadcasted_iota(jnp.int32, (seq, seq), 1)
            == seq - 1
        ).astype(BF)
        for head in range(heads):
            part = slice(head * DKV, (head + 1) * DKV)
            grad_mixed = grad_att[part, :]
            prob = probs[head]
            grad_probs = dot_tn(qkv[2, part, :], grad_mixed)
            inner = jnp.sum(prob * grad_probs, axis=0, keepdims=True)
            grad_scores = (prob * (grad_probs - inner)).astype(BF)
            grad_qkv[0, part, :] = dot(qkv[1, part, :], grad_scores).astype(BF)
            grad_qkv[1, part, :] = dot_nt(qkv[0, part, :], grad_scores).astype(BF)
            grad_qkv[2, part, :] = dot_nt(grad_mixed, prob.astype(BF)).astype(BF)
            flipped = jnp.concatenate(
                [dot(grad_scores, flip), jnp.zeros((seq, seq), F32)], axis=1
            )
            skewed = pltpu.roll(flipped, 0, 1, stride=1, stride_axis=0)
            small[4 + head : 5 + head, : 2 * seq] = jnp.sum(skewed, axis=0, keepdims=True)
        joined = jnp.concatenate(
            [grad_qkv[...].reshape(3 * hw, seq), attended[core]], axis=0
        ).astype(F32)
        for index in range(cfg.chunks - cfg.ff_total):
            chunk = cfg.ff_total + index
            right_own[chunk] = jnp.transpose(joined[index * CW : (index + 1) * CW, :]).astype(BF)

    def norm_one_sums():
        for block in blocks_of(width, 128):
            back_send[block, :] = sum(
                dot_tn(wqkv[part, :, block], grad_qkv[part, :, other_lanes]) for part in range(3)
            ).astype(BF)
        pair_back.start()
        for block in blocks_of(width, 128):
            input_grad[block, :] = sum(
                dot_tn(wqkv[part, :, block], grad_qkv[part, :, own_lanes]) for part in range(3)
            )

    def small_copy(k):
        target = sibling if k == cfg.bits else (peer[k], core)
        return send(
            small, small_in.at[k], small_send_sem.at[k], small_recv_sem.at[k], target
        )

    def finish_rows():
        pair_part.wait()
        pair_back.wait()

        def x_own(block):
            return hid[core, block, :].astype(F32)

        def grad_at(block):
            return input_grad[block, :] + back_in[block, :].astype(F32)

        inv = inverse_rms(x_own, rows)
        inner = (
            column_sum(lambda block: grad_at(block) * gain_at(0, block, rows) * x_own(block), rows)
            * inv
            * (1.0 / width)
        )

        def last_rows(step, carry):
            block = rows_at(step)
            grad = grad_at(block)
            unit = x_own(block) * inv
            input_grad[block, :] = grad_acc[block, own_lanes] + inv * (
                grad * gain_at(0, block, rows) - unit * inner
            )
            layer_out[block, :] = (
                middle[block, own_lanes]
                + out_acc[block, own_lanes]
                + part_in[block, :].astype(F32)
            )
            trans[block, :rows] = grad * unit
            return carry

        lax.fori_loop(0, steps, last_rows, 0)
        put_small(0, lane_sums(jnp.ones((8, rows), F32), trans[:width, :rows]))
        small_copy(0).start()

    def small_stage(k):
        small_copy(k).wait()
        if k == cfg.bits:
            row = lax.broadcasted_iota(jnp.int32, small.shape, 0)
            small_out[...] = small[...] + jnp.where(row < 4, small_in[k], 0.0)
        else:
            small[...] = small[...] + small_in[k]
            small_copy(k + 1).start()

    def stage_copy(k, chunk, target):
        slot = lax.rem(chunk, SLOTS)
        return send(
            stage_send[k].at[slot],
            stage_in[k].at[chunk],
            stage_send_sem.at[k, slot],
            stage_recv_sem.at[k, chunk],
            (target, core),
        )

    def stage_target(k, chunk):
        return pick(chunk, k + 1, peer)

    def form(chunk):
        tail_part = lax.div(chunk, cfg.ff_total)
        which = (1 - tail_part) * lax.rem(chunk, 3) + 3 * tail_part
        slot = lax.rem(chunk, SLOTS)
        first_bit = pick(chunk, 0, bit)
        second_bit = pick(chunk, 1, bit)

        @pl.when(chunk == 0)
        def _():
            left_pass(0)
            left_pass(1)
            left_pass(2)
            left_share(0).wait()

        @pl.when(chunk == 1)
        def _():
            left_pass(3)
            left_share(1).wait()

        @pl.when(chunk == 2)
        def _():
            left_share(2).wait()

        @pl.when(chunk == cfg.ff_total)
        def _():
            left_share(3).wait()

        @pl.when(chunk == cfg.chunks - 2)
        def _():
            left_pass(4)

        right_copy(chunk).wait()

        def product(left, quarter):
            return dot(left_own[left, first_bit, quarter], right_own[chunk]) + dot(
                left_in[left, quarter], right_in[chunk]
            )

        @pl.when(chunk < cfg.chunks - 1)
        def _():
            stage_send[0][slot] = product(which, 1 - second_bit).astype(BF)
            stage_copy(0, chunk, stage_target(0, chunk)).start()
            stage_own[0][slot] = product(which, second_bit)

        @pl.when(chunk == cfg.chunks - 1)
        def _():
            left_share(4).wait()
            split = lax.broadcasted_iota(jnp.int32, (cfg.quarter, CW), 1) < CW - hw

            def mixed(quarter):
                return jnp.where(split, product(3, quarter), product(4, quarter))

            stage_send[0][slot] = mixed(1 - second_bit).astype(BF)
            stage_copy(0, chunk, stage_target(0, chunk)).start()
            stage_own[0][slot] = mixed(second_bit)

    def halve(k, chunk):
        slot = lax.rem(chunk, SLOTS)
        stage_copy(k - 1, chunk, stage_target(k - 1, chunk)).wait()
        if k == stages:
            result = stage_own[k - 1][slot] + stage_in[k - 1][chunk].astype(F32)

            @pl.when(chunk < cfg.ff_total)
            def _():
                columns = pl.ds(pl.multiple_of(lax.div(chunk, 3) * CW, CW), CW)
                ff_out[lax.rem(chunk, 3), :, columns] = result[: cfg.shard, :]

            @pl.when(chunk >= cfg.ff_total)
            def _():
                att_final[lax.rem(chunk, cfg.ff_total)] = result

            return
        half = cfg.stage_rows[k]
        mine = pick(chunk, k + 1, bit)

        def total(which):
            part = pl.ds(pl.multiple_of(which * half, 16), half)
            return stage_own[k - 1][slot, part, :] + stage_in[k - 1][chunk, part, :].astype(F32)

        stage_send[k][slot] = total(1 - mine).astype(BF)
        stage_copy(k, chunk, stage_target(k, chunk)).start()
        stage_own[k][slot] = total(mine)

    last_ff = FF_TICKS * (cfg.ff_chunks - 1)
    pieces = [exchange_sums, norm_two_back, attention_back, norm_one_sums, finish_rows]
    pieces = [(last_ff + index, piece) for index, piece in enumerate(pieces)]
    for k in range(cfg.bits + 1):
        pieces.append((pieces[-1][0] + SMALL_GAP, functools.partial(small_stage, k)))
    ticks = max(LAG + cfg.chunks + GAP * stages, pieces[-1][0] + 1)

    def tick(t, carry):
        for k in range(stages, 0, -1):
            chunk = t - LAG - GAP * k

            @pl.when(jnp.logical_and(chunk >= 0, chunk < cfg.chunks))
            def _(k=k, chunk=chunk):
                halve(k, chunk)

        new = t - LAG

        @pl.when(jnp.logical_and(new >= 0, new < cfg.chunks))
        def _():
            form(new)

        @pl.when(jnp.logical_and(lax.rem(t, FF_TICKS) == 0, t <= last_ff))
        def _():
            feed_forward(lax.div(t, FF_TICKS))

        for when, piece in pieces:

            @pl.when(t == when)
            def _(piece=piece):
                piece()

        for early in range(LEAD):

            @pl.when(t == 0)
            def _(early=early):
                right_copy(early).start()

        @pl.when(t + LEAD < cfg.chunks)
        def _():
            right_copy(t + LEAD).start()

        return carry

    lax.fori_loop(0, ticks, tick, 0)

    flat = jnp.concatenate([att_final[index] for index in range(cfg.chunks - cfg.ff_total)], axis=1)
    for part, ref in enumerate((query_out, key_out, value_out)):
        ref[...] = flat[: cfg.shard, part * hw : (part + 1) * hw]
    output_out[...] = jnp.transpose(flat[:, 3 * hw :])[:, : cfg.shard]


def finish_kernel(
    cfg,
    layer_in,
    grad_in,
    query_in,
    key_in,
    value_in,
    output_in,
    ff_in,
    small,
    bucket_ids,
    layer_out,
    grad_out,
    gain_one,
    query_out,
    key_out,
    value_out,
    output_out,
    bias_out,
    gain_two,
    gate_out,
    up_out,
    down_out,
    *rest,
):
    pairs = [
        (ff_in.at[0], down_out),
        (ff_in.at[1], gate_out),
        (ff_in.at[2], up_out),
        (layer_in, layer_out),
        (grad_in, grad_out),
        (query_in, query_out),
        (key_in, key_out),
        (value_in, value_out),
        (output_in, output_out),
    ]
    buffers, (load_sem, store_sem) = rest[:-2], rest[-2:]
    loads, stores = [], []
    for index, ((src, dst), buffer) in enumerate(zip(pairs, buffers)):
        loads.append(pltpu.make_async_copy(src, buffer, load_sem.at[index]))
        stores.append(pltpu.make_async_copy(buffer, dst, store_sem.at[index]))
    for load in loads:
        load.start()
    for load, store in zip(loads, stores):
        load.wait()
        store.start()
    for row, gain in ((0, gain_one), (2, gain_two)):
        line = jnp.concatenate([small[row : row + 1, :], small[row + 1 : row + 2, :]], axis=1)
        gain[...] = line[:, : cfg.width].reshape(cfg.width)
    offsets = bucket_ids.shape[0]
    bucket = lax.broadcasted_iota(jnp.int32, (cfg.buckets, offsets), 0)
    onehot = (bucket_ids[...].reshape(1, offsets) == bucket).astype(F32)
    sums = lax.dot_general(
        small[:, :offsets],
        onehot,
        (((1,), (1,)), ((), ())),
        precision=lax.Precision.HIGHEST,
        preferred_element_type=F32,
    )
    bias_out[...] = sums[4 : 4 + cfg.heads, :]
    for store in stores:
        store.wait()


def shards(
    mesh,
    hidden_in,
    attention_gain,
    query_weight,
    key_weight,
    value_weight,
    output_weight,
    position_bias,
    feedforward_gain,
    gate_weight,
    up_weight,
    down_weight,
    cotangent,
    item_lengths,
    item_group,
    bucket_ids,
):
    rows, width = hidden_in.shape
    hw = query_weight.shape[1]
    hidden = gate_weight.shape[1]
    buckets = position_bias.shape[0]
    cfg = Sizes(mesh.shape["dp"], rows, width, hw, hidden, buckets)
    seq, stages, shard = cfg.seq, cfg.stages, cfg.shard
    any_spec = pl.BlockSpec(memory_space=pl.ANY)
    vmem = pl.BlockSpec(memory_space=pltpu.VMEM)
    smem = pl.BlockSpec(memory_space=pltpu.SMEM)
    small_shape = (8, cfg.half)
    scratch = [
        pltpu.VMEM((2, width, rows), BF),
        pltpu.VMEM((2, width, rows), BF),
        pltpu.VMEM((seq, width), BF),
        pltpu.VMEM((2, width, 128), F32),
        pltpu.VMEM((3, hw, width), BF),
        pltpu.VMEM((2, hw, width), BF),
        pltpu.VMEM((width, 2 * hw), BF),
        pltpu.VMEM((2, width, CW), BF),
        pltpu.VMEM((2, width, CW), BF),
        pltpu.VMEM((2, width, CW), BF),
        pltpu.VMEM((width, seq), BF),
        pltpu.VMEM((seq, width), BF),
        pltpu.VMEM((width, seq), F32),
        pltpu.VMEM((3, hw, seq), BF),
        pltpu.VMEM((cfg.heads, seq, seq), F32),
        pltpu.VMEM((2, hw, seq), BF),
        pltpu.VMEM((cfg.tall, seq), F32),
        pltpu.VMEM((len(AXES), 2, 2, cfg.quarter, seq), BF),
        pltpu.VMEM((len(AXES), 2, cfg.quarter, seq), BF),
        pltpu.VMEM((cfg.chunks, seq, CW), BF),
        pltpu.VMEM((cfg.chunks, seq, CW), BF),
        pltpu.VMEM((width, seq), F32),
        pltpu.VMEM((cfg.tall, seq), F32),
        pltpu.VMEM((width, seq), BF),
        pltpu.VMEM((width, rows), BF),
        pltpu.VMEM((width, rows), BF),
        pltpu.VMEM((width, rows), BF),
        pltpu.VMEM((width, rows), BF),
        pltpu.VMEM((width, seq), BF),
        pltpu.VMEM((3, hw, seq), BF),
        pltpu.VMEM(small_shape, F32),
        pltpu.VMEM((cfg.bits + 1,) + small_shape, F32),
        pltpu.VMEM((cfg.chunks - cfg.ff_total, cfg.shard_pad, CW), F32),
        pltpu.VMEM((1, 2 * seq), jnp.int32),
    ]
    scratch += [pltpu.VMEM((SLOTS, size, CW), F32) for size in cfg.stage_rows]
    scratch += [pltpu.VMEM((SLOTS, size, CW), BF) for size in cfg.stage_rows]
    scratch += [pltpu.VMEM((cfg.chunks, size, CW), BF) for size in cfg.stage_rows]
    dma = pltpu.SemaphoreType.DMA
    scratch += [
        dma((6,)),
        dma((2, 3)),
        dma((7,)),
        dma((7,)),
        dma((len(AXES),)),
        dma((len(AXES),)),
        dma((len(AXES),)),
        dma((len(AXES),)),
        dma((cfg.chunks,)),
        dma((cfg.chunks,)),
        dma((stages, SLOTS)),
        dma((stages, cfg.chunks)),
        dma((cfg.bits + 1,)),
        dma((cfg.bits + 1,)),
    ]
    (
        layer_out,
        input_grad,
        small_sum,
        ff_sum,
        query_sum,
        key_sum,
        value_sum,
        output_sum,
    ) = pl.pallas_call(
        functools.partial(layer_kernel, cfg),
        out_shape=[
            jax.ShapeDtypeStruct((width, rows), F32),
            jax.ShapeDtypeStruct((width, rows), F32),
            jax.ShapeDtypeStruct(small_shape, F32),
            jax.ShapeDtypeStruct((3, shard, hidden), F32),
            jax.ShapeDtypeStruct((shard, hw), F32),
            jax.ShapeDtypeStruct((shard, hw), F32),
            jax.ShapeDtypeStruct((shard, hw), F32),
            jax.ShapeDtypeStruct((hw, shard), F32),
        ],
        in_specs=[
            any_spec,
            vmem,
            any_spec,
            any_spec,
            any_spec,
            any_spec,
            smem,
            vmem,
            any_spec,
            any_spec,
            any_spec,
            any_spec,
            smem,
            smem,
            vmem,
        ],
        out_specs=[vmem] * 8,
        scratch_shapes=scratch,
        compiler_params=pltpu.CompilerParams(
            collective_id=0, has_side_effects=True, vmem_limit_bytes=62 * 1024 * 1024
        ),
        cost_estimate=pl.CostEstimate(
            flops=14 * 10**9, bytes_accessed=24 * 10**6, transcendentals=10**6
        ),
    )(
        hidden_in.T,
        attention_gain,
        query_weight.T,
        key_weight.T,
        value_weight.T,
        output_weight,
        position_bias.T,
        feedforward_gain,
        gate_weight,
        up_weight,
        down_weight.T,
        cotangent.T,
        item_lengths,
        item_group,
        bucket_ids,
    )
    def like(array):
        return jax.ShapeDtypeStruct(array.shape, array.dtype)

    one_ff = jax.ShapeDtypeStruct((shard, hidden), F32)
    outs = pl.pallas_call(
        functools.partial(finish_kernel, cfg),
        out_shape=[
            like(layer_out),
            like(input_grad),
            like(attention_gain),
            like(query_sum),
            like(key_sum),
            like(value_sum),
            like(output_sum),
            jax.ShapeDtypeStruct((cfg.heads, buckets), F32),
            like(feedforward_gain),
            one_ff,
            one_ff,
            one_ff,
        ],
        in_specs=[any_spec] * 7 + [vmem, vmem],
        out_specs=[any_spec] * 2 + [vmem] + [any_spec] * 4 + [vmem] * 2 + [any_spec] * 3,
        scratch_shapes=[
            pltpu.VMEM(array.shape, F32)
            for array in (one_ff,) * 3
            + (layer_out, input_grad, query_sum, key_sum, value_sum, output_sum)
        ]
        + [dma((9,)), dma((9,))],
        compiler_params=pltpu.CompilerParams(vmem_limit_bytes=62 * 1024 * 1024),
    )(
        layer_out,
        input_grad,
        query_sum,
        key_sum,
        value_sum,
        output_sum,
        ff_sum,
        small_sum,
        bucket_ids,
    )
    layer_out, input_grad, gain_one, query, key, value, output, bias, gain_two, gate, up, down = outs
    return (
        layer_out.T,
        input_grad.T,
        gain_one,
        query,
        key,
        value,
        output,
        bias.T,
        gain_two,
        gate,
        up,
        down.T,
    )


def solution(mesh):
    in_specs = (
        P(("dp", "mp"), None),
        P(),
        P(None, "mp"),
        P(None, "mp"),
        P(None, "mp"),
        P("mp", None),
        P(None, "mp"),
        P(),
        P(None, "mp"),
        P(None, "mp"),
        P("mp", None),
        P(("dp", "mp"), None),
        P(),
        P(),
        P(),
    )
    out_specs = (
        P(("dp", "mp"), None),
        P(("dp", "mp"), None),
        P(),
        P("dp", "mp"),
        P("dp", "mp"),
        P("dp", "mp"),
        P("mp", "dp"),
        P(None, "mp"),
        P(),
        P("dp", "mp"),
        P("dp", "mp"),
        P("mp", "dp"),
    )
    return jax.shard_map(
        functools.partial(shards, mesh),
        mesh=mesh,
        in_specs=in_specs,
        out_specs=out_specs,
        check_vma=False,
    )
```

```python
import functools
import math

import jax
import jax.numpy as jnp
from jax import lax
from jax.experimental import pallas as pl
from jax.experimental.pallas import tpu as pltpu
from jax.sharding import PartitionSpec as P

DKV = 64
CW = 256
EPS = 1e-06
AXES = ((1, 0, 2), (1, 2, 0), (2, 1, 0), (2, 1, 0), (2, 0, 1), (2, 1, 0), (1, 0, 2), (2, 1, 0))
TOGETHER = (2, 3, 2)
FF_TICKS = (0, 1, 4, 7, 8, 10, 12)
RING_BLOCKS = 5
LAG = 0
GAP = 4
SLOTS = GAP + 1
RING = 3 * RING_BLOCKS
SMALL_GAP = 3
STEP = 64
MROWS = 368
BF = jnp.bfloat16
F32 = jnp.float32
MESH = pl.DeviceIdType.MESH
GELU_C = math.sqrt(2.0 / math.pi)


def dot(left, right):
    return lax.dot_general(left, right, (((1,), (0,)), ((), ())), preferred_element_type=F32)


def dot_nt(left, right):
    return lax.dot_general(left, right, (((1,), (1,)), ((), ())), preferred_element_type=F32)


def dot_tn(left, right):
    return lax.dot_general(left, right, (((0,), (0,)), ((), ())), preferred_element_type=F32)


def blocks_of(extent, step):
    return [slice(begin, min(begin + step, extent)) for begin in range(0, extent, step)]


def fold(block):
    return jnp.sum(block.reshape(block.shape[0] // 8, 8, block.shape[1]), axis=0)


def lookup(table, index):
    bits = max(table).bit_length()
    if bits == 0:
        return 0 * index
    per = 30 // bits
    words = [
        sum(value << (bits * place) for place, value in enumerate(table[begin : begin + per]))
        for begin in range(0, len(table), per)
    ]
    word = jnp.int32(words[0])
    for place in range(1, len(words)):
        word = jnp.where(index >= place * per, words[place], word)
    shifted = lax.shift_right_logical(word, bits * lax.rem(index, per))
    return lax.rem(shifted, 1 << bits)


class Sizes:
    def __init__(self, dp, local_rows, width, head_width, hidden, buckets):
        self.dp = dp
        self.bits = dp.bit_length() - 1
        self.local_rows = local_rows
        self.seq = 2 * local_rows
        self.width = width
        self.head_width = head_width
        self.heads = head_width // DKV
        self.hidden = hidden
        self.buckets = buckets
        self.shard = width // dp
        self.shard_pad = -(-self.shard // 16) * 16
        self.quarter = self.shard_pad * dp // 4
        self.ff_chunks = hidden // CW
        self.ff_total = 3 * self.ff_chunks
        self.chunks = self.ff_total + 4 * head_width // CW
        self.stage_rows = [self.quarter >> k for k in range(self.bits - 1)]
        self.stages = len(self.stage_rows)
        self.half = -(-width // 256) * 128
        self.tall = width + self.shard_pad
        self.eighth = self.quarter // 2
        self.order = []
        begin = 0
        for count in TOGETHER:
            self.order += [3 * (begin + f) + kind for kind in range(3) for f in range(count)]
            begin += count
        self.order += range(self.ff_total, self.chunks)
        self.near = sorted({axes[0] for axes in AXES[: self.ff_chunks]})
        self.first_use = [[axes[0] for axes in AXES].index(axis) for axis in self.near]


def layer_kernel(
    cfg,
    hidden_hbm,
    gain_one,
    wq_hbm,
    wk_hbm,
    wv_hbm,
    wo_hbm,
    position_bias,
    gain_two,
    wg_hbm,
    wu_hbm,
    wd_hbm,
    cot_hbm,
    lengths,
    groups,
    bucket_ids,
    layer_out,
    input_grad,
    small_out,
    ff_out,
    query_out,
    key_out,
    value_out,
    output_out,
    hid,
    cot_raw,
    cot,
    gains,
    wqkv,
    wo,
    wo_t,
    wg,
    wu,
    wd,
    normed_one,
    normed_two,
    middle,
    qkv,
    probs,
    attended,
    trans,
    left_own,
    left_in,
    near_rows,
    right_own,
    right_in,
    out_acc,
    grad_acc,
    grad_in,
    part_send,
    part_in,
    back_send,
    back_in,
    grad_branch,
    grad_qkv,
    small,
    small_in,
    att_final,
    ids_row,
    *rest,
):
    grad_send = normed_one
    stages = cfg.stages
    stage_own = rest[:stages]
    stage_send = rest[stages : 2 * stages]
    stage_in = rest[2 * stages : 3 * stages]
    (
        load_sem,
        weight_sem,
        pair_send_sem,
        pair_recv_sem,
        left_send_sem,
        left_recv_sem,
        share_send_sem,
        share_recv_sem,
        near_send_sem,
        near_recv_sem,
        pass_send_sem,
        pass_recv_sem,
        right_send_sem,
        right_recv_sem,
        stage_send_sem,
        stage_recv_sem,
        small_send_sem,
        small_recv_sem,
    ) = rest[3 * stages :]

    seq, rows, width, hw, heads = cfg.seq, cfg.local_rows, cfg.width, cfg.head_width, cfg.heads
    me = lax.axis_index("dp")
    core = lax.axis_index("mp")
    bit = [lax.rem(lax.div(me, 1 << k), 2) for k in range(cfg.bits)]
    peer = [me + (1 - 2 * bit[k]) * (1 << k) for k in range(cfg.bits)]
    sibling = (me, 1 - core)
    own_lanes = pl.ds(pl.multiple_of(core * rows, rows), rows)
    own_rows = own_lanes
    other_lanes = pl.ds(pl.multiple_of((1 - core) * rows, rows), rows)

    def send(src, dst, send_sem, recv_sem, target):
        return pltpu.make_async_remote_copy(
            src_ref=src,
            dst_ref=dst,
            send_sem=send_sem,
            recv_sem=recv_sem,
            device_id=target,
            device_id_type=MESH,
        )

    loads = [
        pltpu.make_async_copy(hidden_hbm, hid.at[core], load_sem.at[0]),
        pltpu.make_async_copy(cot_hbm, cot_raw.at[core], load_sem.at[1]),
        pltpu.make_async_copy(wq_hbm, wqkv.at[0], load_sem.at[2]),
        pltpu.make_async_copy(wk_hbm, wqkv.at[1], load_sem.at[3]),
        pltpu.make_async_copy(wv_hbm, wqkv.at[2], load_sem.at[4]),
        pltpu.make_async_copy(wo_hbm, wo.at[core], load_sem.at[5]),
    ]
    for load in loads:
        load.start()

    def weight_loads(chunk, slot):
        columns = pl.ds(pl.multiple_of(chunk * CW, CW), CW)
        return [
            pltpu.make_async_copy(src.at[:, columns], dst.at[slot], weight_sem.at[slot, index])
            for index, (src, dst) in enumerate(((wg_hbm, wg), (wu_hbm, wu), (wd_hbm, wd)))
        ]

    barrier = pltpu.get_barrier_semaphore()
    pl.semaphore_signal(barrier, inc=1, device_id=sibling, device_id_type=MESH)
    for k in range(cfg.bits):
        pl.semaphore_signal(barrier, inc=1, device_id=(peer[k], core), device_id_type=MESH)
    for index, gain in enumerate((gain_one, gain_two)):
        line = gain[...].reshape(1, width)
        for block in blocks_of(width, 128):
            size = block.stop - block.start
            gains[index, block, :] = jnp.transpose(
                jnp.broadcast_to(line[:, block], (128, size))
            )
    group_len = jnp.int32(0)
    for item in range(lengths.shape[0]):
        group_len = group_len + jnp.where(groups[item] == me, lengths[item], 0)

    loads[1].wait()
    lane_valid = lax.broadcasted_iota(jnp.int32, (1, rows), 1) + core * rows < group_len
    for block in blocks_of(width, 128):
        part = jnp.where(lane_valid, cot_raw[core, block, :].astype(F32), 0.0)
        cot[own_rows, block] = jnp.transpose(part).astype(BF)
    pl.semaphore_wait(barrier, cfg.bits + 1)

    pair_hid = send(
        hidden_hbm, hid.at[core], pair_send_sem.at[0], pair_recv_sem.at[0], sibling
    )
    pair_cot = send(
        cot_hbm, cot_raw.at[core], pair_send_sem.at[1], pair_recv_sem.at[1], sibling
    )
    pair_wo = send(wo_hbm, wo.at[core], pair_send_sem.at[2], pair_recv_sem.at[2], sibling)
    pair_rows = send(
        cot.at[own_rows], cot.at[own_rows], pair_send_sem.at[7], pair_recv_sem.at[7], sibling
    )

    natural = (cot, normed_two)

    def near_copy(near, which):
        return send(
            natural[which].at[own_rows],
            near_rows.at[near, which, own_rows],
            near_send_sem.at[near, which],
            near_recv_sem.at[near, which],
            (peer[cfg.near[near]], core),
        )

    def near_pass(near, which):
        return send(
            near_rows.at[near, which, own_rows],
            near_rows.at[near, which, own_rows],
            pass_send_sem.at[near, which],
            pass_recv_sem.at[near, which],
            sibling,
        )

    pair_hid.start()
    pair_cot.start()
    pair_wo.start()
    pair_rows.start()
    for near in range(len(cfg.near)):
        near_copy(near, 0).start()
    pair_att = send(
        attended.at[core], attended.at[core], pair_send_sem.at[3], pair_recv_sem.at[3], sibling
    )
    pair_grad = send(grad_send, grad_in, pair_send_sem.at[4], pair_recv_sem.at[4], sibling)
    pair_part = send(part_send, part_in, pair_send_sem.at[5], pair_recv_sem.at[5], sibling)
    pair_back = send(back_send, back_in, pair_send_sem.at[6], pair_recv_sem.at[6], sibling)

    for slot in range(2):
        for load in weight_loads(slot, slot):
            load.start()

    def place_of(index):
        place = 0
        for k in range(3, cfg.bits):
            place = 2 * place + ((index >> k) & 1)
        return slice(place * cfg.shard_pad, (place + 1) * cfg.shard_pad)

    def shard_of(source, index):
        return source[index * cfg.shard : index * cfg.shard + cfg.shard_pad, :].astype(BF)

    def build_left(source, which):
        for index in range(cfg.dp):
            left_own[which, index & 7, place_of(index), :] = shard_of(source, index)

    def adopt(near, which):
        near_copy(near, which).wait()
        near_pass(near, which).start()
        near_pass(near, which).wait()
        axis = cfg.near[near]
        high, low = (k for k in (2, 1, 0) if k != axis)
        for block in blocks_of(width, 128):
            trans[block, :] = jnp.transpose(near_rows[near, which, :, block].astype(F32))
        for value in range(2):

            @pl.when(bit[axis] == value)
            def _(value=value):
                for index in range(cfg.dp):
                    if (index >> axis) & 1 == value:
                        place = 2 * ((index >> high) & 1) + ((index >> low) & 1)
                        left_in[near, which, place, place_of(index), :] = shard_of(trans, index)

    def left_copy(which):
        return send(
            left_own.at[2 + which, pl.ds(4 * (1 - bit[2]) + 2 * core, 2)],
            left_in.at[len(cfg.near), which, pl.ds(2 * core, 2)],
            left_send_sem.at[which],
            left_recv_sem.at[which],
            (peer[2], core),
        )

    def left_share(which):
        return send(
            left_in.at[len(cfg.near), which, pl.ds(2 * core, 2)],
            left_in.at[len(cfg.near), which, pl.ds(2 * core, 2)],
            share_send_sem.at[which],
            share_recv_sem.at[which],
            sibling,
        )

    def left_pass(which):
        left_copy(which).wait()
        left_share(which).start()

    def block_of(chunk):
        return lax.div(chunk, 3)

    def pick(chunk, level, values):
        if level > 2:
            return values[level]
        k = lookup([axes[level] for axes in AXES], block_of(chunk))
        parts = (lax.div((1 - k) * (2 - k), 2), k * (2 - k), lax.div(k * (k - 1), 2))
        return sum(part * value for part, value in zip(parts, values))

    def right_slot(chunk):
        tail_part = lax.div(chunk, cfg.ff_total)
        return (1 - tail_part) * lax.rem(chunk, RING) + tail_part * (RING + chunk - cfg.ff_total)

    def right_copy(index):
        return send(
            right_own.at[RING + index],
            right_in.at[RING + index],
            right_send_sem.at[index],
            right_recv_sem.at[index],
            (peer[2], core),
        )

    for scratch in (trans, grad_acc):
        scratch[width:, :] = jnp.zeros((cfg.tall - width, seq), F32)

    step_rows = STEP
    steps = width // step_rows

    def rows_at(step):
        return pl.ds(pl.multiple_of(step * step_rows, step_rows), step_rows)

    def whole(ref, block):
        return jnp.concatenate([ref[0, block, :], ref[1, block, :]], axis=1)

    def gain_at(index, block, lanes):
        part = gains[index, block, :]
        return jnp.concatenate([part] * (lanes // 128), axis=1)

    def column_sum(term, lanes):
        zero = jnp.zeros((8, lanes), F32)
        total = lax.fori_loop(0, steps, lambda i, acc: acc + fold(term(rows_at(i))), zero)
        return jnp.sum(total, axis=0, keepdims=True)

    def inverse_rms(term, lanes):
        def square(block):
            x = term(block)
            return x * x

        return lax.rsqrt(column_sum(square, lanes) * (1.0 / width) + EPS)

    loads[0].wait()
    pair_hid.wait()

    def x_at(block):
        return whole(hid, block).astype(F32)

    inv_one = inverse_rms(x_at, seq)

    def norm_one_rows(step, carry):
        block = rows_at(step)
        normed = x_at(block) * inv_one * gain_at(0, block, seq)
        trans[block, :] = normed
        normed_one[block, :] = normed.astype(BF)
        return carry

    lax.fori_loop(0, steps, norm_one_rows, 0)

    for part in range(3):
        loads[2 + part].wait()
        qkv[part] = dot(wqkv[part], normed_one[...]).astype(BF)

    key_valid = lax.broadcasted_iota(jnp.int32, (seq, seq), 0) < group_len
    ids_row[...] = jnp.full(ids_row.shape, -1, jnp.int32)
    ids_row[:, : bucket_ids.shape[0]] = bucket_ids[...].reshape(1, -1)
    ids = ids_row[...]
    for head in range(heads):
        part = slice(head * DKV, (head + 1) * DKV)
        by_offset = jnp.zeros(ids.shape, F32)
        for bucket in range(cfg.buckets):
            by_offset = jnp.where(ids == bucket, position_bias[head, bucket], by_offset)
        bias = pltpu.roll(
            jnp.broadcast_to(by_offset, (seq, 2 * seq)),
            seq + 1,
            1,
            stride=1,
            stride_axis=0,
        )[:, :seq]
        scores = dot_tn(qkv[1, part, :], qkv[0, part, :]) + jnp.transpose(bias)
        scores = jnp.where(key_valid, scores, -1e30)
        exps = jnp.exp(scores - jnp.max(scores, axis=0, keepdims=True))
        prob = exps / jnp.sum(exps, axis=0, keepdims=True)
        probs[head] = prob
        attended[core, part, :] = dot(qkv[2, part, :], prob.astype(BF)).astype(BF)
    pair_att.start()

    build_left(trans, 2)
    pair_cot.wait()
    pair_rows.wait()
    row_valid = lax.broadcasted_iota(jnp.int32, (step_rows, seq), 1) < group_len

    def mask_rows(step, carry):
        block = rows_at(step)
        trans[block, :] = jnp.where(row_valid, whole(cot_raw, block).astype(F32), 0.0)
        return carry

    lax.fori_loop(0, steps, mask_rows, 0)
    build_left(trans, 0)

    loads[5].wait()
    pair_wo.wait()
    for block in blocks_of(width, 128):
        wo_t[block, :] = jnp.transpose(
            jnp.concatenate([wo[0, :, block], wo[1, :, block]], axis=0).astype(F32)
        ).astype(BF)
    pair_att.wait()
    both = attended[...].reshape(2 * hw, seq)
    for block in blocks_of(width, MROWS):
        middle[block, :] = x_at(block) + dot(wo_t[block, :], both)

    inv_two = inverse_rms(lambda block: middle[block, :], seq)

    def norm_two_rows(step, carry):
        block = rows_at(step)
        trans[block, :] = middle[block, :] * inv_two * gain_at(1, block, seq)
        out_acc[block, :] = jnp.zeros((step_rows, seq), F32)
        grad_acc[block, :] = jnp.zeros((step_rows, seq), F32)
        return carry

    lax.fori_loop(0, steps, norm_two_rows, 0)
    for block in blocks_of(width, 128):
        normed_two[:, block] = jnp.transpose(trans[block, :]).astype(BF)
    for near in range(len(cfg.near)):
        near_copy(near, 1).start()
    build_left(trans, 1)
    small[...] = jnp.zeros_like(small)

    def feed_forward(chunk):
        slot = lax.rem(chunk, 2)
        for load in weight_loads(chunk, slot):
            load.wait()
        first = lax.rem(3 * chunk, RING)

        def activations(normed, grad_rows, target):
            gate = dot(normed, wg[slot])
            up = dot(normed, wu[slot])
            grad_hidden = dot(grad_rows, wd[slot])
            square = gate * gate
            tanh = jnp.tanh(GELU_C * (gate + 0.044715 * (square * gate)))
            half = 0.5 * (1.0 + tanh)
            gelu = gate * half
            slope = half + (0.5 * GELU_C) * gate * (1.0 - tanh * tanh) * (
                1.0 + (3 * 0.044715) * square
            )
            target[first] = (gelu * up).astype(BF)
            target[first + 1] = (grad_hidden * up * slope).astype(BF)
            target[first + 2] = (grad_hidden * gelu).astype(BF)

        activations(normed_two[...], cot[...], right_own)
        hidden, grad_gate, grad_up = (right_own[first + kind] for kind in range(3))
        for block in blocks_of(width, MROWS):
            out_acc[block, :] += dot_nt(wd[slot, block, :], hidden)
            grad_acc[block, :] += dot_nt(wg[slot, block, :], grad_gate) + dot_nt(
                wu[slot, block, :], grad_up
            )

        for near, use in enumerate(cfg.first_use):

            @pl.when(chunk == use)
            def _(near=near):
                adopt(near, 0)
                adopt(near, 1)

        near = lookup([cfg.near.index(axes[0]) for axes in AXES[: cfg.ff_chunks]], chunk)
        activations(near_rows[near, 1], near_rows[near, 0], right_in)

        @pl.when(chunk < cfg.ff_chunks - 2)
        def _():
            for load in weight_loads(chunk + 2, slot):
                load.start()

    def exchange_sums():
        left_copy(0).start()
        grad_send[...] = grad_acc[:width, :].astype(BF)
        pair_grad.start()
        part_send[...] = out_acc[:, other_lanes].astype(BF)
        pair_part.start()

    def lane_mask(shape, dimension):
        lane = lax.broadcasted_iota(jnp.int32, shape, dimension)
        return (lax.div(lane, rows) == core).astype(F32)

    def lane_sums(weights, source):
        return lax.dot_general(
            weights,
            source,
            (((1,), (1,)), ((), ())),
            precision=lax.Precision.HIGHEST,
            preferred_element_type=F32,
        )[0:1, :]

    def put_small(row, line):
        small[row : row + 1, :] = line[:, : cfg.half]
        small[row + 1 : row + 2, : width - cfg.half] = line[:, cfg.half :]

    def norm_two_back():
        pair_grad.wait()

        def grad_at(block):
            return grad_acc[block, :] + grad_in[block, :].astype(F32)

        inv = inverse_rms(lambda block: middle[block, :], seq)
        inner = (
            column_sum(
                lambda block: grad_at(block) * gain_at(1, block, seq) * middle[block, :], seq
            )
            * inv
            * (1.0 / width)
        )

        def back_rows(step, carry):
            block = rows_at(step)
            grad = grad_at(block)
            unit = middle[block, :] * inv
            masked = jnp.where(row_valid, whole(cot_raw, block).astype(F32), 0.0)
            total = masked + inv * (grad * gain_at(1, block, seq) - unit * inner)
            trans[block, :] = grad * unit
            grad_acc[block, :] = total
            grad_branch[block, :] = total.astype(BF)
            return carry

        lax.fori_loop(0, steps, back_rows, 0)
        build_left(grad_acc, 3)
        left_copy(1).start()
        mask = lane_mask((8, seq), 1)
        put_small(2, lane_sums(mask, trans[:width, :]))

    def attention_back():
        grad_att = dot(wo[core], grad_branch[...]).astype(BF)
        flip = (
            lax.broadcasted_iota(jnp.int32, (seq, seq), 0)
            + lax.broadcasted_iota(jnp.int32, (seq, seq), 1)
            == seq - 1
        ).astype(BF)
        for head in range(heads):
            part = slice(head * DKV, (head + 1) * DKV)
            grad_mixed = grad_att[part, :]
            prob = probs[head]
            grad_probs = dot_tn(qkv[2, part, :], grad_mixed)
            inner = jnp.sum(prob * grad_probs, axis=0, keepdims=True)
            grad_scores = (prob * (grad_probs - inner)).astype(BF)
            grad_qkv[0, part, :] = dot(qkv[1, part, :], grad_scores).astype(BF)
            grad_qkv[1, part, :] = dot_nt(qkv[0, part, :], grad_scores).astype(BF)
            grad_qkv[2, part, :] = dot_nt(grad_mixed, prob.astype(BF)).astype(BF)
            flipped = jnp.concatenate(
                [dot(grad_scores, flip), jnp.zeros((seq, seq), F32)], axis=1
            )
            skewed = pltpu.roll(flipped, 0, 1, stride=1, stride_axis=0)
            small[4 + head : 5 + head, : 2 * seq] = jnp.sum(skewed, axis=0, keepdims=True)
        joined = jnp.concatenate(
            [grad_qkv[...].reshape(3 * hw, seq), attended[core]], axis=0
        ).astype(F32)
        for index in range(cfg.chunks - cfg.ff_total):
            right_own[RING + index] = jnp.transpose(
                joined[index * CW : (index + 1) * CW, :]
            ).astype(BF)
            right_copy(index).start()

    def norm_one_sums():
        for block in blocks_of(width, 128):
            back_send[block, :] = sum(
                dot_tn(wqkv[part, :, block], grad_qkv[part, :, other_lanes]) for part in range(3)
            ).astype(BF)
        pair_back.start()
        for block in blocks_of(width, 128):
            input_grad[block, :] = sum(
                dot_tn(wqkv[part, :, block], grad_qkv[part, :, own_lanes]) for part in range(3)
            )

    def small_copy(k):
        target = sibling if k == cfg.bits else (peer[k], core)
        return send(
            small, small_in.at[k], small_send_sem.at[k], small_recv_sem.at[k], target
        )

    def finish_rows():
        pair_part.wait()
        pair_back.wait()

        def x_own(block):
            return hid[core, block, :].astype(F32)

        def grad_at(block):
            return input_grad[block, :] + back_in[block, :].astype(F32)

        inv = inverse_rms(x_own, rows)
        inner = (
            column_sum(lambda block: grad_at(block) * gain_at(0, block, rows) * x_own(block), rows)
            * inv
            * (1.0 / width)
        )

        def last_rows(step, carry):
            block = rows_at(step)
            grad = grad_at(block)
            unit = x_own(block) * inv
            input_grad[block, :] = grad_acc[block, own_lanes] + inv * (
                grad * gain_at(0, block, rows) - unit * inner
            )
            layer_out[block, :] = (
                middle[block, own_lanes]
                + out_acc[block, own_lanes]
                + part_in[block, :].astype(F32)
            )
            trans[block, :rows] = grad * unit
            return carry

        lax.fori_loop(0, steps, last_rows, 0)
        put_small(0, lane_sums(jnp.ones((8, rows), F32), trans[:width, :rows]))
        small_copy(0).start()

    def small_stage(k):
        small_copy(k).wait()
        if k == cfg.bits:
            row = lax.broadcasted_iota(jnp.int32, small.shape, 0)
            small_out[...] = small[...] + jnp.where(row < 4, small_in[k], 0.0)
        else:
            small[...] = small[...] + small_in[k]
            small_copy(k + 1).start()

    def stage_copy(k, chunk, slot, target):
        return send(
            stage_send[k].at[slot],
            stage_in[k].at[chunk],
            stage_send_sem.at[k, slot],
            stage_recv_sem.at[k, chunk],
            (target, core),
        )

    def stage_target(k, chunk):
        return pick(chunk, k + 1, peer)

    def form(chunk, slot):
        tail_part = lax.div(chunk, cfg.ff_total)
        which = (1 - tail_part) * lax.div(lax.rem(chunk, 3) + 1, 2)
        block = block_of(chunk)
        spot = right_slot(chunk)
        second_bit = pick(chunk, 1, bit)
        weights = [pick(chunk, level, (1, 2, 4)) for level in range(3)]
        descending = lookup([int(axes[1] > axes[2]) for axes in AXES], block)
        near_weights = 1 + descending, 2 - descending
        begin = weights[0] * pick(chunk, 0, bit)

        @pl.when(chunk == cfg.ff_total)
        def _():
            left_pass(0)
            left_share(0).wait()

        @pl.when(chunk == cfg.chunks - 1)
        def _():
            left_pass(1)
            left_share(1).wait()

        for index in range(cfg.chunks - cfg.ff_total):

            @pl.when(chunk == cfg.ff_total + index)
            def _(index=index):
                right_copy(index).wait()

        def product(own, near, second, third):
            eighth = begin + weights[1] * second + weights[2] * third
            return dot(left_own[own, eighth], right_own[spot]) + dot(
                left_in[near, which, near_weights[0] * second + near_weights[1] * third],
                right_in[spot],
            )

        def fill(value):
            for third in range(2):
                part = slice(third * cfg.eighth, (third + 1) * cfg.eighth)
                stage_send[0][slot, part, :] = value(1 - second_bit, third).astype(BF)
            stage_copy(0, chunk, slot, stage_target(0, chunk)).start()
            for third in range(2):
                part = slice(third * cfg.eighth, (third + 1) * cfg.eighth)
                stage_own[0][slot, part, :] = value(second_bit, third)

        own = 2 * tail_part + which
        near = lookup(
            [cfg.near.index(axes[0]) for axes in AXES[: cfg.ff_chunks]] + [len(cfg.near)], block
        )

        @pl.when(chunk < cfg.chunks - 1)
        def _():
            fill(functools.partial(product, own, near))

        @pl.when(chunk == cfg.chunks - 1)
        def _():
            split = lax.broadcasted_iota(jnp.int32, (cfg.eighth, CW), 1) < CW - hw

            def mixed(second, third):
                eighth = begin + weights[1] * second + weights[2] * third
                parts = [
                    dot(left_own[2 + index, eighth], right_own[spot])
                    + dot(
                        left_in[
                            len(cfg.near),
                            index,
                            near_weights[0] * second + near_weights[1] * third,
                        ],
                        right_in[spot],
                    )
                    for index in range(2)
                ]
                return jnp.where(split, *parts)

            fill(mixed)

    def halve(k, chunk, slot):
        stage_copy(k - 1, chunk, slot, stage_target(k - 1, chunk)).wait()
        if k == stages:
            result = stage_own[k - 1][slot] + stage_in[k - 1][chunk].astype(F32)

            @pl.when(chunk < cfg.ff_total)
            def _():
                columns = pl.ds(pl.multiple_of(lax.div(chunk, 3) * CW, CW), CW)
                ff_out[lax.rem(chunk, 3), :, columns] = result[: cfg.shard, :]

            @pl.when(chunk >= cfg.ff_total)
            def _():
                att_final[lax.rem(chunk, cfg.ff_total)] = result

            return
        half = cfg.stage_rows[k]
        mine = pick(chunk, k + 1, bit)

        def total(which):
            part = pl.ds(pl.multiple_of(which * half, 16), half)
            return stage_own[k - 1][slot, part, :] + stage_in[k - 1][chunk, part, :].astype(F32)

        stage_send[k][slot] = total(1 - mine).astype(BF)
        stage_copy(k, chunk, slot, stage_target(k, chunk)).start()
        stage_own[k][slot] = total(mine)

    last_ff = FF_TICKS[-1]
    pieces = [exchange_sums, norm_two_back, attention_back, norm_one_sums, finish_rows]
    pieces = [(last_ff + index, piece) for index, piece in enumerate(pieces)]
    for k in range(cfg.bits + 1):
        pieces.append((pieces[-1][0] + SMALL_GAP, functools.partial(small_stage, k)))
    ticks = max(LAG + cfg.chunks + GAP * stages, pieces[-1][0] + 1)

    def tick(t, carry):
        ff_now = sum(jnp.where(t == when, 1, 0) for when in FF_TICKS)
        ff_done = sum(jnp.where(t > when, 1, 0) for when in FF_TICKS)

        @pl.when(ff_now > 0)
        def _():
            feed_forward(ff_done)

        for k in range(stages, 0, -1):
            spot = t - LAG - GAP * k

            @pl.when(jnp.logical_and(spot >= 0, spot < cfg.chunks))
            def _(k=k, spot=spot):
                halve(k, lookup(cfg.order, spot), lax.rem(spot, SLOTS))

        new = t - LAG

        @pl.when(jnp.logical_and(new >= 0, new < cfg.chunks))
        def _():
            form(lookup(cfg.order, new), lax.rem(new, SLOTS))

        for when, piece in pieces:

            @pl.when(t == when)
            def _(piece=piece):
                piece()

        return carry

    lax.fori_loop(0, ticks, tick, 0)

    flat = jnp.concatenate([att_final[index] for index in range(cfg.chunks - cfg.ff_total)], axis=1)
    for part, ref in enumerate((query_out, key_out, value_out)):
        ref[...] = flat[: cfg.shard, part * hw : (part + 1) * hw]
    output_out[...] = jnp.transpose(flat[:, 3 * hw :])[:, : cfg.shard]


def finish_kernel(
    cfg,
    layer_in,
    grad_in,
    query_in,
    key_in,
    value_in,
    output_in,
    ff_in,
    small,
    bucket_ids,
    layer_out,
    grad_out,
    gain_one,
    query_out,
    key_out,
    value_out,
    output_out,
    bias_out,
    gain_two,
    gate_out,
    up_out,
    down_out,
    *rest,
):
    pairs = [
        (ff_in.at[0], down_out),
        (ff_in.at[1], gate_out),
        (ff_in.at[2], up_out),
        (layer_in, layer_out),
        (grad_in, grad_out),
        (query_in, query_out),
        (key_in, key_out),
        (value_in, value_out),
        (output_in, output_out),
    ]
    buffers, (load_sem, store_sem) = rest[:-2], rest[-2:]
    loads, stores = [], []
    for index, ((src, dst), buffer) in enumerate(zip(pairs, buffers)):
        loads.append(pltpu.make_async_copy(src, buffer, load_sem.at[index]))
        stores.append(pltpu.make_async_copy(buffer, dst, store_sem.at[index]))
    for load in loads:
        load.start()
    for load, store in zip(loads, stores):
        load.wait()
        store.start()
    for row, gain in ((0, gain_one), (2, gain_two)):
        line = jnp.concatenate([small[row : row + 1, :], small[row + 1 : row + 2, :]], axis=1)
        gain[...] = line[:, : cfg.width].reshape(cfg.width)
    offsets = bucket_ids.shape[0]
    bucket = lax.broadcasted_iota(jnp.int32, (cfg.buckets, offsets), 0)
    onehot = (bucket_ids[...].reshape(1, offsets) == bucket).astype(F32)
    sums = lax.dot_general(
        small[:, :offsets],
        onehot,
        (((1,), (1,)), ((), ())),
        precision=lax.Precision.HIGHEST,
        preferred_element_type=F32,
    )
    bias_out[...] = sums[4 : 4 + cfg.heads, :]
    for store in stores:
        store.wait()


def shards(
    mesh,
    hidden_in,
    attention_gain,
    query_weight,
    key_weight,
    value_weight,
    output_weight,
    position_bias,
    feedforward_gain,
    gate_weight,
    up_weight,
    down_weight,
    cotangent,
    item_lengths,
    item_group,
    bucket_ids,
):
    rows, width = hidden_in.shape
    hw = query_weight.shape[1]
    hidden = gate_weight.shape[1]
    buckets = position_bias.shape[0]
    cfg = Sizes(mesh.shape["dp"], rows, width, hw, hidden, buckets)
    seq, stages, shard = cfg.seq, cfg.stages, cfg.shard
    any_spec = pl.BlockSpec(memory_space=pl.ANY)
    vmem = pl.BlockSpec(memory_space=pltpu.VMEM)
    smem = pl.BlockSpec(memory_space=pltpu.SMEM)
    small_shape = (8, cfg.half)
    scratch = [
        pltpu.VMEM((2, width, rows), BF),
        pltpu.VMEM((2, width, rows), BF),
        pltpu.VMEM((seq, width), BF),
        pltpu.VMEM((2, width, 128), F32),
        pltpu.VMEM((3, hw, width), BF),
        pltpu.VMEM((2, hw, width), BF),
        pltpu.VMEM((width, 2 * hw), BF),
        pltpu.VMEM((2, width, CW), BF),
        pltpu.VMEM((2, width, CW), BF),
        pltpu.VMEM((2, width, CW), BF),
        pltpu.VMEM((width, seq), BF),
        pltpu.VMEM((seq, width), BF),
        pltpu.VMEM((width, seq), F32),
        pltpu.VMEM((3, hw, seq), BF),
        pltpu.VMEM((cfg.heads, seq, seq), F32),
        pltpu.VMEM((2, hw, seq), BF),
        pltpu.VMEM((cfg.tall, seq), F32),
        pltpu.VMEM((4, 8, cfg.eighth, seq), BF),
        pltpu.VMEM((len(cfg.near) + 1, 2, 4, cfg.eighth, seq), BF),
        pltpu.VMEM((len(cfg.near), 2, seq, width), BF),
        pltpu.VMEM((RING + cfg.chunks - cfg.ff_total, seq, CW), BF),
        pltpu.VMEM((RING + cfg.chunks - cfg.ff_total, seq, CW), BF),
        pltpu.VMEM((width, seq), F32),
        pltpu.VMEM((cfg.tall, seq), F32),
        pltpu.VMEM((width, seq), BF),
        pltpu.VMEM((width, rows), BF),
        pltpu.VMEM((width, rows), BF),
        pltpu.VMEM((width, rows), BF),
        pltpu.VMEM((width, rows), BF),
        pltpu.VMEM((width, seq), BF),
        pltpu.VMEM((3, hw, seq), BF),
        pltpu.VMEM(small_shape, F32),
        pltpu.VMEM((cfg.bits + 1,) + small_shape, F32),
        pltpu.VMEM((cfg.chunks - cfg.ff_total, cfg.shard_pad, CW), F32),
        pltpu.VMEM((1, 2 * seq), jnp.int32),
    ]
    scratch += [pltpu.VMEM((SLOTS, size, CW), F32) for size in cfg.stage_rows]
    scratch += [pltpu.VMEM((SLOTS, size, CW), BF) for size in cfg.stage_rows]
    scratch += [pltpu.VMEM((cfg.chunks, size, CW), BF) for size in cfg.stage_rows]
    dma = pltpu.SemaphoreType.DMA
    scratch += [
        dma((6,)),
        dma((2, 3)),
        dma((8,)),
        dma((8,)),
        dma((2,)),
        dma((2,)),
        dma((2,)),
        dma((2,)),
        dma((3, 2)),
        dma((3, 2)),
        dma((3, 2)),
        dma((3, 2)),
        dma((cfg.chunks - cfg.ff_total,)),
        dma((cfg.chunks - cfg.ff_total,)),
        dma((stages, SLOTS)),
        dma((stages, cfg.chunks)),
        dma((cfg.bits + 1,)),
        dma((cfg.bits + 1,)),
    ]
    (
        layer_out,
        input_grad,
        small_sum,
        ff_sum,
        query_sum,
        key_sum,
        value_sum,
        output_sum,
    ) = pl.pallas_call(
        functools.partial(layer_kernel, cfg),
        out_shape=[
            jax.ShapeDtypeStruct((width, rows), F32),
            jax.ShapeDtypeStruct((width, rows), F32),
            jax.ShapeDtypeStruct(small_shape, F32),
            jax.ShapeDtypeStruct((3, shard, hidden), F32),
            jax.ShapeDtypeStruct((shard, hw), F32),
            jax.ShapeDtypeStruct((shard, hw), F32),
            jax.ShapeDtypeStruct((shard, hw), F32),
            jax.ShapeDtypeStruct((hw, shard), F32),
        ],
        in_specs=[
            any_spec,
            vmem,
            any_spec,
            any_spec,
            any_spec,
            any_spec,
            smem,
            vmem,
            any_spec,
            any_spec,
            any_spec,
            any_spec,
            smem,
            smem,
            vmem,
        ],
        out_specs=[vmem] * 8,
        scratch_shapes=scratch,
        compiler_params=pltpu.CompilerParams(
            collective_id=0, has_side_effects=True, vmem_limit_bytes=62 * 1024 * 1024
        ),
        cost_estimate=pl.CostEstimate(
            flops=14 * 10**9, bytes_accessed=24 * 10**6, transcendentals=10**6
        ),
    )(
        hidden_in.T,
        attention_gain,
        query_weight.T,
        key_weight.T,
        value_weight.T,
        output_weight,
        position_bias.T,
        feedforward_gain,
        gate_weight,
        up_weight,
        down_weight.T,
        cotangent.T,
        item_lengths,
        item_group,
        bucket_ids,
    )
    def like(array):
        return jax.ShapeDtypeStruct(array.shape, array.dtype)

    one_ff = jax.ShapeDtypeStruct((shard, hidden), F32)
    outs = pl.pallas_call(
        functools.partial(finish_kernel, cfg),
        out_shape=[
            like(layer_out),
            like(input_grad),
            like(attention_gain),
            like(query_sum),
            like(key_sum),
            like(value_sum),
            like(output_sum),
            jax.ShapeDtypeStruct((cfg.heads, buckets), F32),
            like(feedforward_gain),
            one_ff,
            one_ff,
            one_ff,
        ],
        in_specs=[any_spec] * 7 + [vmem, vmem],
        out_specs=[any_spec] * 2 + [vmem] + [any_spec] * 4 + [vmem] * 2 + [any_spec] * 3,
        scratch_shapes=[
            pltpu.VMEM(array.shape, F32)
            for array in (one_ff,) * 3
            + (layer_out, input_grad, query_sum, key_sum, value_sum, output_sum)
        ]
        + [dma((9,)), dma((9,))],
        compiler_params=pltpu.CompilerParams(vmem_limit_bytes=62 * 1024 * 1024),
    )(
        layer_out,
        input_grad,
        query_sum,
        key_sum,
        value_sum,
        output_sum,
        ff_sum,
        small_sum,
        bucket_ids,
    )
    layer_out, input_grad, gain_one, query, key, value, output, bias, gain_two, gate, up, down = outs
    return (
        layer_out.T,
        input_grad.T,
        gain_one,
        query,
        key,
        value,
        output,
        bias.T,
        gain_two,
        gate,
        up,
        down.T,
    )


def solution(mesh):
    in_specs = (
        P(("dp", "mp"), None),
        P(),
        P(None, "mp"),
        P(None, "mp"),
        P(None, "mp"),
        P("mp", None),
        P(None, "mp"),
        P(),
        P(None, "mp"),
        P(None, "mp"),
        P("mp", None),
        P(("dp", "mp"), None),
        P(),
        P(),
        P(),
    )
    out_specs = (
        P(("dp", "mp"), None),
        P(("dp", "mp"), None),
        P(),
        P("dp", "mp"),
        P("dp", "mp"),
        P("dp", "mp"),
        P("mp", "dp"),
        P(None, "mp"),
        P(),
        P("dp", "mp"),
        P("dp", "mp"),
        P("mp", "dp"),
    )
    return jax.shard_map(
        functools.partial(shards, mesh),
        mesh=mesh,
        in_specs=in_specs,
        out_specs=out_specs,
        check_vma=False,
    )
```

```python
import functools
import math

import jax
import jax.numpy as jnp
from jax import lax
from jax.experimental import pallas as pl
from jax.experimental.pallas import tpu as pltpu
from jax.sharding import PartitionSpec as P

DKV = 64
CW = 256
EPS = 1e-06
AXES = ((1, 0, 2), (1, 2, 0), (2, 1, 0), (2, 1, 0), (2, 0, 1), (2, 1, 0), (1, 0, 2), (2, 1, 0))
TOGETHER = (2, 3, 2)
OWN_TICKS = (0, 1, 5, 8, 10, 11, 13)
NEAR_TICKS = (2, 3, 6, 9, 10, 12, 14)
RING_BLOCKS = 5
LAG = 2
GAPS = (4, 4, 4)
RING = 3 * RING_BLOCKS
SMALL_GAP = 3
STEP = 64
MROWS = 368
BF = jnp.bfloat16
F32 = jnp.float32
MESH = pl.DeviceIdType.MESH
GELU_C = math.sqrt(2.0 / math.pi)


def dot(left, right):
    return lax.dot_general(left, right, (((1,), (0,)), ((), ())), preferred_element_type=F32)


def dot_nt(left, right):
    return lax.dot_general(left, right, (((1,), (1,)), ((), ())), preferred_element_type=F32)


def dot_tn(left, right):
    return lax.dot_general(left, right, (((0,), (0,)), ((), ())), preferred_element_type=F32)


def blocks_of(extent, step):
    return [slice(begin, min(begin + step, extent)) for begin in range(0, extent, step)]


def fold(block):
    return jnp.sum(block.reshape(block.shape[0] // 8, 8, block.shape[1]), axis=0)


def lookup(table, index):
    bits = max(table).bit_length()
    if bits == 0:
        return 0 * index
    per = 30 // bits
    words = [
        sum(value << (bits * place) for place, value in enumerate(table[begin : begin + per]))
        for begin in range(0, len(table), per)
    ]
    word = jnp.int32(words[0])
    for place in range(1, len(words)):
        word = jnp.where(index >= place * per, words[place], word)
    shifted = lax.shift_right_logical(word, bits * lax.rem(index, per))
    return lax.rem(shifted, 1 << bits)


class Sizes:
    def __init__(self, dp, local_rows, width, head_width, hidden, buckets):
        self.dp = dp
        self.bits = dp.bit_length() - 1
        self.local_rows = local_rows
        self.seq = 2 * local_rows
        self.width = width
        self.head_width = head_width
        self.heads = head_width // DKV
        self.hidden = hidden
        self.buckets = buckets
        self.shard = width // dp
        self.shard_pad = -(-self.shard // 16) * 16
        self.quarter = self.shard_pad * dp // 4
        self.ff_chunks = hidden // CW
        self.ff_total = 3 * self.ff_chunks
        self.chunks = self.ff_total + 4 * head_width // CW
        self.stage_rows = [self.quarter >> k for k in range(self.bits - 1)]
        self.stages = len(self.stage_rows)
        self.half = -(-width // 256) * 128
        self.tall = width + self.shard_pad
        self.eighth = self.quarter // 2
        self.gaps = [GAPS[min(k, 2)] for k in range(self.stages)]
        self.late = [sum(self.gaps[:k]) for k in range(self.stages + 1)]
        self.order = []
        begin = 0
        for count in TOGETHER:
            self.order += [3 * (begin + f) + kind for kind in range(3) for f in range(count)]
            begin += count
        self.order += range(self.ff_total, self.chunks)
        self.near = sorted({axes[0] for axes in AXES[: self.ff_chunks]})
        self.first_use = [[axes[0] for axes in AXES].index(axis) for axis in self.near]


def layer_kernel(
    cfg,
    hidden_hbm,
    gain_one,
    wq_hbm,
    wk_hbm,
    wv_hbm,
    wo_hbm,
    position_bias,
    gain_two,
    wg_hbm,
    wu_hbm,
    wd_hbm,
    cot_hbm,
    lengths,
    groups,
    bucket_ids,
    layer_out,
    input_grad,
    small_out,
    ff_out,
    query_out,
    key_out,
    value_out,
    output_out,
    hid,
    cot_raw,
    cot,
    gains,
    wqkv,
    wo,
    wo_t,
    wg,
    wu,
    wd,
    normed_one,
    normed_two,
    middle,
    qkv,
    probs,
    attended,
    trans,
    left_own,
    left_in,
    near_rows,
    right_own,
    right_in,
    out_acc,
    grad_acc,
    grad_in,
    part_send,
    part_in,
    back_send,
    back_in,
    grad_branch,
    grad_qkv,
    small,
    small_in,
    att_final,
    ids_row,
    *rest,
):
    grad_send = normed_one
    stages = cfg.stages
    stage_own = rest[:stages]
    stage_send = rest[stages : 2 * stages]
    stage_in = rest[2 * stages : 3 * stages]
    (
        load_sem,
        weight_sem,
        pair_send_sem,
        pair_recv_sem,
        left_send_sem,
        left_recv_sem,
        share_send_sem,
        share_recv_sem,
        near_send_sem,
        near_recv_sem,
        pass_send_sem,
        pass_recv_sem,
        right_send_sem,
        right_recv_sem,
        stage_send_sem,
        stage_recv_sem,
        small_send_sem,
        small_recv_sem,
    ) = rest[3 * stages :]

    seq, rows, width, hw, heads = cfg.seq, cfg.local_rows, cfg.width, cfg.head_width, cfg.heads
    me = lax.axis_index("dp")
    core = lax.axis_index("mp")
    bit = [lax.rem(lax.div(me, 1 << k), 2) for k in range(cfg.bits)]
    peer = [me + (1 - 2 * bit[k]) * (1 << k) for k in range(cfg.bits)]
    sibling = (me, 1 - core)
    own_lanes = pl.ds(pl.multiple_of(core * rows, rows), rows)
    own_rows = own_lanes
    other_lanes = pl.ds(pl.multiple_of((1 - core) * rows, rows), rows)

    def send(src, dst, send_sem, recv_sem, target):
        return pltpu.make_async_remote_copy(
            src_ref=src,
            dst_ref=dst,
            send_sem=send_sem,
            recv_sem=recv_sem,
            device_id=target,
            device_id_type=MESH,
        )

    loads = [
        pltpu.make_async_copy(hidden_hbm, hid.at[core], load_sem.at[0]),
        pltpu.make_async_copy(cot_hbm, cot_raw.at[core], load_sem.at[1]),
        pltpu.make_async_copy(wq_hbm, wqkv.at[0], load_sem.at[2]),
        pltpu.make_async_copy(wk_hbm, wqkv.at[1], load_sem.at[3]),
        pltpu.make_async_copy(wv_hbm, wqkv.at[2], load_sem.at[4]),
        pltpu.make_async_copy(wo_hbm, wo.at[core], load_sem.at[5]),
    ]
    for load in loads:
        load.start()

    def weight_loads(chunk, slot):
        columns = pl.ds(pl.multiple_of(chunk * CW, CW), CW)
        return [
            pltpu.make_async_copy(src.at[:, columns], dst.at[slot], weight_sem.at[slot, index])
            for index, (src, dst) in enumerate(((wg_hbm, wg), (wu_hbm, wu), (wd_hbm, wd)))
        ]

    barrier = pltpu.get_barrier_semaphore()
    pl.semaphore_signal(barrier, inc=1, device_id=sibling, device_id_type=MESH)
    for k in range(cfg.bits):
        pl.semaphore_signal(barrier, inc=1, device_id=(peer[k], core), device_id_type=MESH)
    for index, gain in enumerate((gain_one, gain_two)):
        line = gain[...].reshape(1, width)
        for block in blocks_of(width, 128):
            size = block.stop - block.start
            gains[index, block, :] = jnp.transpose(
                jnp.broadcast_to(line[:, block], (128, size))
            )
    group_len = jnp.int32(0)
    for item in range(lengths.shape[0]):
        group_len = group_len + jnp.where(groups[item] == me, lengths[item], 0)

    loads[1].wait()
    lane_valid = lax.broadcasted_iota(jnp.int32, (1, rows), 1) + core * rows < group_len
    for block in blocks_of(width, 128):
        part = jnp.where(lane_valid, cot_raw[core, block, :].astype(F32), 0.0)
        cot[own_rows, block] = jnp.transpose(part).astype(BF)
    pl.semaphore_wait(barrier, cfg.bits + 1)

    pair_hid = send(
        hidden_hbm, hid.at[core], pair_send_sem.at[0], pair_recv_sem.at[0], sibling
    )
    pair_cot = send(
        cot_hbm, cot_raw.at[core], pair_send_sem.at[1], pair_recv_sem.at[1], sibling
    )
    pair_wo = send(wo_hbm, wo.at[core], pair_send_sem.at[2], pair_recv_sem.at[2], sibling)
    pair_rows = send(
        cot.at[own_rows], cot.at[own_rows], pair_send_sem.at[7], pair_recv_sem.at[7], sibling
    )

    natural = (cot, normed_two)

    def near_copy(near, which):
        return send(
            natural[which].at[own_rows],
            near_rows.at[near, which, own_rows],
            near_send_sem.at[near, which],
            near_recv_sem.at[near, which],
            (peer[cfg.near[near]], core),
        )

    def near_pass(near, which):
        return send(
            near_rows.at[near, which, own_rows],
            near_rows.at[near, which, own_rows],
            pass_send_sem.at[near, which],
            pass_recv_sem.at[near, which],
            sibling,
        )

    pair_hid.start()
    pair_cot.start()
    pair_wo.start()
    pair_rows.start()
    for near in range(len(cfg.near)):
        near_copy(near, 0).start()
    pair_att = send(
        attended.at[core], attended.at[core], pair_send_sem.at[3], pair_recv_sem.at[3], sibling
    )
    pair_grad = send(grad_send, grad_in, pair_send_sem.at[4], pair_recv_sem.at[4], sibling)
    pair_part = send(part_send, part_in, pair_send_sem.at[5], pair_recv_sem.at[5], sibling)
    pair_back = send(back_send, back_in, pair_send_sem.at[6], pair_recv_sem.at[6], sibling)

    for slot in range(2):
        for load in weight_loads(slot, slot):
            load.start()

    def place_of(index):
        place = 0
        for k in range(3, cfg.bits):
            place = 2 * place + ((index >> k) & 1)
        return slice(place * cfg.shard_pad, (place + 1) * cfg.shard_pad)

    def shard_of(source, index):
        return source[index * cfg.shard : index * cfg.shard + cfg.shard_pad, :].astype(BF)

    def build_left(source, which):
        for index in range(cfg.dp):
            left_own[which, index & 7, place_of(index), :] = shard_of(source, index)

    def adopt(near, which):
        near_copy(near, which).wait()
        near_pass(near, which).start()
        near_pass(near, which).wait()
        axis = cfg.near[near]
        high, low = (k for k in (2, 1, 0) if k != axis)
        for block in blocks_of(width, 128):
            trans[block, :] = jnp.transpose(near_rows[near, which, :, block].astype(F32))
        for value in range(2):

            @pl.when(bit[axis] == value)
            def _(value=value):
                for index in range(cfg.dp):
                    if (index >> axis) & 1 == value:
                        place = 2 * ((index >> high) & 1) + ((index >> low) & 1)
                        left_in[near, which, place, place_of(index), :] = shard_of(trans, index)

    def left_copy(which):
        return send(
            left_own.at[2 + which, pl.ds(4 * (1 - bit[2]) + 2 * core, 2)],
            left_in.at[len(cfg.near), which, pl.ds(2 * core, 2)],
            left_send_sem.at[which],
            left_recv_sem.at[which],
            (peer[2], core),
        )

    def left_share(which):
        return send(
            left_in.at[len(cfg.near), which, pl.ds(2 * core, 2)],
            left_in.at[len(cfg.near), which, pl.ds(2 * core, 2)],
            share_send_sem.at[which],
            share_recv_sem.at[which],
            sibling,
        )

    def left_pass(which):
        left_copy(which).wait()
        left_share(which).start()

    def block_of(chunk):
        return lax.div(chunk, 3)

    def pick(chunk, level, values):
        if level > 2:
            return values[level]
        k = lookup([axes[level] for axes in AXES], block_of(chunk))
        parts = (lax.div((1 - k) * (2 - k), 2), k * (2 - k), lax.div(k * (k - 1), 2))
        return sum(part * value for part, value in zip(parts, values))

    def right_slot(chunk):
        tail_part = lax.div(chunk, cfg.ff_total)
        return (1 - tail_part) * lax.rem(chunk, RING) + tail_part * (RING + chunk - cfg.ff_total)

    def right_copy(index):
        return send(
            right_own.at[RING + index],
            right_in.at[RING + index],
            right_send_sem.at[index],
            right_recv_sem.at[index],
            (peer[2], core),
        )

    for scratch in (trans, grad_acc):
        scratch[width:, :] = jnp.zeros((cfg.tall - width, seq), F32)

    step_rows = STEP
    steps = width // step_rows

    def rows_at(step):
        return pl.ds(pl.multiple_of(step * step_rows, step_rows), step_rows)

    def whole(ref, block):
        return jnp.concatenate([ref[0, block, :], ref[1, block, :]], axis=1)

    def gain_at(index, block, lanes):
        part = gains[index, block, :]
        return jnp.concatenate([part] * (lanes // 128), axis=1)

    def column_sum(term, lanes):
        zero = jnp.zeros((8, lanes), F32)
        total = lax.fori_loop(0, steps, lambda i, acc: acc + fold(term(rows_at(i))), zero)
        return jnp.sum(total, axis=0, keepdims=True)

    def inverse_rms(term, lanes):
        def square(block):
            x = term(block)
            return x * x

        return lax.rsqrt(column_sum(square, lanes) * (1.0 / width) + EPS)

    loads[0].wait()
    pair_hid.wait()

    def x_at(block):
        return whole(hid, block).astype(F32)

    inv_one = inverse_rms(x_at, seq)

    def norm_one_rows(step, carry):
        block = rows_at(step)
        normed = x_at(block) * inv_one * gain_at(0, block, seq)
        trans[block, :] = normed
        normed_one[block, :] = normed.astype(BF)
        return carry

    lax.fori_loop(0, steps, norm_one_rows, 0)

    for part in range(3):
        loads[2 + part].wait()
        qkv[part] = dot(wqkv[part], normed_one[...]).astype(BF)

    key_valid = lax.broadcasted_iota(jnp.int32, (seq, seq), 0) < group_len
    ids_row[...] = jnp.full(ids_row.shape, -1, jnp.int32)
    ids_row[:, : bucket_ids.shape[0]] = bucket_ids[...].reshape(1, -1)
    ids = ids_row[...]
    for head in range(heads):
        part = slice(head * DKV, (head + 1) * DKV)
        by_offset = jnp.zeros(ids.shape, F32)
        for bucket in range(cfg.buckets):
            by_offset = jnp.where(ids == bucket, position_bias[head, bucket], by_offset)
        bias = pltpu.roll(
            jnp.broadcast_to(by_offset, (seq, 2 * seq)),
            seq + 1,
            1,
            stride=1,
            stride_axis=0,
        )[:, :seq]
        scores = dot_tn(qkv[1, part, :], qkv[0, part, :]) + jnp.transpose(bias)
        scores = jnp.where(key_valid, scores, -1e30)
        exps = jnp.exp(scores - jnp.max(scores, axis=0, keepdims=True))
        prob = exps / jnp.sum(exps, axis=0, keepdims=True)
        probs[head] = prob
        attended[core, part, :] = dot(qkv[2, part, :], prob.astype(BF)).astype(BF)
    pair_att.start()

    build_left(trans, 2)
    pair_cot.wait()
    pair_rows.wait()
    row_valid = lax.broadcasted_iota(jnp.int32, (step_rows, seq), 1) < group_len

    def mask_rows(step, carry):
        block = rows_at(step)
        trans[block, :] = jnp.where(row_valid, whole(cot_raw, block).astype(F32), 0.0)
        return carry

    lax.fori_loop(0, steps, mask_rows, 0)
    build_left(trans, 0)

    loads[5].wait()
    pair_wo.wait()
    for block in blocks_of(width, 128):
        wo_t[block, :] = jnp.transpose(
            jnp.concatenate([wo[0, :, block], wo[1, :, block]], axis=0).astype(F32)
        ).astype(BF)
    pair_att.wait()
    both = attended[...].reshape(2 * hw, seq)
    for block in blocks_of(width, MROWS):
        middle[block, :] = x_at(block) + dot(wo_t[block, :], both)

    inv_two = inverse_rms(lambda block: middle[block, :], seq)

    def norm_two_rows(step, carry):
        block = rows_at(step)
        trans[block, :] = middle[block, :] * inv_two * gain_at(1, block, seq)
        out_acc[block, :] = jnp.zeros((step_rows, seq), F32)
        grad_acc[block, :] = jnp.zeros((step_rows, seq), F32)
        return carry

    lax.fori_loop(0, steps, norm_two_rows, 0)
    for block in blocks_of(width, 128):
        normed_two[:, block] = jnp.transpose(trans[block, :]).astype(BF)
    for near in range(len(cfg.near)):
        near_copy(near, 1).start()
    build_left(trans, 1)
    small[...] = jnp.zeros_like(small)

    def activations(chunk, normed, grad_rows, target):
        slot = lax.rem(chunk, 2)
        first = lax.rem(3 * chunk, RING)
        gate = dot(normed, wg[slot])
        up = dot(normed, wu[slot])
        grad_hidden = dot(grad_rows, wd[slot])
        square = gate * gate
        tanh = jnp.tanh(GELU_C * (gate + 0.044715 * (square * gate)))
        half = 0.5 * (1.0 + tanh)
        gelu = gate * half
        slope = half + (0.5 * GELU_C) * gate * (1.0 - tanh * tanh) * (
            1.0 + (3 * 0.044715) * square
        )
        target[first] = (gelu * up).astype(BF)
        target[first + 1] = (grad_hidden * up * slope).astype(BF)
        target[first + 2] = (grad_hidden * gelu).astype(BF)

    def forward_own(chunk):
        slot = lax.rem(chunk, 2)
        first = lax.rem(3 * chunk, RING)
        for load in weight_loads(chunk, slot):
            load.wait()
        activations(chunk, normed_two[...], cot[...], right_own)
        hidden, grad_gate, grad_up = (right_own[first + kind] for kind in range(3))
        for block in blocks_of(width, MROWS):
            out_acc[block, :] += dot_nt(wd[slot, block, :], hidden)
            grad_acc[block, :] += dot_nt(wg[slot, block, :], grad_gate) + dot_nt(
                wu[slot, block, :], grad_up
            )

    def forward_near(chunk):
        slot = lax.rem(chunk, 2)
        for near, use in enumerate(cfg.first_use):

            @pl.when(chunk == use)
            def _(near=near):
                adopt(near, 1)

        near = lookup([cfg.near.index(axes[0]) for axes in AXES[: cfg.ff_chunks]], chunk)
        activations(chunk, near_rows[near, 1], near_rows[near, 0], right_in)

        @pl.when(chunk < cfg.ff_chunks - 2)
        def _():
            for load in weight_loads(chunk + 2, slot):
                load.start()

    def exchange_sums():
        left_copy(0).start()
        grad_send[...] = grad_acc[:width, :].astype(BF)
        pair_grad.start()
        part_send[...] = out_acc[:, other_lanes].astype(BF)
        pair_part.start()

    def lane_mask(shape, dimension):
        lane = lax.broadcasted_iota(jnp.int32, shape, dimension)
        return (lax.div(lane, rows) == core).astype(F32)

    def lane_sums(weights, source):
        high = source.astype(BF)
        low = (source - high.astype(F32)).astype(BF)
        return (dot_nt(weights.astype(BF), high) + dot_nt(weights.astype(BF), low))[0:1, :]

    def put_small(row, line):
        small[row : row + 1, :] = line[:, : cfg.half]
        small[row + 1 : row + 2, : width - cfg.half] = line[:, cfg.half :]

    def norm_two_back():
        pair_grad.wait()

        def grad_at(block):
            return grad_acc[block, :] + grad_in[block, :].astype(F32)

        inv = inverse_rms(lambda block: middle[block, :], seq)
        inner = (
            column_sum(
                lambda block: grad_at(block) * gain_at(1, block, seq) * middle[block, :], seq
            )
            * inv
            * (1.0 / width)
        )

        def back_rows(step, carry):
            block = rows_at(step)
            grad = grad_at(block)
            unit = middle[block, :] * inv
            masked = jnp.where(row_valid, whole(cot_raw, block).astype(F32), 0.0)
            total = masked + inv * (grad * gain_at(1, block, seq) - unit * inner)
            trans[block, :] = grad * unit
            grad_acc[block, :] = total
            grad_branch[block, :] = total.astype(BF)
            return carry

        lax.fori_loop(0, steps, back_rows, 0)
        build_left(grad_acc, 3)
        left_copy(1).start()
        mask = lane_mask((8, seq), 1)
        put_small(2, lane_sums(mask, trans[:width, :]))

    def attention_back():
        grad_att = dot(wo[core], grad_branch[...]).astype(BF)
        flip = (
            lax.broadcasted_iota(jnp.int32, (seq, seq), 0)
            + lax.broadcasted_iota(jnp.int32, (seq, seq), 1)
            == seq - 1
        ).astype(BF)
        for head in range(heads):
            part = slice(head * DKV, (head + 1) * DKV)
            grad_mixed = grad_att[part, :]
            prob = probs[head]
            grad_probs = dot_tn(qkv[2, part, :], grad_mixed)
            inner = jnp.sum(prob * grad_probs, axis=0, keepdims=True)
            grad_scores = (prob * (grad_probs - inner)).astype(BF)
            grad_qkv[0, part, :] = dot(qkv[1, part, :], grad_scores).astype(BF)
            grad_qkv[1, part, :] = dot_nt(qkv[0, part, :], grad_scores).astype(BF)
            grad_qkv[2, part, :] = dot_nt(grad_mixed, prob.astype(BF)).astype(BF)
            flipped = jnp.concatenate(
                [dot(grad_scores, flip), jnp.zeros((seq, seq), F32)], axis=1
            )
            skewed = pltpu.roll(flipped, 0, 1, stride=1, stride_axis=0)
            small[4 + head : 5 + head, : 2 * seq] = jnp.sum(skewed, axis=0, keepdims=True)
        joined = jnp.concatenate(
            [grad_qkv[...].reshape(3 * hw, seq), attended[core]], axis=0
        ).astype(F32)
        for index in range(cfg.chunks - cfg.ff_total):
            right_own[RING + index] = jnp.transpose(
                joined[index * CW : (index + 1) * CW, :]
            ).astype(BF)
            right_copy(index).start()

    def norm_one_sums():
        for block in blocks_of(width, 128):
            back_send[block, :] = sum(
                dot_tn(wqkv[part, :, block], grad_qkv[part, :, other_lanes]) for part in range(3)
            ).astype(BF)
        pair_back.start()
        for block in blocks_of(width, 128):
            input_grad[block, :] = sum(
                dot_tn(wqkv[part, :, block], grad_qkv[part, :, own_lanes]) for part in range(3)
            )

    def small_copy(k):
        target = sibling if k == cfg.bits else (peer[k], core)
        return send(
            small, small_in.at[k], small_send_sem.at[k], small_recv_sem.at[k], target
        )

    def finish_rows():
        pair_part.wait()
        pair_back.wait()

        def x_own(block):
            return hid[core, block, :].astype(F32)

        def grad_at(block):
            return input_grad[block, :] + back_in[block, :].astype(F32)

        inv = inverse_rms(x_own, rows)
        inner = (
            column_sum(lambda block: grad_at(block) * gain_at(0, block, rows) * x_own(block), rows)
            * inv
            * (1.0 / width)
        )

        def last_rows(step, carry):
            block = rows_at(step)
            grad = grad_at(block)
            unit = x_own(block) * inv
            input_grad[block, :] = grad_acc[block, own_lanes] + inv * (
                grad * gain_at(0, block, rows) - unit * inner
            )
            layer_out[block, :] = (
                middle[block, own_lanes]
                + out_acc[block, own_lanes]
                + part_in[block, :].astype(F32)
            )
            trans[block, :rows] = grad * unit
            return carry

        lax.fori_loop(0, steps, last_rows, 0)
        put_small(0, lane_sums(jnp.ones((8, rows), F32), trans[:width, :rows]))
        small_copy(0).start()

    def small_stage(k):
        small_copy(k).wait()
        if k == cfg.bits:
            row = lax.broadcasted_iota(jnp.int32, small.shape, 0)
            small_out[...] = small[...] + jnp.where(row < 4, small_in[k], 0.0)
        else:
            small[...] = small[...] + small_in[k]
            small_copy(k + 1).start()

    def slot_of(k, spot):
        return lax.rem(spot, cfg.gaps[k] + 1)

    def stage_copy(k, chunk, spot, target):
        slot = slot_of(k, spot)
        return send(
            stage_send[k].at[slot],
            stage_in[k].at[chunk],
            stage_send_sem.at[k, slot],
            stage_recv_sem.at[k, chunk],
            (target, core),
        )

    def stage_target(k, chunk):
        return pick(chunk, k + 1, peer)

    def form(chunk, position):
        slot = slot_of(0, position)
        tail_part = lax.div(chunk, cfg.ff_total)
        which = (1 - tail_part) * lax.div(lax.rem(chunk, 3) + 1, 2)
        block = block_of(chunk)
        spot = right_slot(chunk)
        second_bit = pick(chunk, 1, bit)
        weights = [pick(chunk, level, (1, 2, 4)) for level in range(3)]
        descending = lookup([int(axes[1] > axes[2]) for axes in AXES], block)
        near_weights = 1 + descending, 2 - descending
        begin = weights[0] * pick(chunk, 0, bit)

        @pl.when(chunk == cfg.ff_total)
        def _():
            left_pass(0)
            left_share(0).wait()

        @pl.when(chunk == cfg.chunks - 1)
        def _():
            left_pass(1)
            left_share(1).wait()

        for index in range(cfg.chunks - cfg.ff_total):

            @pl.when(chunk == cfg.ff_total + index)
            def _(index=index):
                right_copy(index).wait()

        parts = [(second, third) for second in (1 - second_bit, second_bit) for third in range(2)]

        def product(own, near, index):
            left = [
                jnp.concatenate(
                    [left_own[own, begin + weights[1] * s + weights[2] * t] for s, t in parts], axis=0
                ),
                jnp.concatenate(
                    [
                        left_in[near, index, near_weights[0] * s + near_weights[1] * t]
                        for s, t in parts
                    ],
                    axis=0,
                ),
            ]
            return dot(
                jnp.concatenate(left, axis=1),
                jnp.concatenate([right_own[spot], right_in[spot]], axis=0),
            )

        def fill(sums):
            stage_send[0][slot] = sums[: cfg.quarter, :].astype(BF)
            stage_copy(0, chunk, position, stage_target(0, chunk)).start()
            stage_own[0][slot] = sums[cfg.quarter :, :]

        own = 2 * tail_part + which
        near = lookup(
            [cfg.near.index(axes[0]) for axes in AXES[: cfg.ff_chunks]] + [len(cfg.near)], block
        )

        @pl.when(chunk < cfg.chunks - 1)
        def _():
            fill(product(own, near, which))

        @pl.when(chunk == cfg.chunks - 1)
        def _():
            split = lax.broadcasted_iota(jnp.int32, (2 * cfg.quarter, CW), 1) < CW - hw
            fill(jnp.where(split, *(product(2 + index, len(cfg.near), index) for index in range(2))))

    def halve(k, chunk, position):
        stage_copy(k - 1, chunk, position, stage_target(k - 1, chunk)).wait()
        old = slot_of(k - 1, position)
        if k == stages:
            result = stage_own[k - 1][old] + stage_in[k - 1][chunk].astype(F32)

            @pl.when(chunk < cfg.ff_total)
            def _():
                columns = pl.ds(pl.multiple_of(lax.div(chunk, 3) * CW, CW), CW)
                ff_out[lax.rem(chunk, 3), :, columns] = result[: cfg.shard, :]

            @pl.when(chunk >= cfg.ff_total)
            def _():
                att_final[lax.rem(chunk, cfg.ff_total)] = result

            return
        half = cfg.stage_rows[k]
        mine = pick(chunk, k + 1, bit)

        def total(which):
            part = pl.ds(pl.multiple_of(which * half, 16), half)
            return stage_own[k - 1][old, part, :] + stage_in[k - 1][chunk, part, :].astype(F32)

        slot = slot_of(k, position)
        stage_send[k][slot] = total(1 - mine).astype(BF)
        stage_copy(k, chunk, position, stage_target(k, chunk)).start()
        stage_own[k][slot] = total(mine)

    last_ff = OWN_TICKS[-1]
    pieces = [exchange_sums, norm_two_back, attention_back, norm_one_sums, finish_rows]
    pieces = [(last_ff + index, piece) for index, piece in enumerate(pieces)]
    for k in range(cfg.bits + 1):
        pieces.append((pieces[-1][0] + SMALL_GAP, functools.partial(small_stage, k)))
    ticks = max(LAG + cfg.chunks + cfg.late[stages], pieces[-1][0] + 1)

    def tick(t, carry):
        for ticks_of, forward in ((OWN_TICKS, forward_own), (NEAR_TICKS, forward_near)):
            now = sum(jnp.where(t == when, 1, 0) for when in ticks_of)
            past = sum(jnp.where(t > when, 1, 0) for when in ticks_of)

            @pl.when(now > 0)
            def _(forward=forward, past=past):
                forward(past)

        @pl.when(t == NEAR_TICKS[0] - 1)
        def _():
            for near in range(len(cfg.near)):
                adopt(near, 0)

        for k in range(stages, 0, -1):
            spot = t - LAG - cfg.late[k]

            @pl.when(jnp.logical_and(spot >= 0, spot < cfg.chunks))
            def _(k=k, spot=spot):
                halve(k, lookup(cfg.order, spot), spot)

        new = t - LAG

        @pl.when(jnp.logical_and(new >= 0, new < cfg.chunks))
        def _():
            form(lookup(cfg.order, new), new)

        for when, piece in pieces:

            @pl.when(t == when)
            def _(piece=piece):
                piece()

        return carry

    lax.fori_loop(0, ticks, tick, 0)

    flat = jnp.concatenate([att_final[index] for index in range(cfg.chunks - cfg.ff_total)], axis=1)
    for part, ref in enumerate((query_out, key_out, value_out)):
        ref[...] = flat[: cfg.shard, part * hw : (part + 1) * hw]
    output_out[...] = jnp.transpose(flat[:, 3 * hw :])[:, : cfg.shard]


def finish_kernel(
    cfg,
    layer_in,
    grad_in,
    query_in,
    key_in,
    value_in,
    output_in,
    ff_in,
    small,
    bucket_ids,
    layer_out,
    grad_out,
    gain_one,
    query_out,
    key_out,
    value_out,
    output_out,
    bias_out,
    gain_two,
    gate_out,
    up_out,
    down_out,
    *rest,
):
    pairs = [
        (ff_in.at[0], down_out),
        (ff_in.at[1], gate_out),
        (ff_in.at[2], up_out),
        (layer_in, layer_out),
        (grad_in, grad_out),
        (query_in, query_out),
        (key_in, key_out),
        (value_in, value_out),
        (output_in, output_out),
    ]
    buffers, (load_sem, store_sem) = rest[:-2], rest[-2:]
    loads, stores = [], []
    for index, ((src, dst), buffer) in enumerate(zip(pairs, buffers)):
        loads.append(pltpu.make_async_copy(src, buffer, load_sem.at[index]))
        stores.append(pltpu.make_async_copy(buffer, dst, store_sem.at[index]))
    for load in loads:
        load.start()
    for load, store in zip(loads, stores):
        load.wait()
        store.start()
    for row, gain in ((0, gain_one), (2, gain_two)):
        line = jnp.concatenate([small[row : row + 1, :], small[row + 1 : row + 2, :]], axis=1)
        gain[...] = line[:, : cfg.width].reshape(cfg.width)
    offsets = bucket_ids.shape[0]
    bucket = lax.broadcasted_iota(jnp.int32, (cfg.buckets, offsets), 0)
    onehot = (bucket_ids[...].reshape(1, offsets) == bucket).astype(F32)
    sums = lax.dot_general(
        small[:, :offsets],
        onehot,
        (((1,), (1,)), ((), ())),
        precision=lax.Precision.HIGHEST,
        preferred_element_type=F32,
    )
    bias_out[...] = sums[4 : 4 + cfg.heads, :]
    for store in stores:
        store.wait()


def shards(
    mesh,
    hidden_in,
    attention_gain,
    query_weight,
    key_weight,
    value_weight,
    output_weight,
    position_bias,
    feedforward_gain,
    gate_weight,
    up_weight,
    down_weight,
    cotangent,
    item_lengths,
    item_group,
    bucket_ids,
):
    rows, width = hidden_in.shape
    hw = query_weight.shape[1]
    hidden = gate_weight.shape[1]
    buckets = position_bias.shape[0]
    cfg = Sizes(mesh.shape["dp"], rows, width, hw, hidden, buckets)
    seq, stages, shard = cfg.seq, cfg.stages, cfg.shard
    any_spec = pl.BlockSpec(memory_space=pl.ANY)
    vmem = pl.BlockSpec(memory_space=pltpu.VMEM)
    smem = pl.BlockSpec(memory_space=pltpu.SMEM)
    small_shape = (8, cfg.half)
    scratch = [
        pltpu.VMEM((2, width, rows), BF),
        pltpu.VMEM((2, width, rows), BF),
        pltpu.VMEM((seq, width), BF),
        pltpu.VMEM((2, width, 128), F32),
        pltpu.VMEM((3, hw, width), BF),
        pltpu.VMEM((2, hw, width), BF),
        pltpu.VMEM((width, 2 * hw), BF),
        pltpu.VMEM((2, width, CW), BF),
        pltpu.VMEM((2, width, CW), BF),
        pltpu.VMEM((2, width, CW), BF),
        pltpu.VMEM((width, seq), BF),
        pltpu.VMEM((seq, width), BF),
        pltpu.VMEM((width, seq), F32),
        pltpu.VMEM((3, hw, seq), BF),
        pltpu.VMEM((cfg.heads, seq, seq), F32),
        pltpu.VMEM((2, hw, seq), BF),
        pltpu.VMEM((cfg.tall, seq), F32),
        pltpu.VMEM((4, 8, cfg.eighth, seq), BF),
        pltpu.VMEM((len(cfg.near) + 1, 2, 4, cfg.eighth, seq), BF),
        pltpu.VMEM((len(cfg.near), 2, seq, width), BF),
        pltpu.VMEM((RING + cfg.chunks - cfg.ff_total, seq, CW), BF),
        pltpu.VMEM((RING + cfg.chunks - cfg.ff_total, seq, CW), BF),
        pltpu.VMEM((width, seq), F32),
        pltpu.VMEM((cfg.tall, seq), F32),
        pltpu.VMEM((width, seq), BF),
        pltpu.VMEM((width, rows), BF),
        pltpu.VMEM((width, rows), BF),
        pltpu.VMEM((width, rows), BF),
        pltpu.VMEM((width, rows), BF),
        pltpu.VMEM((width, seq), BF),
        pltpu.VMEM((3, hw, seq), BF),
        pltpu.VMEM(small_shape, F32),
        pltpu.VMEM((cfg.bits + 1,) + small_shape, F32),
        pltpu.VMEM((cfg.chunks - cfg.ff_total, cfg.shard_pad, CW), F32),
        pltpu.VMEM((1, 2 * seq), jnp.int32),
    ]
    for dtype in (F32, BF):
        scratch += [
            pltpu.VMEM((gap + 1, size, CW), dtype) for gap, size in zip(cfg.gaps, cfg.stage_rows)
        ]
    scratch += [pltpu.VMEM((cfg.chunks, size, CW), BF) for size in cfg.stage_rows]
    dma = pltpu.SemaphoreType.DMA
    scratch += [
        dma((6,)),
        dma((2, 3)),
        dma((8,)),
        dma((8,)),
        dma((2,)),
        dma((2,)),
        dma((2,)),
        dma((2,)),
        dma((3, 2)),
        dma((3, 2)),
        dma((3, 2)),
        dma((3, 2)),
        dma((cfg.chunks - cfg.ff_total,)),
        dma((cfg.chunks - cfg.ff_total,)),
        dma((stages, max(cfg.gaps) + 1)),
        dma((stages, cfg.chunks)),
        dma((cfg.bits + 1,)),
        dma((cfg.bits + 1,)),
    ]
    (
        layer_out,
        input_grad,
        small_sum,
        ff_sum,
        query_sum,
        key_sum,
        value_sum,
        output_sum,
    ) = pl.pallas_call(
        functools.partial(layer_kernel, cfg),
        out_shape=[
            jax.ShapeDtypeStruct((width, rows), F32),
            jax.ShapeDtypeStruct((width, rows), F32),
            jax.ShapeDtypeStruct(small_shape, F32),
            jax.ShapeDtypeStruct((3, shard, hidden), F32),
            jax.ShapeDtypeStruct((shard, hw), F32),
            jax.ShapeDtypeStruct((shard, hw), F32),
            jax.ShapeDtypeStruct((shard, hw), F32),
            jax.ShapeDtypeStruct((hw, shard), F32),
        ],
        in_specs=[
            any_spec,
            vmem,
            any_spec,
            any_spec,
            any_spec,
            any_spec,
            smem,
            vmem,
            any_spec,
            any_spec,
            any_spec,
            any_spec,
            smem,
            smem,
            vmem,
        ],
        out_specs=[vmem] * 8,
        scratch_shapes=scratch,
        compiler_params=pltpu.CompilerParams(
            collective_id=0, has_side_effects=True, vmem_limit_bytes=62 * 1024 * 1024
        ),
        cost_estimate=pl.CostEstimate(
            flops=14 * 10**9, bytes_accessed=24 * 10**6, transcendentals=10**6
        ),
    )(
        hidden_in.T,
        attention_gain,
        query_weight.T,
        key_weight.T,
        value_weight.T,
        output_weight,
        position_bias.T,
        feedforward_gain,
        gate_weight,
        up_weight,
        down_weight.T,
        cotangent.T,
        item_lengths,
        item_group,
        bucket_ids,
    )
    def like(array):
        return jax.ShapeDtypeStruct(array.shape, array.dtype)

    one_ff = jax.ShapeDtypeStruct((shard, hidden), F32)
    outs = pl.pallas_call(
        functools.partial(finish_kernel, cfg),
        out_shape=[
            like(layer_out),
            like(input_grad),
            like(attention_gain),
            like(query_sum),
            like(key_sum),
            like(value_sum),
            like(output_sum),
            jax.ShapeDtypeStruct((cfg.heads, buckets), F32),
            like(feedforward_gain),
            one_ff,
            one_ff,
            one_ff,
        ],
        in_specs=[any_spec] * 7 + [vmem, vmem],
        out_specs=[any_spec] * 2 + [vmem] + [any_spec] * 4 + [vmem] * 2 + [any_spec] * 3,
        scratch_shapes=[
            pltpu.VMEM(array.shape, F32)
            for array in (one_ff,) * 3
            + (layer_out, input_grad, query_sum, key_sum, value_sum, output_sum)
        ]
        + [dma((9,)), dma((9,))],
        compiler_params=pltpu.CompilerParams(vmem_limit_bytes=62 * 1024 * 1024),
    )(
        layer_out,
        input_grad,
        query_sum,
        key_sum,
        value_sum,
        output_sum,
        ff_sum,
        small_sum,
        bucket_ids,
    )
    layer_out, input_grad, gain_one, query, key, value, output, bias, gain_two, gate, up, down = outs
    return (
        layer_out.T,
        input_grad.T,
        gain_one,
        query,
        key,
        value,
        output,
        bias.T,
        gain_two,
        gate,
        up,
        down.T,
    )


def solution(mesh):
    in_specs = (
        P(("dp", "mp"), None),
        P(),
        P(None, "mp"),
        P(None, "mp"),
        P(None, "mp"),
        P("mp", None),
        P(None, "mp"),
        P(),
        P(None, "mp"),
        P(None, "mp"),
        P("mp", None),
        P(("dp", "mp"), None),
        P(),
        P(),
        P(),
    )
    out_specs = (
        P(("dp", "mp"), None),
        P(("dp", "mp"), None),
        P(),
        P("dp", "mp"),
        P("dp", "mp"),
        P("dp", "mp"),
        P("mp", "dp"),
        P(None, "mp"),
        P(),
        P("dp", "mp"),
        P("dp", "mp"),
        P("mp", "dp"),
    )
    return jax.shard_map(
        functools.partial(shards, mesh),
        mesh=mesh,
        in_specs=in_specs,
        out_specs=out_specs,
        check_vma=False,
    )
```

```python
import functools
import math

import jax
import jax.numpy as jnp
from jax import lax
from jax.experimental import pallas as pl
from jax.experimental.pallas import tpu as pltpu
from jax.sharding import PartitionSpec as P

DKV = 64
CW = 256
EPS = 1e-06
AXES = ((1, 0, 2), (1, 2, 0), (2, 1, 0), (2, 1, 0), (2, 0, 1), (2, 1, 0), (1, 0, 2), (2, 1, 0))
TOGETHER = (2, 3, 2)
OWN_TICKS = (0, 1, 5, 8, 10, 11, 13)
NEAR_TICKS = (2, 3, 6, 9, 10, 12, 14)
RING_BLOCKS = 5
LAG = 2
GAPS = (4, 4, 4)
RING = 3 * RING_BLOCKS
SMALL_GAP = 3
STEP = 64
MROWS = 368
BF = jnp.bfloat16
F32 = jnp.float32
MESH = pl.DeviceIdType.MESH
GELU_C = math.sqrt(2.0 / math.pi)


def dot(left, right):
    return lax.dot_general(left, right, (((1,), (0,)), ((), ())), preferred_element_type=F32)


def dot_nt(left, right):
    return lax.dot_general(left, right, (((1,), (1,)), ((), ())), preferred_element_type=F32)


def dot_tn(left, right):
    return lax.dot_general(left, right, (((0,), (0,)), ((), ())), preferred_element_type=F32)


def blocks_of(extent, step):
    return [slice(begin, min(begin + step, extent)) for begin in range(0, extent, step)]


def fold(block):
    return jnp.sum(block.reshape(block.shape[0] // 8, 8, block.shape[1]), axis=0)


def lookup(table, index):
    bits = max(table).bit_length()
    if bits == 0:
        return 0 * index
    per = 30 // bits
    words = [
        sum(value << (bits * place) for place, value in enumerate(table[begin : begin + per]))
        for begin in range(0, len(table), per)
    ]
    word = jnp.int32(words[0])
    for place in range(1, len(words)):
        word = jnp.where(index >= place * per, words[place], word)
    shifted = lax.shift_right_logical(word, bits * lax.rem(index, per))
    return lax.rem(shifted, 1 << bits)


class Sizes:
    def __init__(self, dp, local_rows, width, head_width, hidden, buckets):
        self.dp = dp
        self.bits = dp.bit_length() - 1
        self.local_rows = local_rows
        self.seq = 2 * local_rows
        self.width = width
        self.head_width = head_width
        self.heads = head_width // DKV
        self.hidden = hidden
        self.buckets = buckets
        self.shard = width // dp
        self.shard_pad = -(-self.shard // 16) * 16
        self.quarter = self.shard_pad * dp // 4
        self.ff_chunks = hidden // CW
        self.ff_total = 3 * self.ff_chunks
        self.chunks = self.ff_total + 4 * head_width // CW
        self.stage_rows = [self.quarter >> k for k in range(self.bits - 1)]
        self.stages = len(self.stage_rows)
        self.half = -(-width // 256) * 128
        self.tall = width + self.shard_pad
        self.eighth = self.quarter // 2
        self.gaps = [GAPS[min(k, 2)] for k in range(self.stages)]
        self.late = [sum(self.gaps[:k]) for k in range(self.stages + 1)]
        self.order = []
        begin = 0
        for count in TOGETHER:
            self.order += [3 * (begin + f) + kind for kind in range(3) for f in range(count)]
            begin += count
        self.order += range(self.ff_total, self.chunks)
        self.near = sorted({axes[0] for axes in AXES[: self.ff_chunks]})
        self.first_use = [[axes[0] for axes in AXES].index(axis) for axis in self.near]


def layer_kernel(
    cfg,
    hidden_hbm,
    gain_one,
    wq_hbm,
    wk_hbm,
    wv_hbm,
    wo_hbm,
    position_bias,
    gain_two,
    wg_hbm,
    wu_hbm,
    wd_hbm,
    cot_hbm,
    lengths,
    groups,
    bucket_ids,
    layer_hbm,
    input_hbm,
    small_out,
    ff_hbm,
    query_out,
    key_out,
    value_out,
    output_out,
    hid,
    cot_raw,
    cot,
    gains,
    wqkv,
    wo,
    wo_t,
    wg,
    wu,
    wd,
    normed_one,
    normed_two,
    middle,
    qkv,
    probs,
    attended,
    trans,
    left_own,
    left_in,
    near_rows,
    right_own,
    right_in,
    out_acc,
    grad_acc,
    grad_in,
    part_send,
    part_in,
    back_send,
    back_in,
    grad_branch,
    grad_qkv,
    small,
    small_in,
    att_final,
    ids_row,
    layer_out,
    input_grad,
    ff_out,
    *rest,
):
    grad_send = normed_one
    stages = cfg.stages
    stage_own = rest[:stages]
    stage_send = rest[stages : 2 * stages]
    stage_in = rest[2 * stages : 3 * stages]
    (
        load_sem,
        weight_sem,
        pair_send_sem,
        pair_recv_sem,
        left_send_sem,
        left_recv_sem,
        share_send_sem,
        share_recv_sem,
        near_send_sem,
        near_recv_sem,
        pass_send_sem,
        pass_recv_sem,
        right_send_sem,
        right_recv_sem,
        stage_send_sem,
        stage_recv_sem,
        small_send_sem,
        small_recv_sem,
        out_sem,
    ) = rest[3 * stages :]

    seq, rows, width, hw, heads = cfg.seq, cfg.local_rows, cfg.width, cfg.head_width, cfg.heads
    me = lax.axis_index("dp")
    core = lax.axis_index("mp")
    bit = [lax.rem(lax.div(me, 1 << k), 2) for k in range(cfg.bits)]
    peer = [me + (1 - 2 * bit[k]) * (1 << k) for k in range(cfg.bits)]
    sibling = (me, 1 - core)
    own_lanes = pl.ds(pl.multiple_of(core * rows, rows), rows)
    own_rows = own_lanes
    other_lanes = pl.ds(pl.multiple_of((1 - core) * rows, rows), rows)

    def send(src, dst, send_sem, recv_sem, target):
        return pltpu.make_async_remote_copy(
            src_ref=src,
            dst_ref=dst,
            send_sem=send_sem,
            recv_sem=recv_sem,
            device_id=target,
            device_id_type=MESH,
        )

    loads = [
        pltpu.make_async_copy(hidden_hbm, hid.at[core], load_sem.at[0]),
        pltpu.make_async_copy(cot_hbm, cot_raw.at[core], load_sem.at[1]),
        pltpu.make_async_copy(wq_hbm, wqkv.at[0], load_sem.at[2]),
        pltpu.make_async_copy(wk_hbm, wqkv.at[1], load_sem.at[3]),
        pltpu.make_async_copy(wv_hbm, wqkv.at[2], load_sem.at[4]),
        pltpu.make_async_copy(wo_hbm, wo.at[core], load_sem.at[5]),
    ]
    for load in loads:
        load.start()

    def weight_loads(chunk, slot):
        columns = pl.ds(pl.multiple_of(chunk * CW, CW), CW)
        return [
            pltpu.make_async_copy(src.at[:, columns], dst.at[slot], weight_sem.at[slot, index])
            for index, (src, dst) in enumerate(((wg_hbm, wg), (wu_hbm, wu), (wd_hbm, wd)))
        ]

    barrier = pltpu.get_barrier_semaphore()
    pl.semaphore_signal(barrier, inc=1, device_id=sibling, device_id_type=MESH)
    for k in range(cfg.bits):
        pl.semaphore_signal(barrier, inc=1, device_id=(peer[k], core), device_id_type=MESH)
    for index, gain in enumerate((gain_one, gain_two)):
        line = gain[...].reshape(1, width)
        for block in blocks_of(width, 128):
            size = block.stop - block.start
            gains[index, block, :] = jnp.transpose(
                jnp.broadcast_to(line[:, block], (128, size))
            )
    group_len = jnp.int32(0)
    for item in range(lengths.shape[0]):
        group_len = group_len + jnp.where(groups[item] == me, lengths[item], 0)

    loads[1].wait()
    lane_valid = lax.broadcasted_iota(jnp.int32, (1, rows), 1) + core * rows < group_len
    for block in blocks_of(width, 128):
        part = jnp.where(lane_valid, cot_raw[core, block, :].astype(F32), 0.0)
        cot[own_rows, block] = jnp.transpose(part).astype(BF)
    pl.semaphore_wait(barrier, cfg.bits + 1)

    pair_hid = send(
        hidden_hbm, hid.at[core], pair_send_sem.at[0], pair_recv_sem.at[0], sibling
    )
    pair_cot = send(
        cot_hbm, cot_raw.at[core], pair_send_sem.at[1], pair_recv_sem.at[1], sibling
    )
    pair_wo = send(wo_hbm, wo.at[core], pair_send_sem.at[2], pair_recv_sem.at[2], sibling)
    pair_rows = send(
        cot.at[own_rows], cot.at[own_rows], pair_send_sem.at[7], pair_recv_sem.at[7], sibling
    )

    natural = (cot, normed_two)

    def near_copy(near, which):
        return send(
            natural[which].at[own_rows],
            near_rows.at[near, which, own_rows],
            near_send_sem.at[near, which],
            near_recv_sem.at[near, which],
            (peer[cfg.near[near]], core),
        )

    def near_pass(near, which):
        return send(
            near_rows.at[near, which, own_rows],
            near_rows.at[near, which, own_rows],
            pass_send_sem.at[near, which],
            pass_recv_sem.at[near, which],
            sibling,
        )

    pair_hid.start()
    pair_cot.start()
    pair_wo.start()
    pair_rows.start()
    for near in range(len(cfg.near)):
        near_copy(near, 0).start()
    pair_att = send(
        attended.at[core], attended.at[core], pair_send_sem.at[3], pair_recv_sem.at[3], sibling
    )
    pair_grad = send(grad_send, grad_in, pair_send_sem.at[4], pair_recv_sem.at[4], sibling)
    pair_part = send(part_send, part_in, pair_send_sem.at[5], pair_recv_sem.at[5], sibling)
    pair_back = send(back_send, back_in, pair_send_sem.at[6], pair_recv_sem.at[6], sibling)

    for slot in range(2):
        for load in weight_loads(slot, slot):
            load.start()

    def place_of(index):
        place = 0
        for k in range(3, cfg.bits):
            place = 2 * place + ((index >> k) & 1)
        return slice(place * cfg.shard_pad, (place + 1) * cfg.shard_pad)

    def shard_of(source, index):
        return source[index * cfg.shard : index * cfg.shard + cfg.shard_pad, :].astype(BF)

    def build_left(source, which):
        for index in range(cfg.dp):
            left_own[which, index & 7, place_of(index), :] = shard_of(source, index)

    def adopt(near, which):
        near_copy(near, which).wait()
        near_pass(near, which).start()
        near_pass(near, which).wait()
        axis = cfg.near[near]
        high, low = (k for k in (2, 1, 0) if k != axis)
        for block in blocks_of(width, 128):
            trans[block, :] = jnp.transpose(near_rows[near, which, :, block].astype(F32))
        for value in range(2):

            @pl.when(bit[axis] == value)
            def _(value=value):
                for index in range(cfg.dp):
                    if (index >> axis) & 1 == value:
                        place = 2 * ((index >> high) & 1) + ((index >> low) & 1)
                        left_in[near, which, place, place_of(index), :] = shard_of(trans, index)

    def left_copy(which):
        return send(
            left_own.at[2 + which, pl.ds(4 * (1 - bit[2]) + 2 * core, 2)],
            left_in.at[len(cfg.near), which, pl.ds(2 * core, 2)],
            left_send_sem.at[which],
            left_recv_sem.at[which],
            (peer[2], core),
        )

    def left_share(which):
        return send(
            left_in.at[len(cfg.near), which, pl.ds(2 * core, 2)],
            left_in.at[len(cfg.near), which, pl.ds(2 * core, 2)],
            share_send_sem.at[which],
            share_recv_sem.at[which],
            sibling,
        )

    def left_pass(which):
        left_copy(which).wait()
        left_share(which).start()

    def block_of(chunk):
        return lax.div(chunk, 3)

    def pick(chunk, level, values):
        if level > 2:
            return values[level]
        k = lookup([axes[level] for axes in AXES], block_of(chunk))
        parts = (lax.div((1 - k) * (2 - k), 2), k * (2 - k), lax.div(k * (k - 1), 2))
        return sum(part * value for part, value in zip(parts, values))

    def right_slot(chunk):
        tail_part = lax.div(chunk, cfg.ff_total)
        return (1 - tail_part) * lax.rem(chunk, RING) + tail_part * (RING + chunk - cfg.ff_total)

    def right_copy(index):
        return send(
            right_own.at[RING + index],
            right_in.at[RING + index],
            right_send_sem.at[index],
            right_recv_sem.at[index],
            (peer[2], core),
        )

    for scratch in (trans, grad_acc):
        scratch[width:, :] = jnp.zeros((cfg.tall - width, seq), F32)

    step_rows = STEP
    steps = width // step_rows

    def rows_at(step):
        return pl.ds(pl.multiple_of(step * step_rows, step_rows), step_rows)

    def whole(ref, block):
        return jnp.concatenate([ref[0, block, :], ref[1, block, :]], axis=1)

    def gain_at(index, block, lanes):
        part = gains[index, block, :]
        return jnp.concatenate([part] * (lanes // 128), axis=1)

    def column_sum(term, lanes):
        zero = jnp.zeros((8, lanes), F32)
        total = lax.fori_loop(0, steps, lambda i, acc: acc + fold(term(rows_at(i))), zero)
        return jnp.sum(total, axis=0, keepdims=True)

    def inverse_rms(term, lanes):
        def square(block):
            x = term(block)
            return x * x

        return lax.rsqrt(column_sum(square, lanes) * (1.0 / width) + EPS)

    loads[0].wait()
    pair_hid.wait()

    def x_at(block):
        return whole(hid, block).astype(F32)

    inv_one = inverse_rms(x_at, seq)

    def norm_one_rows(step, carry):
        block = rows_at(step)
        normed = x_at(block) * inv_one * gain_at(0, block, seq)
        trans[block, :] = normed
        normed_one[block, :] = normed.astype(BF)
        return carry

    lax.fori_loop(0, steps, norm_one_rows, 0)

    for part in range(3):
        loads[2 + part].wait()
        qkv[part] = dot(wqkv[part], normed_one[...]).astype(BF)

    key_valid = lax.broadcasted_iota(jnp.int32, (seq, seq), 0) < group_len
    ids_row[...] = jnp.full(ids_row.shape, -1, jnp.int32)
    ids_row[:, : bucket_ids.shape[0]] = bucket_ids[...].reshape(1, -1)
    ids = ids_row[...]
    for head in range(heads):
        part = slice(head * DKV, (head + 1) * DKV)
        by_offset = jnp.zeros(ids.shape, F32)
        for bucket in range(cfg.buckets):
            by_offset = jnp.where(ids == bucket, position_bias[head, bucket], by_offset)
        bias = pltpu.roll(
            jnp.broadcast_to(by_offset, (seq, 2 * seq)),
            seq + 1,
            1,
            stride=1,
            stride_axis=0,
        )[:, :seq]
        scores = dot_tn(qkv[1, part, :], qkv[0, part, :]) + jnp.transpose(bias)
        scores = jnp.where(key_valid, scores, -1e30)
        exps = jnp.exp(scores - jnp.max(scores, axis=0, keepdims=True))
        prob = exps / jnp.sum(exps, axis=0, keepdims=True)
        probs[head] = prob
        attended[core, part, :] = dot(qkv[2, part, :], prob.astype(BF)).astype(BF)
    pair_att.start()

    row_valid = lax.broadcasted_iota(jnp.int32, (step_rows, seq), 1) < group_len

    def build_argument_lefts():
        def first_rows(step, carry):
            block = rows_at(step)
            trans[block, :] = normed_one[block, :].astype(F32)
            return carry

        lax.fori_loop(0, steps, first_rows, 0)
        build_left(trans, 2)
        pair_cot.wait()

        def mask_rows(step, carry):
            block = rows_at(step)
            trans[block, :] = jnp.where(row_valid, whole(cot_raw, block).astype(F32), 0.0)
            return carry

        lax.fori_loop(0, steps, mask_rows, 0)
        build_left(trans, 0)

    loads[5].wait()
    pair_wo.wait()
    for block in blocks_of(width, 128):
        wo_t[block, :] = jnp.transpose(
            jnp.concatenate([wo[0, :, block], wo[1, :, block]], axis=0).astype(F32)
        ).astype(BF)
    pair_att.wait()
    both = attended[...].reshape(2 * hw, seq)
    for block in blocks_of(width, MROWS):
        middle[block, :] = x_at(block) + dot(wo_t[block, :], both)

    inv_two = inverse_rms(lambda block: middle[block, :], seq)

    def norm_two_rows(step, carry):
        block = rows_at(step)
        trans[block, :] = middle[block, :] * inv_two * gain_at(1, block, seq)
        out_acc[block, :] = jnp.zeros((step_rows, seq), F32)
        grad_acc[block, :] = jnp.zeros((step_rows, seq), F32)
        return carry

    lax.fori_loop(0, steps, norm_two_rows, 0)
    for block in blocks_of(width, 128):
        normed_two[:, block] = jnp.transpose(trans[block, :]).astype(BF)
    for near in range(len(cfg.near)):
        near_copy(near, 1).start()
    build_left(trans, 1)
    pair_rows.wait()
    small[...] = jnp.zeros_like(small)

    def activations(chunk, normed, grad_rows, target):
        slot = lax.rem(chunk, 2)
        first = lax.rem(3 * chunk, RING)
        gate = dot(normed, wg[slot])
        up = dot(normed, wu[slot])
        grad_hidden = dot(grad_rows, wd[slot])
        square = gate * gate
        tanh = jnp.tanh(GELU_C * (gate + 0.044715 * (square * gate)))
        half = 0.5 * (1.0 + tanh)
        gelu = gate * half
        slope = half + (0.5 * GELU_C) * gate * (1.0 - tanh * tanh) * (
            1.0 + (3 * 0.044715) * square
        )
        target[first] = (gelu * up).astype(BF)
        target[first + 1] = (grad_hidden * up * slope).astype(BF)
        target[first + 2] = (grad_hidden * gelu).astype(BF)

    def forward_own(chunk):
        slot = lax.rem(chunk, 2)
        first = lax.rem(3 * chunk, RING)
        for load in weight_loads(chunk, slot):
            load.wait()
        activations(chunk, normed_two[...], cot[...], right_own)
        hidden, grad_gate, grad_up = (right_own[first + kind] for kind in range(3))
        for block in blocks_of(width, MROWS):
            out_acc[block, :] += dot_nt(wd[slot, block, :], hidden)
            grad_acc[block, :] += dot_nt(wg[slot, block, :], grad_gate) + dot_nt(
                wu[slot, block, :], grad_up
            )

    def forward_near(chunk):
        slot = lax.rem(chunk, 2)
        for near, use in enumerate(cfg.first_use):

            @pl.when(chunk == use)
            def _(near=near):
                adopt(near, 1)

        near = lookup([cfg.near.index(axes[0]) for axes in AXES[: cfg.ff_chunks]], chunk)
        activations(chunk, near_rows[near, 1], near_rows[near, 0], right_in)

        @pl.when(chunk < cfg.ff_chunks - 2)
        def _():
            for load in weight_loads(chunk + 2, slot):
                load.start()

    def exchange_sums():
        left_copy(0).start()
        grad_send[...] = grad_acc[:width, :].astype(BF)
        pair_grad.start()
        part_send[...] = out_acc[:, other_lanes].astype(BF)
        pair_part.start()

    def lane_mask(shape, dimension):
        lane = lax.broadcasted_iota(jnp.int32, shape, dimension)
        return (lax.div(lane, rows) == core).astype(F32)

    def lane_sums(weights, source):
        high = source.astype(BF)
        low = (source - high.astype(F32)).astype(BF)
        return (dot_nt(weights.astype(BF), high) + dot_nt(weights.astype(BF), low))[0:1, :]

    def put_small(row, line):
        small[row : row + 1, :] = line[:, : cfg.half]
        small[row + 1 : row + 2, : width - cfg.half] = line[:, cfg.half :]

    def norm_two_back():
        pair_grad.wait()

        def grad_at(block):
            return grad_acc[block, :] + grad_in[block, :].astype(F32)

        inv = inverse_rms(lambda block: middle[block, :], seq)
        inner = (
            column_sum(
                lambda block: grad_at(block) * gain_at(1, block, seq) * middle[block, :], seq
            )
            * inv
            * (1.0 / width)
        )

        def back_rows(step, carry):
            block = rows_at(step)
            grad = grad_at(block)
            unit = middle[block, :] * inv
            masked = jnp.where(row_valid, whole(cot_raw, block).astype(F32), 0.0)
            total = masked + inv * (grad * gain_at(1, block, seq) - unit * inner)
            trans[block, :] = grad * unit
            grad_acc[block, :] = total
            grad_branch[block, :] = total.astype(BF)
            return carry

        lax.fori_loop(0, steps, back_rows, 0)
        build_left(grad_acc, 3)
        left_copy(1).start()
        mask = lane_mask((8, seq), 1)
        put_small(2, lane_sums(mask, trans[:width, :]))

    def attention_back():
        grad_att = dot(wo[core], grad_branch[...]).astype(BF)
        flip = (
            lax.broadcasted_iota(jnp.int32, (seq, seq), 0)
            + lax.broadcasted_iota(jnp.int32, (seq, seq), 1)
            == seq - 1
        ).astype(BF)
        for head in range(heads):
            part = slice(head * DKV, (head + 1) * DKV)
            grad_mixed = grad_att[part, :]
            prob = probs[head]
            grad_probs = dot_tn(qkv[2, part, :], grad_mixed)
            inner = jnp.sum(prob * grad_probs, axis=0, keepdims=True)
            grad_scores = (prob * (grad_probs - inner)).astype(BF)
            grad_qkv[0, part, :] = dot(qkv[1, part, :], grad_scores).astype(BF)
            grad_qkv[1, part, :] = dot_nt(qkv[0, part, :], grad_scores).astype(BF)
            grad_qkv[2, part, :] = dot_nt(grad_mixed, prob.astype(BF)).astype(BF)
            flipped = jnp.concatenate(
                [dot(grad_scores, flip), jnp.zeros((seq, seq), F32)], axis=1
            )
            skewed = pltpu.roll(flipped, 0, 1, stride=1, stride_axis=0)
            small[4 + head : 5 + head, : 2 * seq] = jnp.sum(skewed, axis=0, keepdims=True)
        joined = jnp.concatenate(
            [grad_qkv[...].reshape(3 * hw, seq), attended[core]], axis=0
        ).astype(F32)
        for index in range(cfg.chunks - cfg.ff_total):
            right_own[RING + index] = jnp.transpose(
                joined[index * CW : (index + 1) * CW, :]
            ).astype(BF)
            right_copy(index).start()

    def norm_one_sums():
        for block in blocks_of(width, 128):
            back_send[block, :] = sum(
                dot_tn(wqkv[part, :, block], grad_qkv[part, :, other_lanes]) for part in range(3)
            ).astype(BF)
        pair_back.start()
        for block in blocks_of(width, 128):
            input_grad[block, :] = sum(
                dot_tn(wqkv[part, :, block], grad_qkv[part, :, own_lanes]) for part in range(3)
            )

    row_stores = [
        pltpu.make_async_copy(src, dst, out_sem.at[cfg.ff_total + index])
        for index, (src, dst) in enumerate(((layer_out, layer_hbm), (input_grad, input_hbm)))
    ]

    def ff_store(chunk):
        columns = pl.ds(pl.multiple_of(lax.div(chunk, 3) * CW, CW), CW)
        kind = lax.rem(chunk, 3)
        return pltpu.make_async_copy(
            ff_out.at[kind, :, columns], ff_hbm.at[kind, :, columns], out_sem.at[chunk]
        )

    def small_copy(k):
        target = sibling if k == cfg.bits else (peer[k], core)
        return send(
            small, small_in.at[k], small_send_sem.at[k], small_recv_sem.at[k], target
        )

    def finish_rows():
        pair_part.wait()
        pair_back.wait()

        def x_own(block):
            return hid[core, block, :].astype(F32)

        def grad_at(block):
            return input_grad[block, :] + back_in[block, :].astype(F32)

        inv = inverse_rms(x_own, rows)
        inner = (
            column_sum(lambda block: grad_at(block) * gain_at(0, block, rows) * x_own(block), rows)
            * inv
            * (1.0 / width)
        )

        def last_rows(step, carry):
            block = rows_at(step)
            grad = grad_at(block)
            unit = x_own(block) * inv
            input_grad[block, :] = grad_acc[block, own_lanes] + inv * (
                grad * gain_at(0, block, rows) - unit * inner
            )
            layer_out[block, :] = (
                middle[block, own_lanes]
                + out_acc[block, own_lanes]
                + part_in[block, :].astype(F32)
            )
            trans[block, :rows] = grad * unit
            return carry

        lax.fori_loop(0, steps, last_rows, 0)
        put_small(0, lane_sums(jnp.ones((8, rows), F32), trans[:width, :rows]))
        small_copy(0).start()
        for store in row_stores:
            store.start()

    def small_stage(k):
        small_copy(k).wait()
        if k == cfg.bits:
            row = lax.broadcasted_iota(jnp.int32, small.shape, 0)
            small_out[...] = small[...] + jnp.where(row < 4, small_in[k], 0.0)
        else:
            small[...] = small[...] + small_in[k]
            small_copy(k + 1).start()

    def slot_of(k, spot):
        return lax.rem(spot, cfg.gaps[k] + 1)

    def stage_copy(k, chunk, spot, target):
        slot = slot_of(k, spot)
        return send(
            stage_send[k].at[slot],
            stage_in[k].at[chunk],
            stage_send_sem.at[k, slot],
            stage_recv_sem.at[k, chunk],
            (target, core),
        )

    def stage_target(k, chunk):
        return pick(chunk, k + 1, peer)

    def form(chunk, position):
        slot = slot_of(0, position)
        tail_part = lax.div(chunk, cfg.ff_total)
        which = (1 - tail_part) * lax.div(lax.rem(chunk, 3) + 1, 2)
        block = block_of(chunk)
        spot = right_slot(chunk)
        second_bit = pick(chunk, 1, bit)
        weights = [pick(chunk, level, (1, 2, 4)) for level in range(3)]
        descending = lookup([int(axes[1] > axes[2]) for axes in AXES], block)
        near_weights = 1 + descending, 2 - descending
        begin = weights[0] * pick(chunk, 0, bit)

        @pl.when(chunk == cfg.ff_total)
        def _():
            left_pass(0)
            left_share(0).wait()

        @pl.when(chunk == cfg.chunks - 1)
        def _():
            left_pass(1)
            left_share(1).wait()

        for index in range(cfg.chunks - cfg.ff_total):

            @pl.when(chunk == cfg.ff_total + index)
            def _(index=index):
                right_copy(index).wait()

        parts = [(second, third) for second in (1 - second_bit, second_bit) for third in range(2)]

        def product(own, near, index):
            left = [
                jnp.concatenate(
                    [left_own[own, begin + weights[1] * s + weights[2] * t] for s, t in parts], axis=0
                ),
                jnp.concatenate(
                    [
                        left_in[near, index, near_weights[0] * s + near_weights[1] * t]
                        for s, t in parts
                    ],
                    axis=0,
                ),
            ]
            return dot(
                jnp.concatenate(left, axis=1),
                jnp.concatenate([right_own[spot], right_in[spot]], axis=0),
            )

        def fill(sums):
            stage_send[0][slot] = sums[: cfg.quarter, :].astype(BF)
            stage_copy(0, chunk, position, stage_target(0, chunk)).start()
            stage_own[0][slot] = sums[cfg.quarter :, :]

        own = 2 * tail_part + which
        near = lookup(
            [cfg.near.index(axes[0]) for axes in AXES[: cfg.ff_chunks]] + [len(cfg.near)], block
        )

        @pl.when(chunk < cfg.chunks - 1)
        def _():
            fill(product(own, near, which))

        @pl.when(chunk == cfg.chunks - 1)
        def _():
            split = lax.broadcasted_iota(jnp.int32, (2 * cfg.quarter, CW), 1) < CW - hw
            fill(jnp.where(split, *(product(2 + index, len(cfg.near), index) for index in range(2))))

    def halve(k, chunk, position):
        stage_copy(k - 1, chunk, position, stage_target(k - 1, chunk)).wait()
        old = slot_of(k - 1, position)
        if k == stages:
            result = stage_own[k - 1][old] + stage_in[k - 1][chunk].astype(F32)

            @pl.when(chunk < cfg.ff_total)
            def _():
                columns = pl.ds(pl.multiple_of(lax.div(chunk, 3) * CW, CW), CW)
                ff_out[lax.rem(chunk, 3), :, columns] = result[: cfg.shard, :]
                ff_store(chunk).start()

            @pl.when(chunk >= cfg.ff_total)
            def _():
                att_final[lax.rem(chunk, cfg.ff_total)] = result

            return
        half = cfg.stage_rows[k]
        mine = pick(chunk, k + 1, bit)

        def total(which):
            part = pl.ds(pl.multiple_of(which * half, 16), half)
            return stage_own[k - 1][old, part, :] + stage_in[k - 1][chunk, part, :].astype(F32)

        slot = slot_of(k, position)
        stage_send[k][slot] = total(1 - mine).astype(BF)
        stage_copy(k, chunk, position, stage_target(k, chunk)).start()
        stage_own[k][slot] = total(mine)

    last_ff = OWN_TICKS[-1]
    pieces = [exchange_sums, norm_two_back, attention_back, norm_one_sums, finish_rows]
    pieces = [(last_ff + index, piece) for index, piece in enumerate(pieces)]
    for k in range(cfg.bits + 1):
        pieces.append((pieces[-1][0] + SMALL_GAP, functools.partial(small_stage, k)))
    ticks = max(LAG + cfg.chunks + cfg.late[stages], pieces[-1][0] + 1)

    def tick(t, carry):
        for ticks_of, forward in ((OWN_TICKS, forward_own), (NEAR_TICKS, forward_near)):
            now = sum(jnp.where(t == when, 1, 0) for when in ticks_of)
            past = sum(jnp.where(t > when, 1, 0) for when in ticks_of)

            @pl.when(now > 0)
            def _(forward=forward, past=past):
                forward(past)

        @pl.when(t == NEAR_TICKS[0] - 1)
        def _():
            build_argument_lefts()
            for near in range(len(cfg.near)):
                adopt(near, 0)

        for k in range(stages, 0, -1):
            spot = t - LAG - cfg.late[k]

            @pl.when(jnp.logical_and(spot >= 0, spot < cfg.chunks))
            def _(k=k, spot=spot):
                halve(k, lookup(cfg.order, spot), spot)

        new = t - LAG

        @pl.when(jnp.logical_and(new >= 0, new < cfg.chunks))
        def _():
            form(lookup(cfg.order, new), new)

        for when, piece in pieces:

            @pl.when(t == when)
            def _(piece=piece):
                piece()

        return carry

    lax.fori_loop(0, ticks, tick, 0)

    flat = jnp.concatenate([att_final[index] for index in range(cfg.chunks - cfg.ff_total)], axis=1)
    for part, ref in enumerate((query_out, key_out, value_out)):
        ref[...] = flat[: cfg.shard, part * hw : (part + 1) * hw]
    output_out[...] = jnp.transpose(flat[:, 3 * hw :])[:, : cfg.shard]
    for store in row_stores:
        store.wait()

    def wait_store(chunk, carry):
        ff_store(chunk).wait()
        return carry

    lax.fori_loop(0, cfg.ff_total, wait_store, 0)


def finish_kernel(
    cfg,
    layer_in,
    grad_in,
    query_in,
    key_in,
    value_in,
    output_in,
    ff_in,
    small,
    bucket_ids,
    layer_out,
    grad_out,
    gain_one,
    query_out,
    key_out,
    value_out,
    output_out,
    bias_out,
    gain_two,
    gate_out,
    up_out,
    down_out,
    *rest,
):
    pairs = [
        (ff_in.at[0], down_out),
        (ff_in.at[1], gate_out),
        (ff_in.at[2], up_out),
        (layer_in, layer_out),
        (grad_in, grad_out),
        (query_in, query_out),
        (key_in, key_out),
        (value_in, value_out),
        (output_in, output_out),
    ]
    buffers, (load_sem, store_sem) = rest[:-2], rest[-2:]
    loads, stores = [], []
    for index, ((src, dst), buffer) in enumerate(zip(pairs, buffers)):
        loads.append(pltpu.make_async_copy(src, buffer, load_sem.at[index]))
        stores.append(pltpu.make_async_copy(buffer, dst, store_sem.at[index]))
    for load in loads:
        load.start()
    for row, gain in ((0, gain_one), (2, gain_two)):
        line = jnp.concatenate([small[row : row + 1, :], small[row + 1 : row + 2, :]], axis=1)
        gain[...] = line[:, : cfg.width].reshape(cfg.width)
    offsets = bucket_ids.shape[0]
    bucket = lax.broadcasted_iota(jnp.int32, (cfg.buckets, offsets), 0)
    onehot = (bucket_ids[...].reshape(1, offsets) == bucket).astype(F32)
    sums = lax.dot_general(
        small[:, :offsets],
        onehot,
        (((1,), (1,)), ((), ())),
        precision=lax.Precision.HIGHEST,
        preferred_element_type=F32,
    )
    bias_out[...] = sums[4 : 4 + cfg.heads, :]
    for load, store in zip(loads, stores):
        load.wait()
        store.start()
    for store in stores:
        store.wait()


def shards(
    mesh,
    hidden_in,
    attention_gain,
    query_weight,
    key_weight,
    value_weight,
    output_weight,
    position_bias,
    feedforward_gain,
    gate_weight,
    up_weight,
    down_weight,
    cotangent,
    item_lengths,
    item_group,
    bucket_ids,
):
    rows, width = hidden_in.shape
    hw = query_weight.shape[1]
    hidden = gate_weight.shape[1]
    buckets = position_bias.shape[0]
    cfg = Sizes(mesh.shape["dp"], rows, width, hw, hidden, buckets)
    seq, stages, shard = cfg.seq, cfg.stages, cfg.shard
    any_spec = pl.BlockSpec(memory_space=pl.ANY)
    vmem = pl.BlockSpec(memory_space=pltpu.VMEM)
    smem = pl.BlockSpec(memory_space=pltpu.SMEM)
    small_shape = (8, cfg.half)
    scratch = [
        pltpu.VMEM((2, width, rows), BF),
        pltpu.VMEM((2, width, rows), BF),
        pltpu.VMEM((seq, width), BF),
        pltpu.VMEM((2, width, 128), F32),
        pltpu.VMEM((3, hw, width), BF),
        pltpu.VMEM((2, hw, width), BF),
        pltpu.VMEM((width, 2 * hw), BF),
        pltpu.VMEM((2, width, CW), BF),
        pltpu.VMEM((2, width, CW), BF),
        pltpu.VMEM((2, width, CW), BF),
        pltpu.VMEM((width, seq), BF),
        pltpu.VMEM((seq, width), BF),
        pltpu.VMEM((width, seq), F32),
        pltpu.VMEM((3, hw, seq), BF),
        pltpu.VMEM((cfg.heads, seq, seq), F32),
        pltpu.VMEM((2, hw, seq), BF),
        pltpu.VMEM((cfg.tall, seq), F32),
        pltpu.VMEM((4, 8, cfg.eighth, seq), BF),
        pltpu.VMEM((len(cfg.near) + 1, 2, 4, cfg.eighth, seq), BF),
        pltpu.VMEM((len(cfg.near), 2, seq, width), BF),
        pltpu.VMEM((RING + cfg.chunks - cfg.ff_total, seq, CW), BF),
        pltpu.VMEM((RING + cfg.chunks - cfg.ff_total, seq, CW), BF),
        pltpu.VMEM((width, seq), F32),
        pltpu.VMEM((cfg.tall, seq), F32),
        pltpu.VMEM((width, seq), BF),
        pltpu.VMEM((width, rows), BF),
        pltpu.VMEM((width, rows), BF),
        pltpu.VMEM((width, rows), BF),
        pltpu.VMEM((width, rows), BF),
        pltpu.VMEM((width, seq), BF),
        pltpu.VMEM((3, hw, seq), BF),
        pltpu.VMEM(small_shape, F32),
        pltpu.VMEM((cfg.bits + 1,) + small_shape, F32),
        pltpu.VMEM((cfg.chunks - cfg.ff_total, cfg.shard_pad, CW), F32),
        pltpu.VMEM((1, 2 * seq), jnp.int32),
        pltpu.VMEM((width, rows), F32),
        pltpu.VMEM((width, rows), F32),
        pltpu.VMEM((3, shard, hidden), F32),
    ]
    for dtype in (F32, BF):
        scratch += [
            pltpu.VMEM((gap + 1, size, CW), dtype) for gap, size in zip(cfg.gaps, cfg.stage_rows)
        ]
    scratch += [pltpu.VMEM((cfg.chunks, size, CW), BF) for size in cfg.stage_rows]
    dma = pltpu.SemaphoreType.DMA
    scratch += [
        dma((6,)),
        dma((2, 3)),
        dma((8,)),
        dma((8,)),
        dma((2,)),
        dma((2,)),
        dma((2,)),
        dma((2,)),
        dma((3, 2)),
        dma((3, 2)),
        dma((3, 2)),
        dma((3, 2)),
        dma((cfg.chunks - cfg.ff_total,)),
        dma((cfg.chunks - cfg.ff_total,)),
        dma((stages, max(cfg.gaps) + 1)),
        dma((stages, cfg.chunks)),
        dma((cfg.bits + 1,)),
        dma((cfg.bits + 1,)),
        dma((cfg.ff_total + 2,)),
    ]
    (
        layer_out,
        input_grad,
        small_sum,
        ff_sum,
        query_sum,
        key_sum,
        value_sum,
        output_sum,
    ) = pl.pallas_call(
        functools.partial(layer_kernel, cfg),
        out_shape=[
            jax.ShapeDtypeStruct((width, rows), F32),
            jax.ShapeDtypeStruct((width, rows), F32),
            jax.ShapeDtypeStruct(small_shape, F32),
            jax.ShapeDtypeStruct((3, shard, hidden), F32),
            jax.ShapeDtypeStruct((shard, hw), F32),
            jax.ShapeDtypeStruct((shard, hw), F32),
            jax.ShapeDtypeStruct((shard, hw), F32),
            jax.ShapeDtypeStruct((hw, shard), F32),
        ],
        in_specs=[
            any_spec,
            vmem,
            any_spec,
            any_spec,
            any_spec,
            any_spec,
            smem,
            vmem,
            any_spec,
            any_spec,
            any_spec,
            any_spec,
            smem,
            smem,
            vmem,
        ],
        out_specs=[any_spec, any_spec, vmem, any_spec] + [vmem] * 4,
        scratch_shapes=scratch,
        compiler_params=pltpu.CompilerParams(
            collective_id=0, has_side_effects=True, vmem_limit_bytes=62 * 1024 * 1024
        ),
        cost_estimate=pl.CostEstimate(
            flops=14 * 10**9, bytes_accessed=24 * 10**6, transcendentals=10**6
        ),
    )(
        hidden_in.T,
        attention_gain,
        query_weight.T,
        key_weight.T,
        value_weight.T,
        output_weight,
        position_bias.T,
        feedforward_gain,
        gate_weight,
        up_weight,
        down_weight.T,
        cotangent.T,
        item_lengths,
        item_group,
        bucket_ids,
    )
    def like(array):
        return jax.ShapeDtypeStruct(array.shape, array.dtype)

    one_ff = jax.ShapeDtypeStruct((shard, hidden), F32)
    outs = pl.pallas_call(
        functools.partial(finish_kernel, cfg),
        out_shape=[
            like(layer_out),
            like(input_grad),
            like(attention_gain),
            like(query_sum),
            like(key_sum),
            like(value_sum),
            like(output_sum),
            jax.ShapeDtypeStruct((cfg.heads, buckets), F32),
            like(feedforward_gain),
            one_ff,
            one_ff,
            one_ff,
        ],
        in_specs=[any_spec] * 7 + [vmem, vmem],
        out_specs=[any_spec] * 2 + [vmem] + [any_spec] * 4 + [vmem] * 2 + [any_spec] * 3,
        scratch_shapes=[
            pltpu.VMEM(array.shape, F32)
            for array in (one_ff,) * 3
            + (layer_out, input_grad, query_sum, key_sum, value_sum, output_sum)
        ]
        + [dma((9,)), dma((9,))],
        compiler_params=pltpu.CompilerParams(vmem_limit_bytes=62 * 1024 * 1024),
    )(
        layer_out,
        input_grad,
        query_sum,
        key_sum,
        value_sum,
        output_sum,
        ff_sum,
        small_sum,
        bucket_ids,
    )
    layer_out, input_grad, gain_one, query, key, value, output, bias, gain_two, gate, up, down = outs
    return (
        layer_out.T,
        input_grad.T,
        gain_one,
        query,
        key,
        value,
        output,
        bias.T,
        gain_two,
        gate,
        up,
        down.T,
    )


def solution(mesh):
    in_specs = (
        P(("dp", "mp"), None),
        P(),
        P(None, "mp"),
        P(None, "mp"),
        P(None, "mp"),
        P("mp", None),
        P(None, "mp"),
        P(),
        P(None, "mp"),
        P(None, "mp"),
        P("mp", None),
        P(("dp", "mp"), None),
        P(),
        P(),
        P(),
    )
    out_specs = (
        P(("dp", "mp"), None),
        P(("dp", "mp"), None),
        P(),
        P("dp", "mp"),
        P("dp", "mp"),
        P("dp", "mp"),
        P("mp", "dp"),
        P(None, "mp"),
        P(),
        P("dp", "mp"),
        P("dp", "mp"),
        P("mp", "dp"),
    )
    return jax.shard_map(
        functools.partial(shards, mesh),
        mesh=mesh,
        in_specs=in_specs,
        out_specs=out_specs,
        check_vma=False,
    )
```

```python
import functools
import math

import jax
import jax.numpy as jnp
from jax import lax
from jax.experimental import pallas as pl
from jax.experimental.pallas import tpu as pltpu
from jax.sharding import PartitionSpec as P

DKV = 64
CW = 256
EPS = 1e-06
AXES = ((1, 0, 2), (1, 2, 0), (2, 1, 0), (2, 1, 0), (2, 0, 1), (2, 1, 0), (1, 0, 2), (2, 1, 0))
TOGETHER = (2, 3, 2)
OWN_TICKS = (0, 1, 4, 7, 9, 11, 13)
NEAR_TICKS = (2, 3, 6, 9, 10, 12, 14)
RING_BLOCKS = 5
LAG = 2
GAPS = (4, 4, 4)
RING = 3 * RING_BLOCKS
SMALL_GAP = 3
STEP = 64
MROWS = 368
BF = jnp.bfloat16
F32 = jnp.float32
MESH = pl.DeviceIdType.MESH
GELU_C = math.sqrt(2.0 / math.pi)


def dot(left, right):
    return lax.dot_general(left, right, (((1,), (0,)), ((), ())), preferred_element_type=F32)


def dot_nt(left, right):
    return lax.dot_general(left, right, (((1,), (1,)), ((), ())), preferred_element_type=F32)


def dot_tn(left, right):
    return lax.dot_general(left, right, (((0,), (0,)), ((), ())), preferred_element_type=F32)


def blocks_of(extent, step):
    return [slice(begin, min(begin + step, extent)) for begin in range(0, extent, step)]


def fold(block):
    return jnp.sum(block.reshape(block.shape[0] // 8, 8, block.shape[1]), axis=0)


def lookup(table, index):
    bits = max(table).bit_length()
    if bits == 0:
        return 0 * index
    per = 30 // bits
    words = [
        sum(value << (bits * place) for place, value in enumerate(table[begin : begin + per]))
        for begin in range(0, len(table), per)
    ]
    word = jnp.int32(words[0])
    for place in range(1, len(words)):
        word = jnp.where(index >= place * per, words[place], word)
    shifted = lax.shift_right_logical(word, bits * lax.rem(index, per))
    return lax.rem(shifted, 1 << bits)


class Sizes:
    def __init__(self, dp, local_rows, width, head_width, hidden, buckets):
        self.dp = dp
        self.bits = dp.bit_length() - 1
        self.local_rows = local_rows
        self.seq = 2 * local_rows
        self.width = width
        self.head_width = head_width
        self.heads = head_width // DKV
        self.hidden = hidden
        self.buckets = buckets
        self.shard = width // dp
        self.shard_pad = -(-self.shard // 16) * 16
        self.quarter = self.shard_pad * dp // 4
        self.ff_chunks = hidden // CW
        self.ff_total = 3 * self.ff_chunks
        self.chunks = self.ff_total + 4 * head_width // CW
        self.stage_rows = [self.quarter >> k for k in range(self.bits - 1)]
        self.stages = len(self.stage_rows)
        self.half = -(-width // 256) * 128
        self.tall = width + self.shard_pad
        self.eighth = self.quarter // 2
        self.gaps = [GAPS[min(k, 2)] for k in range(self.stages)]
        self.late = [sum(self.gaps[:k]) for k in range(self.stages + 1)]
        self.order = []
        begin = 0
        for count in TOGETHER:
            self.order += [3 * (begin + f) + kind for kind in range(3) for f in range(count)]
            begin += count
        self.order += range(self.ff_total, self.chunks)
        self.near = sorted({axes[0] for axes in AXES[: self.ff_chunks]})
        self.first_use = [[axes[0] for axes in AXES].index(axis) for axis in self.near]


def layer_kernel(
    cfg,
    hidden_hbm,
    gain_one,
    wq_hbm,
    wk_hbm,
    wv_hbm,
    wo_hbm,
    position_bias,
    gain_two,
    wg_hbm,
    wu_hbm,
    wd_hbm,
    cot_hbm,
    lengths,
    groups,
    bucket_ids,
    layer_hbm,
    input_hbm,
    small_out,
    ff_hbm,
    query_out,
    key_out,
    value_out,
    output_out,
    hid,
    cot_raw,
    cot,
    gains,
    wqkv,
    wo,
    wo_t,
    wg,
    wu,
    wd,
    normed_one,
    normed_two,
    middle,
    qkv,
    probs,
    attended,
    trans,
    left_own,
    left_in,
    near_rows,
    right_own,
    right_in,
    out_acc,
    grad_acc,
    grad_in,
    part_send,
    part_in,
    back_send,
    back_in,
    grad_branch,
    grad_qkv,
    small,
    small_in,
    att_final,
    ids_row,
    layer_out,
    input_grad,
    ff_out,
    *rest,
):
    grad_send = normed_one
    stages = cfg.stages
    stage_own = rest[:stages]
    stage_send = rest[stages : 2 * stages]
    stage_in = rest[2 * stages : 3 * stages]
    (
        load_sem,
        weight_sem,
        pair_send_sem,
        pair_recv_sem,
        left_send_sem,
        left_recv_sem,
        share_send_sem,
        share_recv_sem,
        near_send_sem,
        near_recv_sem,
        pass_send_sem,
        pass_recv_sem,
        right_send_sem,
        right_recv_sem,
        stage_send_sem,
        stage_recv_sem,
        small_send_sem,
        small_recv_sem,
        out_sem,
    ) = rest[3 * stages :]

    seq, rows, width, hw, heads = cfg.seq, cfg.local_rows, cfg.width, cfg.head_width, cfg.heads
    me = lax.axis_index("dp")
    core = lax.axis_index("mp")
    bit = [lax.rem(lax.div(me, 1 << k), 2) for k in range(cfg.bits)]
    peer = [me + (1 - 2 * bit[k]) * (1 << k) for k in range(cfg.bits)]
    sibling = (me, 1 - core)
    own_lanes = pl.ds(pl.multiple_of(core * rows, rows), rows)
    own_rows = own_lanes
    other_lanes = pl.ds(pl.multiple_of((1 - core) * rows, rows), rows)

    def send(src, dst, send_sem, recv_sem, target):
        return pltpu.make_async_remote_copy(
            src_ref=src,
            dst_ref=dst,
            send_sem=send_sem,
            recv_sem=recv_sem,
            device_id=target,
            device_id_type=MESH,
        )

    loads = [
        pltpu.make_async_copy(hidden_hbm, hid.at[core], load_sem.at[0]),
        pltpu.make_async_copy(cot_hbm, cot_raw.at[core], load_sem.at[1]),
        pltpu.make_async_copy(wq_hbm, wqkv.at[0], load_sem.at[2]),
        pltpu.make_async_copy(wk_hbm, wqkv.at[1], load_sem.at[3]),
        pltpu.make_async_copy(wv_hbm, wqkv.at[2], load_sem.at[4]),
        pltpu.make_async_copy(wo_hbm, wo.at[core], load_sem.at[5]),
    ]
    for load in loads:
        load.start()

    def weight_loads(chunk, slot):
        columns = pl.ds(pl.multiple_of(chunk * CW, CW), CW)
        return [
            pltpu.make_async_copy(src.at[:, columns], dst.at[slot], weight_sem.at[slot, index])
            for index, (src, dst) in enumerate(((wg_hbm, wg), (wu_hbm, wu), (wd_hbm, wd)))
        ]

    barrier = pltpu.get_barrier_semaphore()
    pl.semaphore_signal(barrier, inc=1, device_id=sibling, device_id_type=MESH)
    for k in range(cfg.bits):
        pl.semaphore_signal(barrier, inc=1, device_id=(peer[k], core), device_id_type=MESH)
    for index, gain in enumerate((gain_one, gain_two)):
        line = gain[...].reshape(1, width)
        for block in blocks_of(width, 128):
            size = block.stop - block.start
            gains[index, block, :] = jnp.transpose(
                jnp.broadcast_to(line[:, block], (128, size))
            )
    group_len = jnp.int32(0)
    for item in range(lengths.shape[0]):
        group_len = group_len + jnp.where(groups[item] == me, lengths[item], 0)

    loads[1].wait()
    lane_valid = lax.broadcasted_iota(jnp.int32, (1, rows), 1) + core * rows < group_len
    for block in blocks_of(width, 128):
        part = jnp.where(lane_valid, cot_raw[core, block, :].astype(F32), 0.0)
        cot[own_rows, block] = jnp.transpose(part).astype(BF)
    pl.semaphore_wait(barrier, cfg.bits + 1)

    pair_hid = send(
        hidden_hbm, hid.at[core], pair_send_sem.at[0], pair_recv_sem.at[0], sibling
    )
    pair_cot = send(
        cot_hbm, cot_raw.at[core], pair_send_sem.at[1], pair_recv_sem.at[1], sibling
    )
    pair_wo = send(wo_hbm, wo.at[core], pair_send_sem.at[2], pair_recv_sem.at[2], sibling)
    pair_rows = send(
        cot.at[own_rows], cot.at[own_rows], pair_send_sem.at[7], pair_recv_sem.at[7], sibling
    )

    natural = (cot, normed_two)

    def near_copy(near, which):
        return send(
            natural[which].at[own_rows],
            near_rows.at[near, which, own_rows],
            near_send_sem.at[near, which],
            near_recv_sem.at[near, which],
            (peer[cfg.near[near]], core),
        )

    def near_pass(near, which):
        return send(
            near_rows.at[near, which, own_rows],
            near_rows.at[near, which, own_rows],
            pass_send_sem.at[near, which],
            pass_recv_sem.at[near, which],
            sibling,
        )

    pair_hid.start()
    pair_cot.start()
    pair_wo.start()
    pair_rows.start()
    for near in range(len(cfg.near)):
        near_copy(near, 0).start()
    pair_att = send(
        attended.at[core], attended.at[core], pair_send_sem.at[3], pair_recv_sem.at[3], sibling
    )
    pair_grad = send(grad_send, grad_in, pair_send_sem.at[4], pair_recv_sem.at[4], sibling)
    pair_part = send(part_send, part_in, pair_send_sem.at[5], pair_recv_sem.at[5], sibling)
    pair_back = send(back_send, back_in, pair_send_sem.at[6], pair_recv_sem.at[6], sibling)

    for slot in range(2):
        for load in weight_loads(slot, slot):
            load.start()

    def place_of(index):
        place = 0
        for k in range(3, cfg.bits):
            place = 2 * place + ((index >> k) & 1)
        return slice(place * cfg.shard_pad, (place + 1) * cfg.shard_pad)

    def shard_of(source, index):
        return source[index * cfg.shard : index * cfg.shard + cfg.shard_pad, :].astype(BF)

    def build_left(source, which):
        for index in range(cfg.dp):
            left_own[which, index & 7, place_of(index), :] = shard_of(source, index)

    def adopt(near, which):
        near_copy(near, which).wait()
        near_pass(near, which).start()
        near_pass(near, which).wait()
        axis = cfg.near[near]
        high, low = (k for k in (2, 1, 0) if k != axis)
        for block in blocks_of(width, 128):
            trans[block, :] = jnp.transpose(near_rows[near, which, :, block]).astype(F32)
        for value in range(2):

            @pl.when(bit[axis] == value)
            def _(value=value):
                for index in range(cfg.dp):
                    if (index >> axis) & 1 == value:
                        place = 2 * ((index >> high) & 1) + ((index >> low) & 1)
                        left_in[near, which, place, place_of(index), :] = shard_of(trans, index)

    def left_copy(which):
        return send(
            left_own.at[2 + which, pl.ds(4 * (1 - bit[2]) + 2 * core, 2)],
            left_in.at[len(cfg.near), which, pl.ds(2 * core, 2)],
            left_send_sem.at[which],
            left_recv_sem.at[which],
            (peer[2], core),
        )

    def left_share(which):
        return send(
            left_in.at[len(cfg.near), which, pl.ds(2 * core, 2)],
            left_in.at[len(cfg.near), which, pl.ds(2 * core, 2)],
            share_send_sem.at[which],
            share_recv_sem.at[which],
            sibling,
        )

    def left_pass(which):
        left_copy(which).wait()
        left_share(which).start()

    def block_of(chunk):
        return lax.div(chunk, 3)

    def pick(chunk, level, values):
        if level > 2:
            return values[level]
        k = lookup([axes[level] for axes in AXES], block_of(chunk))
        parts = (lax.div((1 - k) * (2 - k), 2), k * (2 - k), lax.div(k * (k - 1), 2))
        return sum(part * value for part, value in zip(parts, values))

    def right_slot(chunk):
        tail_part = lax.div(chunk, cfg.ff_total)
        return (1 - tail_part) * lax.rem(chunk, RING) + tail_part * (RING + chunk - cfg.ff_total)

    def right_copy(index):
        return send(
            right_own.at[RING + index],
            right_in.at[RING + index],
            right_send_sem.at[index],
            right_recv_sem.at[index],
            (peer[2], core),
        )

    for scratch in (trans, grad_acc):
        scratch[width:, :] = jnp.zeros((cfg.tall - width, seq), F32)

    step_rows = STEP
    steps = width // step_rows

    def rows_at(step):
        return pl.ds(pl.multiple_of(step * step_rows, step_rows), step_rows)

    def whole(ref, block):
        return jnp.concatenate([ref[0, block, :], ref[1, block, :]], axis=1)

    def gain_at(index, block, lanes):
        part = gains[index, block, :]
        return jnp.concatenate([part] * (lanes // 128), axis=1)

    def column_sum(term, lanes):
        zero = jnp.zeros((8, lanes), F32)
        total = lax.fori_loop(0, steps, lambda i, acc: acc + fold(term(rows_at(i))), zero)
        return jnp.sum(total, axis=0, keepdims=True)

    def inverse_rms(term, lanes):
        def square(block):
            x = term(block)
            return x * x

        return lax.rsqrt(column_sum(square, lanes) * (1.0 / width) + EPS)

    loads[0].wait()
    pair_hid.wait()

    def x_at(block):
        return whole(hid, block).astype(F32)

    inv_one = inverse_rms(x_at, seq)

    def norm_one_rows(step, carry):
        block = rows_at(step)
        normed = x_at(block) * inv_one * gain_at(0, block, seq)
        trans[block, :] = normed
        normed_one[block, :] = normed.astype(BF)
        return carry

    lax.fori_loop(0, steps, norm_one_rows, 0)

    for part in range(3):
        loads[2 + part].wait()
        qkv[part] = dot(wqkv[part], normed_one[...]).astype(BF)

    key_valid = lax.broadcasted_iota(jnp.int32, (seq, seq), 0) < group_len
    ids_row[...] = jnp.full(ids_row.shape, -1, jnp.int32)
    ids_row[:, : bucket_ids.shape[0]] = bucket_ids[...].reshape(1, -1)
    ids = ids_row[...]
    for head in range(heads):
        part = slice(head * DKV, (head + 1) * DKV)
        by_offset = jnp.zeros(ids.shape, F32)
        for bucket in range(cfg.buckets):
            by_offset = jnp.where(ids == bucket, position_bias[head, bucket], by_offset)
        bias = pltpu.roll(
            jnp.broadcast_to(by_offset, (seq, 2 * seq)),
            seq + 1,
            1,
            stride=1,
            stride_axis=0,
        )[:, :seq]
        scores = dot_tn(qkv[1, part, :], qkv[0, part, :]) + jnp.transpose(bias)
        scores = jnp.where(key_valid, scores, -1e30)
        exps = jnp.exp(scores - jnp.max(scores, axis=0, keepdims=True))
        prob = exps / jnp.sum(exps, axis=0, keepdims=True)
        probs[head] = prob
        attended[core, part, :] = dot(qkv[2, part, :], prob.astype(BF)).astype(BF)
    pair_att.start()

    row_valid = lax.broadcasted_iota(jnp.int32, (step_rows, seq), 1) < group_len

    def build_argument_lefts():
        def first_rows(step, carry):
            block = rows_at(step)
            trans[block, :] = normed_one[block, :].astype(F32)
            return carry

        lax.fori_loop(0, steps, first_rows, 0)
        build_left(trans, 2)
        pair_cot.wait()

        def mask_rows(step, carry):
            block = rows_at(step)
            trans[block, :] = jnp.where(row_valid, whole(cot_raw, block).astype(F32), 0.0)
            return carry

        lax.fori_loop(0, steps, mask_rows, 0)
        build_left(trans, 0)

    loads[5].wait()
    pair_wo.wait()
    for block in blocks_of(width, 128):
        wo_t[block, :] = jnp.transpose(
            jnp.concatenate([wo[0, :, block], wo[1, :, block]], axis=0).astype(F32)
        ).astype(BF)
    pair_att.wait()
    both = attended[...].reshape(2 * hw, seq)
    for block in blocks_of(width, MROWS):
        middle[block, :] = x_at(block) + dot(wo_t[block, :], both)

    inv_two = inverse_rms(lambda block: middle[block, :], seq)

    def norm_two_rows(step, carry):
        block = rows_at(step)
        trans[block, :] = middle[block, :] * inv_two * gain_at(1, block, seq)
        out_acc[block, :] = jnp.zeros((step_rows, seq), F32)
        grad_acc[block, :] = jnp.zeros((step_rows, seq), F32)
        return carry

    lax.fori_loop(0, steps, norm_two_rows, 0)
    for block in blocks_of(width, 128):
        normed_two[:, block] = jnp.transpose(trans[block, :]).astype(BF)
    for near in range(len(cfg.near)):
        near_copy(near, 1).start()
    build_left(trans, 1)
    pair_rows.wait()
    small[...] = jnp.zeros_like(small)

    def activations(chunk, normed, grad_rows, target):
        slot = lax.rem(chunk, 2)
        first = lax.rem(3 * chunk, RING)
        gate = dot(normed, wg[slot])
        up = dot(normed, wu[slot])
        grad_hidden = dot(grad_rows, wd[slot])
        square = gate * gate
        tanh = jnp.tanh(GELU_C * (gate + 0.044715 * (square * gate)))
        half = 0.5 * (1.0 + tanh)
        gelu = gate * half
        slope = half + (0.5 * GELU_C) * gate * (1.0 - tanh * tanh) * (
            1.0 + (3 * 0.044715) * square
        )
        target[first] = (gelu * up).astype(BF)
        target[first + 1] = (grad_hidden * up * slope).astype(BF)
        target[first + 2] = (grad_hidden * gelu).astype(BF)

    def forward_own(chunk):
        slot = lax.rem(chunk, 2)
        first = lax.rem(3 * chunk, RING)
        for load in weight_loads(chunk, slot):
            load.wait()
        activations(chunk, normed_two[...], cot[...], right_own)
        hidden, grad_gate, grad_up = (right_own[first + kind] for kind in range(3))
        for block in blocks_of(width, MROWS):
            out_acc[block, :] += dot_nt(wd[slot, block, :], hidden)
            grad_acc[block, :] += dot_nt(wg[slot, block, :], grad_gate) + dot_nt(
                wu[slot, block, :], grad_up
            )

    def forward_near(chunk):
        slot = lax.rem(chunk, 2)
        for near, use in enumerate(cfg.first_use):

            @pl.when(chunk == use)
            def _(near=near):
                adopt(near, 1)

        near = lookup([cfg.near.index(axes[0]) for axes in AXES[: cfg.ff_chunks]], chunk)
        activations(chunk, near_rows[near, 1], near_rows[near, 0], right_in)

        @pl.when(chunk < cfg.ff_chunks - 2)
        def _():
            for load in weight_loads(chunk + 2, slot):
                load.start()

    def exchange_sums():
        left_copy(0).start()
        grad_send[...] = grad_acc[:width, :].astype(BF)
        pair_grad.start()
        part_send[...] = out_acc[:, other_lanes].astype(BF)
        pair_part.start()

    def lane_mask(shape, dimension):
        lane = lax.broadcasted_iota(jnp.int32, shape, dimension)
        return (lax.div(lane, rows) == core).astype(F32)

    def lane_sums(weights, source):
        high = source.astype(BF)
        low = (source - high.astype(F32)).astype(BF)
        return (dot_nt(weights.astype(BF), high) + dot_nt(weights.astype(BF), low))[0:1, :]

    def put_small(row, line):
        small[row : row + 1, :] = line[:, : cfg.half]
        small[row + 1 : row + 2, : width - cfg.half] = line[:, cfg.half :]

    def norm_two_back():
        pair_grad.wait()

        def grad_at(block):
            return grad_acc[block, :] + grad_in[block, :].astype(F32)

        inv = inverse_rms(lambda block: middle[block, :], seq)
        inner = (
            column_sum(
                lambda block: grad_at(block) * gain_at(1, block, seq) * middle[block, :], seq
            )
            * inv
            * (1.0 / width)
        )

        def back_rows(step, carry):
            block = rows_at(step)
            grad = grad_at(block)
            unit = middle[block, :] * inv
            masked = jnp.where(row_valid, whole(cot_raw, block).astype(F32), 0.0)
            total = masked + inv * (grad * gain_at(1, block, seq) - unit * inner)
            trans[block, :] = grad * unit
            grad_acc[block, :] = total
            grad_branch[block, :] = total.astype(BF)
            return carry

        lax.fori_loop(0, steps, back_rows, 0)
        build_left(grad_acc, 3)
        left_copy(1).start()
        mask = lane_mask((8, seq), 1)
        put_small(2, lane_sums(mask, trans[:width, :]))

    def attention_back():
        grad_att = dot(wo[core], grad_branch[...]).astype(BF)
        flip = (
            lax.broadcasted_iota(jnp.int32, (seq, seq), 0)
            + lax.broadcasted_iota(jnp.int32, (seq, seq), 1)
            == seq - 1
        ).astype(BF)
        for head in range(heads):
            part = slice(head * DKV, (head + 1) * DKV)
            grad_mixed = grad_att[part, :]
            prob = probs[head]
            grad_probs = dot_tn(qkv[2, part, :], grad_mixed)
            inner = jnp.sum(prob * grad_probs, axis=0, keepdims=True)
            grad_scores = (prob * (grad_probs - inner)).astype(BF)
            grad_qkv[0, part, :] = dot(qkv[1, part, :], grad_scores).astype(BF)
            grad_qkv[1, part, :] = dot_nt(qkv[0, part, :], grad_scores).astype(BF)
            grad_qkv[2, part, :] = dot_nt(grad_mixed, prob.astype(BF)).astype(BF)
            flipped = jnp.concatenate(
                [dot(grad_scores, flip), jnp.zeros((seq, seq), F32)], axis=1
            )
            skewed = pltpu.roll(flipped, 0, 1, stride=1, stride_axis=0)
            small[4 + head : 5 + head, : 2 * seq] = jnp.sum(skewed, axis=0, keepdims=True)
        joined = jnp.concatenate(
            [grad_qkv[...].reshape(3 * hw, seq), attended[core]], axis=0
        ).astype(F32)
        for index in range(cfg.chunks - cfg.ff_total):
            right_own[RING + index] = jnp.transpose(
                joined[index * CW : (index + 1) * CW, :]
            ).astype(BF)
            right_copy(index).start()

    def norm_one_sums():
        for block in blocks_of(width, 128):
            back_send[block, :] = sum(
                dot_tn(wqkv[part, :, block], grad_qkv[part, :, other_lanes]) for part in range(3)
            ).astype(BF)
        pair_back.start()
        for block in blocks_of(width, 128):
            input_grad[block, :] = sum(
                dot_tn(wqkv[part, :, block], grad_qkv[part, :, own_lanes]) for part in range(3)
            )

    row_stores = [
        pltpu.make_async_copy(src, dst, out_sem.at[cfg.ff_total + index])
        for index, (src, dst) in enumerate(((layer_out, layer_hbm), (input_grad, input_hbm)))
    ]

    def ff_store(chunk):
        columns = pl.ds(pl.multiple_of(lax.div(chunk, 3) * CW, CW), CW)
        kind = lax.rem(chunk, 3)
        return pltpu.make_async_copy(
            ff_out.at[kind, :, columns], ff_hbm.at[kind, :, columns], out_sem.at[chunk]
        )

    def small_copy(k):
        target = sibling if k == cfg.bits else (peer[k], core)
        return send(
            small, small_in.at[k], small_send_sem.at[k], small_recv_sem.at[k], target
        )

    def finish_rows():
        pair_part.wait()
        pair_back.wait()

        def x_own(block):
            return hid[core, block, :].astype(F32)

        def grad_at(block):
            return input_grad[block, :] + back_in[block, :].astype(F32)

        inv = inverse_rms(x_own, rows)
        inner = (
            column_sum(lambda block: grad_at(block) * gain_at(0, block, rows) * x_own(block), rows)
            * inv
            * (1.0 / width)
        )

        def last_rows(step, carry):
            block = rows_at(step)
            grad = grad_at(block)
            unit = x_own(block) * inv
            input_grad[block, :] = grad_acc[block, own_lanes] + inv * (
                grad * gain_at(0, block, rows) - unit * inner
            )
            layer_out[block, :] = (
                middle[block, own_lanes]
                + out_acc[block, own_lanes]
                + part_in[block, :].astype(F32)
            )
            trans[block, :rows] = grad * unit
            return carry

        lax.fori_loop(0, steps, last_rows, 0)
        put_small(0, lane_sums(jnp.ones((8, rows), F32), trans[:width, :rows]))
        small_copy(0).start()
        for store in row_stores:
            store.start()

    def small_stage(k):
        small_copy(k).wait()
        if k == cfg.bits:
            row = lax.broadcasted_iota(jnp.int32, small.shape, 0)
            small_out[...] = small[...] + jnp.where(row < 4, small_in[k], 0.0)
        else:
            small[...] = small[...] + small_in[k]
            small_copy(k + 1).start()

    def slot_of(k, spot):
        return spot % (cfg.gaps[k] + 1) if isinstance(spot, int) else lax.rem(spot, cfg.gaps[k] + 1)

    def stage_copy(k, chunk, spot, target):
        slot = slot_of(k, spot)
        return send(
            stage_send[k].at[slot],
            stage_in[k].at[chunk],
            stage_send_sem.at[k, slot],
            stage_recv_sem.at[k, chunk],
            (target, core),
        )

    def free_slot(k, chunk, position):
        @pl.when(position > cfg.gaps[k])
        def _():
            stage_copy(k, chunk, position, peer[0]).wait_send()

    def stage_target(k, chunk):
        return pick(chunk, k + 1, peer)

    def form(chunk, position):
        slot = slot_of(0, position)
        tail_part = lax.div(chunk, cfg.ff_total)
        which = (1 - tail_part) * lax.div(lax.rem(chunk, 3) + 1, 2)
        block = block_of(chunk)
        spot = right_slot(chunk)
        second_bit = pick(chunk, 1, bit)
        weights = [pick(chunk, level, (1, 2, 4)) for level in range(3)]
        descending = lookup([int(axes[1] > axes[2]) for axes in AXES], block)
        near_weights = 1 + descending, 2 - descending
        begin = weights[0] * pick(chunk, 0, bit)

        @pl.when(chunk == cfg.ff_total)
        def _():
            left_pass(0)
            left_share(0).wait()

        @pl.when(chunk == cfg.chunks - 1)
        def _():
            left_pass(1)
            left_share(1).wait()

        for index in range(cfg.chunks - cfg.ff_total):

            @pl.when(chunk == cfg.ff_total + index)
            def _(index=index):
                right_copy(index).wait()

        parts = [(second, third) for second in (1 - second_bit, second_bit) for third in range(2)]

        def product(own, near, index):
            left = [
                jnp.concatenate(
                    [left_own[own, begin + weights[1] * s + weights[2] * t] for s, t in parts], axis=0
                ),
                jnp.concatenate(
                    [
                        left_in[near, index, near_weights[0] * s + near_weights[1] * t]
                        for s, t in parts
                    ],
                    axis=0,
                ),
            ]
            return dot(
                jnp.concatenate(left, axis=1),
                jnp.concatenate([right_own[spot], right_in[spot]], axis=0),
            )

        def fill(sums):
            free_slot(0, chunk, position)
            stage_send[0][slot] = sums[: cfg.quarter, :].astype(BF)
            stage_copy(0, chunk, position, stage_target(0, chunk)).start()
            stage_own[0][slot] = sums[cfg.quarter :, :]

        own = 2 * tail_part + which
        near = lookup(
            [cfg.near.index(axes[0]) for axes in AXES[: cfg.ff_chunks]] + [len(cfg.near)], block
        )

        @pl.when(chunk < cfg.chunks - 1)
        def _():
            fill(product(own, near, which))

        @pl.when(chunk == cfg.chunks - 1)
        def _():
            split = lax.broadcasted_iota(jnp.int32, (2 * cfg.quarter, CW), 1) < CW - hw
            fill(jnp.where(split, *(product(2 + index, len(cfg.near), index) for index in range(2))))

    def halve(k, chunk, position):
        stage_copy(k - 1, chunk, position, stage_target(k - 1, chunk)).wait_recv()
        old = slot_of(k - 1, position)
        if k == stages:
            result = stage_own[k - 1][old] + stage_in[k - 1][chunk].astype(F32)

            @pl.when(chunk < cfg.ff_total)
            def _():
                columns = pl.ds(pl.multiple_of(lax.div(chunk, 3) * CW, CW), CW)
                ff_out[lax.rem(chunk, 3), :, columns] = result[: cfg.shard, :]
                ff_store(chunk).start()

            @pl.when(chunk >= cfg.ff_total)
            def _():
                att_final[lax.rem(chunk, cfg.ff_total)] = result

            return
        half = cfg.stage_rows[k]
        mine = pick(chunk, k + 1, bit)

        def total(which):
            part = pl.ds(pl.multiple_of(which * half, 16), half)
            return stage_own[k - 1][old, part, :] + stage_in[k - 1][chunk, part, :].astype(F32)

        slot = slot_of(k, position)
        free_slot(k, chunk, position)
        stage_send[k][slot] = total(1 - mine).astype(BF)
        stage_copy(k, chunk, position, stage_target(k, chunk)).start()
        stage_own[k][slot] = total(mine)

    last_ff = OWN_TICKS[-1]
    pieces = [exchange_sums, norm_two_back, attention_back, norm_one_sums, finish_rows]
    pieces = [(last_ff + index, piece) for index, piece in enumerate(pieces)]
    for k in range(cfg.bits + 1):
        pieces.append((pieces[-1][0] + SMALL_GAP, functools.partial(small_stage, k)))
    ticks = max(LAG + cfg.chunks + cfg.late[stages], pieces[-1][0] + 1)

    def tick(t, carry):
        for ticks_of, forward in ((OWN_TICKS, forward_own), (NEAR_TICKS, forward_near)):
            now = sum(jnp.where(t == when, 1, 0) for when in ticks_of)
            past = sum(jnp.where(t > when, 1, 0) for when in ticks_of)

            @pl.when(now > 0)
            def _(forward=forward, past=past):
                forward(past)

        @pl.when(t == NEAR_TICKS[0] - 1)
        def _():
            build_argument_lefts()
            for near in range(len(cfg.near)):
                adopt(near, 0)

        for k in range(stages, 0, -1):
            spot = t - LAG - cfg.late[k]

            @pl.when(jnp.logical_and(spot >= 0, spot < cfg.chunks))
            def _(k=k, spot=spot):
                halve(k, lookup(cfg.order, spot), spot)

        new = t - LAG

        @pl.when(jnp.logical_and(new >= 0, new < cfg.chunks))
        def _():
            form(lookup(cfg.order, new), new)

        for when, piece in pieces:

            @pl.when(t == when)
            def _(piece=piece):
                piece()

        return carry

    lax.fori_loop(0, ticks, tick, 0)

    for k in range(stages):
        for position in range(cfg.chunks - cfg.gaps[k] - 1, cfg.chunks):
            stage_copy(k, cfg.order[position], position, peer[0]).wait_send()

    flat = jnp.concatenate([att_final[index] for index in range(cfg.chunks - cfg.ff_total)], axis=1)
    for part, ref in enumerate((query_out, key_out, value_out)):
        ref[...] = flat[: cfg.shard, part * hw : (part + 1) * hw]
    output_out[...] = jnp.transpose(flat[:, 3 * hw :])[:, : cfg.shard]
    for store in row_stores:
        store.wait()

    def wait_store(chunk, carry):
        ff_store(chunk).wait()
        return carry

    lax.fori_loop(0, cfg.ff_total, wait_store, 0)


def finish_kernel(
    cfg,
    layer_in,
    grad_in,
    query_in,
    key_in,
    value_in,
    output_in,
    ff_in,
    small,
    bucket_ids,
    layer_out,
    grad_out,
    gain_one,
    query_out,
    key_out,
    value_out,
    output_out,
    bias_out,
    gain_two,
    gate_out,
    up_out,
    down_out,
    *rest,
):
    pairs = [
        (ff_in.at[0], down_out),
        (ff_in.at[1], gate_out),
        (ff_in.at[2], up_out),
        (layer_in, layer_out),
        (grad_in, grad_out),
        (query_in, query_out),
        (key_in, key_out),
        (value_in, value_out),
        (output_in, output_out),
    ]
    buffers, (load_sem, store_sem) = rest[:-2], rest[-2:]
    loads, stores = [], []
    for index, ((src, dst), buffer) in enumerate(zip(pairs, buffers)):
        loads.append(pltpu.make_async_copy(src, buffer, load_sem.at[index]))
        stores.append(pltpu.make_async_copy(buffer, dst, store_sem.at[index]))
    for load in loads:
        load.start()
    for row, gain in ((0, gain_one), (2, gain_two)):
        line = jnp.concatenate([small[row : row + 1, :], small[row + 1 : row + 2, :]], axis=1)
        gain[...] = line[:, : cfg.width].reshape(cfg.width)
    offsets = bucket_ids.shape[0]
    bucket = lax.broadcasted_iota(jnp.int32, (cfg.buckets, offsets), 0)
    onehot = (bucket_ids[...].reshape(1, offsets) == bucket).astype(F32)
    sums = lax.dot_general(
        small[:, :offsets],
        onehot,
        (((1,), (1,)), ((), ())),
        precision=lax.Precision.HIGHEST,
        preferred_element_type=F32,
    )
    bias_out[...] = sums[4 : 4 + cfg.heads, :]
    for load, store in zip(loads, stores):
        load.wait()
        store.start()
    for store in stores:
        store.wait()


def shards(
    mesh,
    hidden_in,
    attention_gain,
    query_weight,
    key_weight,
    value_weight,
    output_weight,
    position_bias,
    feedforward_gain,
    gate_weight,
    up_weight,
    down_weight,
    cotangent,
    item_lengths,
    item_group,
    bucket_ids,
):
    rows, width = hidden_in.shape
    hw = query_weight.shape[1]
    hidden = gate_weight.shape[1]
    buckets = position_bias.shape[0]
    cfg = Sizes(mesh.shape["dp"], rows, width, hw, hidden, buckets)
    seq, stages, shard = cfg.seq, cfg.stages, cfg.shard
    any_spec = pl.BlockSpec(memory_space=pl.ANY)
    vmem = pl.BlockSpec(memory_space=pltpu.VMEM)
    smem = pl.BlockSpec(memory_space=pltpu.SMEM)
    small_shape = (8, cfg.half)
    scratch = [
        pltpu.VMEM((2, width, rows), BF),
        pltpu.VMEM((2, width, rows), BF),
        pltpu.VMEM((seq, width), BF),
        pltpu.VMEM((2, width, 128), F32),
        pltpu.VMEM((3, hw, width), BF),
        pltpu.VMEM((2, hw, width), BF),
        pltpu.VMEM((width, 2 * hw), BF),
        pltpu.VMEM((2, width, CW), BF),
        pltpu.VMEM((2, width, CW), BF),
        pltpu.VMEM((2, width, CW), BF),
        pltpu.VMEM((width, seq), BF),
        pltpu.VMEM((seq, width), BF),
        pltpu.VMEM((width, seq), F32),
        pltpu.VMEM((3, hw, seq), BF),
        pltpu.VMEM((cfg.heads, seq, seq), F32),
        pltpu.VMEM((2, hw, seq), BF),
        pltpu.VMEM((cfg.tall, seq), F32),
        pltpu.VMEM((4, 8, cfg.eighth, seq), BF),
        pltpu.VMEM((len(cfg.near) + 1, 2, 4, cfg.eighth, seq), BF),
        pltpu.VMEM((len(cfg.near), 2, seq, width), BF),
        pltpu.VMEM((RING + cfg.chunks - cfg.ff_total, seq, CW), BF),
        pltpu.VMEM((RING + cfg.chunks - cfg.ff_total, seq, CW), BF),
        pltpu.VMEM((width, seq), F32),
        pltpu.VMEM((cfg.tall, seq), F32),
        pltpu.VMEM((width, seq), BF),
        pltpu.VMEM((width, rows), BF),
        pltpu.VMEM((width, rows), BF),
        pltpu.VMEM((width, rows), BF),
        pltpu.VMEM((width, rows), BF),
        pltpu.VMEM((width, seq), BF),
        pltpu.VMEM((3, hw, seq), BF),
        pltpu.VMEM(small_shape, F32),
        pltpu.VMEM((cfg.bits + 1,) + small_shape, F32),
        pltpu.VMEM((cfg.chunks - cfg.ff_total, cfg.shard_pad, CW), F32),
        pltpu.VMEM((1, 2 * seq), jnp.int32),
        pltpu.VMEM((width, rows), F32),
        pltpu.VMEM((width, rows), F32),
        pltpu.VMEM((3, shard, hidden), F32),
    ]
    for dtype in (F32, BF):
        scratch += [
            pltpu.VMEM((gap + 1, size, CW), dtype) for gap, size in zip(cfg.gaps, cfg.stage_rows)
        ]
    scratch += [pltpu.VMEM((cfg.chunks, size, CW), BF) for size in cfg.stage_rows]
    dma = pltpu.SemaphoreType.DMA
    scratch += [
        dma((6,)),
        dma((2, 3)),
        dma((8,)),
        dma((8,)),
        dma((2,)),
        dma((2,)),
        dma((2,)),
        dma((2,)),
        dma((3, 2)),
        dma((3, 2)),
        dma((3, 2)),
        dma((3, 2)),
        dma((cfg.chunks - cfg.ff_total,)),
        dma((cfg.chunks - cfg.ff_total,)),
        dma((stages, max(cfg.gaps) + 1)),
        dma((stages, cfg.chunks)),
        dma((cfg.bits + 1,)),
        dma((cfg.bits + 1,)),
        dma((cfg.ff_total + 2,)),
    ]
    (
        layer_out,
        input_grad,
        small_sum,
        ff_sum,
        query_sum,
        key_sum,
        value_sum,
        output_sum,
    ) = pl.pallas_call(
        functools.partial(layer_kernel, cfg),
        out_shape=[
            jax.ShapeDtypeStruct((width, rows), F32),
            jax.ShapeDtypeStruct((width, rows), F32),
            jax.ShapeDtypeStruct(small_shape, F32),
            jax.ShapeDtypeStruct((3, shard, hidden), F32),
            jax.ShapeDtypeStruct((shard, hw), F32),
            jax.ShapeDtypeStruct((shard, hw), F32),
            jax.ShapeDtypeStruct((shard, hw), F32),
            jax.ShapeDtypeStruct((hw, shard), F32),
        ],
        in_specs=[
            any_spec,
            vmem,
            any_spec,
            any_spec,
            any_spec,
            any_spec,
            smem,
            vmem,
            any_spec,
            any_spec,
            any_spec,
            any_spec,
            smem,
            smem,
            vmem,
        ],
        out_specs=[any_spec, any_spec, vmem, any_spec] + [vmem] * 4,
        scratch_shapes=scratch,
        compiler_params=pltpu.CompilerParams(
            collective_id=0, has_side_effects=True, vmem_limit_bytes=62 * 1024 * 1024
        ),
        cost_estimate=pl.CostEstimate(
            flops=14 * 10**9, bytes_accessed=24 * 10**6, transcendentals=10**6
        ),
    )(
        hidden_in.T,
        attention_gain,
        query_weight.T,
        key_weight.T,
        value_weight.T,
        output_weight,
        position_bias.T,
        feedforward_gain,
        gate_weight,
        up_weight,
        down_weight.T,
        cotangent.T,
        item_lengths,
        item_group,
        bucket_ids,
    )
    def like(array):
        return jax.ShapeDtypeStruct(array.shape, array.dtype)

    one_ff = jax.ShapeDtypeStruct((shard, hidden), F32)
    outs = pl.pallas_call(
        functools.partial(finish_kernel, cfg),
        out_shape=[
            like(layer_out),
            like(input_grad),
            like(attention_gain),
            like(query_sum),
            like(key_sum),
            like(value_sum),
            like(output_sum),
            jax.ShapeDtypeStruct((cfg.heads, buckets), F32),
            like(feedforward_gain),
            one_ff,
            one_ff,
            one_ff,
        ],
        in_specs=[any_spec] * 7 + [vmem, vmem],
        out_specs=[any_spec] * 2 + [vmem] + [any_spec] * 4 + [vmem] * 2 + [any_spec] * 3,
        scratch_shapes=[
            pltpu.VMEM(array.shape, F32)
            for array in (one_ff,) * 3
            + (layer_out, input_grad, query_sum, key_sum, value_sum, output_sum)
        ]
        + [dma((9,)), dma((9,))],
        compiler_params=pltpu.CompilerParams(vmem_limit_bytes=62 * 1024 * 1024),
    )(
        layer_out,
        input_grad,
        query_sum,
        key_sum,
        value_sum,
        output_sum,
        ff_sum,
        small_sum,
        bucket_ids,
    )
    layer_out, input_grad, gain_one, query, key, value, output, bias, gain_two, gate, up, down = outs
    return (
        layer_out.T,
        input_grad.T,
        gain_one,
        query,
        key,
        value,
        output,
        bias.T,
        gain_two,
        gate,
        up,
        down.T,
    )


def solution(mesh):
    in_specs = (
        P(("dp", "mp"), None),
        P(),
        P(None, "mp"),
        P(None, "mp"),
        P(None, "mp"),
        P("mp", None),
        P(None, "mp"),
        P(),
        P(None, "mp"),
        P(None, "mp"),
        P("mp", None),
        P(("dp", "mp"), None),
        P(),
        P(),
        P(),
    )
    out_specs = (
        P(("dp", "mp"), None),
        P(("dp", "mp"), None),
        P(),
        P("dp", "mp"),
        P("dp", "mp"),
        P("dp", "mp"),
        P("mp", "dp"),
        P(None, "mp"),
        P(),
        P("dp", "mp"),
        P("dp", "mp"),
        P("mp", "dp"),
    )
    return jax.shard_map(
        functools.partial(shards, mesh),
        mesh=mesh,
        in_specs=in_specs,
        out_specs=out_specs,
        check_vma=False,
    )
```
